128 devices in a mesh: batch: 4 (over y_lo, core), frames: 4 (over x), chan: 8 (over z, y_hi).
Axes of the slice: x: 4, y: 4 (y_hi: 2, y_lo: 2; y = y_hi * 2 + y_lo), z: 4, core: 2. Of those that a mesh axis runs over, the one named last changes fastest.
Arguments:
- tokens: bfloat16 [8, 2048, 1536], P('batch', 'frames'), may hold values from -6 to 6
- cotangent: bfloat16 [8, 2048, 1536], P('batch', 'frames'), may hold values from -6 to 6
- norm_gain: float32 [1536], replicated, may hold values from 0.5 to 1.5
- norm_bias: float32 [1536], replicated, may hold values from -3 to 3
- qkv_weight: bfloat16 [1536, 3, 1536], P(None, None, 'chan'), may hold values from -2 to 2
- out_weight: bfloat16 [1536, 1536], P('chan'), may hold values from -0.625 to 0.625
- lengths: int32 [8], P('batch'), may hold values from 1024 to 2048, as said below
- segments: int32 [8, 2048], P('batch'), may hold values from 0 to 15, never falling along the last dimension, each value on 1 to 256 neighbouring positions
Outputs:
- output: bfloat16 [8, 2048, 1536], P('batch', 'frames')
- grad_tokens: bfloat16 [8, 2048, 1536], P('batch', 'frames')
- grad_proj: float32 [1536, 4, 1536], P(('batch', 'frames'), None, 'chan')
The draws below stay inside these ranges and needn't reach their ends.
Inputs may be any that keep to these rules, and one draw needn't show every extreme that they name: `lengths`: some recording has all 2048 frames valid and some has exactly 1024. `segments`: along a recording stretch numbers never fall; each stretch has 1 to 256 frames.
All inputs are finite; a program needn't handle non-finite values.
Results may differ from the reference program's by a relative error of at most 0.0067.
Values may be sent and summed in bfloat16 or wider, within the bound.
No kernel may reach another device: no remote copies, remote signals or barrier semaphores. Data moves between devices by JAX's collectives and lax.ppermute only.
A program may use at most 128 MiB of HBM per device.

```python
import math
import jax
import jax.numpy as jnp
import numpy as np
from jax import lax

D = 1536
HEADS = 24
HEAD = 64
CTX = 256
RECS = 8
LEN = 2048


def draw_qkv_weight(key, part):
    key = jax.random.fold_in(key, 7)
    first_key = jax.random.fold_in(key, 0)
    weight_scale = D ** (-0.5)
    base = jax.random.normal(first_key, (D, 3, D), jnp.float32) * weight_scale
    return base.astype(jnp.bfloat16)


def draw_lengths(key, part):
    key = jax.random.fold_in(key, 3)
    first_key, second_key = jax.random.split(key)
    drawn = jax.random.randint(first_key, (RECS,), LEN // 2, LEN + 1, dtype=jnp.int32)
    chosen = jax.random.randint(second_key, (), 0, RECS, dtype=jnp.int32)
    other = (chosen + 1) % RECS
    indices = jnp.arange(RECS, dtype=jnp.int32)
    drawn = jnp.where(indices == chosen, LEN, drawn)
    return jnp.where(indices == other, LEN // 2, drawn).astype(jnp.int32)


def level_of(rng, dims, shards, low, largest):
    level = 1.0
    for dim, blocks in shards:
        draws = jax.random.uniform(jax.random.fold_in(jax.random.fold_in(rng, 6), dim), (blocks,), jnp.float32, low / len(shards), largest / len(shards))
        level = level * jnp.repeat(jnp.exp(draws), dims[dim] // blocks).reshape((-1,) + (1,) * (len(dims) - 1 - dim))
    return level


def profile(count, total, bound, skew):
    weights = [(1 << 20) // math.isqrt(grade ** skew) + 1 for grade in range(2, count + 1)]
    surplus, given = total - bound - (count - 1), [1] * (count - 1)
    while surplus > 0:
        movable = [i for i in range(count - 1) if given[i] < bound]
        mass, budget = sum([weights[i] for i in movable]), surplus
        for i in movable:
            more = min(bound - given[i], max(1, budget * weights[i] // mass), surplus)
            given[i] = given[i] + more
            surplus = surplus - more
    return np.array([bound] + given)


def uneven_parts(stream_key, count, total, most, lean):
    if count == 2:
        one = jax.random.randint(stream_key, (), max(1, total - most), min(most, total - 1) + 1)
        return jnp.stack([one, total - one])
    sizes = jnp.asarray(profile(count, total, most, lean), jnp.int32)
    twos = (count - 1) // 2
    donor, taker = sizes[1:1 + 2 * twos:2], sizes[2:2 + 2 * twos:2]
    slack = jnp.minimum(donor - 1, most - taker)
    passed = jax.random.randint(jax.random.fold_in(stream_key, 1), (twos,), 0, 1 << 20) % (slack + 1)
    sizes = sizes.at[1:1 + 2 * twos:2].set(donor - passed).at[2:2 + 2 * twos:2].set(taker + passed)
    return sizes[jax.random.permutation(jax.random.fold_in(stream_key, 2), count)]


def noise(rng, shape, scale, reach, cuts=(), kind=jnp.bfloat16):
    result = jax.random.normal(rng, shape, jnp.float32) * scale
    if len(cuts) > 0:
        result = level_of(rng, shape, cuts, -0.22, 0.18) * result
    return jnp.clip(result, min=-reach, max=reach).astype(kind)


def setup_inputs(seed: int = 0) -> dict:
    key_of = jax.random.split(jax.random.key(seed), 9)
    tokens = noise(key_of[0], (RECS, LEN, D), 1.0, 6.0, ((0, 4), (1, 4)))
    cotangent = noise(key_of[1], (RECS, LEN, D), 1.0, 6.0, ((0, 4), (1, 4)))
    norm_gain = jnp.clip(1.0 + 0.1 * jax.random.normal(key_of[2], (D,), jnp.float32), 0.5, 1.5)
    norm_bias = noise(key_of[3], (D,), 0.5, 3.0, (), jnp.float32)
    qkv_weight = draw_qkv_weight(jax.random.fold_in(key_of[8], 71), 0)
    out_weight = noise(key_of[5], (D, D), (D // 16) ** -0.5, 0.625, ((0, 8),))
    lengths = draw_lengths(jax.random.fold_in(key_of[8], 71), 0)
    segments = jax.vmap(lambda own: jnp.searchsorted(jnp.cumsum(uneven_parts(own, 2 * LEN // CTX, LEN, CTX, 0)), jnp.arange(LEN), side="right"))(jax.random.split(key_of[7], RECS)).reshape((RECS, LEN)).astype(jnp.int32)
    return dict(tokens=tokens, cotangent=cotangent, norm_gain=norm_gain, norm_bias=norm_bias, qkv_weight=qkv_weight, out_weight=out_weight, lengths=lengths, segments=segments)


EPS = 1e-05
NEG = -1e+30

def normalize(tokens, norm_gain, norm_bias):
    values = tokens.astype(jnp.float32)
    centered = values - lax.optimization_barrier(jnp.mean(values, axis=-1, keepdims=True))
    inverse = lax.rsqrt(lax.optimization_barrier(jnp.mean(centered * centered, axis=-1, keepdims=True)) + EPS)
    scaled = centered * inverse
    return (scaled, inverse, (scaled * norm_gain + norm_bias).astype(jnp.bfloat16))

def head_pass(query, key_rows, value_rows, grad_rows, visible, live_rows):
    score_scale = HEAD ** (-0.5)
    scores = jnp.dot(query, key_rows.T, preferred_element_type=jnp.float32) * score_scale
    scores = jnp.where(visible, scores, NEG)
    highest = lax.optimization_barrier(jnp.max(scores, axis=-1, keepdims=True))
    weights = jnp.exp(scores - highest)
    weights = weights / lax.optimization_barrier(jnp.sum(weights, axis=-1, keepdims=True))
    rounded = weights.astype(jnp.bfloat16)
    mixed = jnp.dot(rounded, value_rows, preferred_element_type=jnp.float32) * live_rows[:, None]
    grad_weights = jnp.dot(grad_rows, value_rows.T, preferred_element_type=jnp.float32)
    grad_values = jnp.dot(rounded.T, grad_rows, preferred_element_type=jnp.float32)
    grad_scores = weights * (grad_weights - lax.optimization_barrier(jnp.sum(weights * grad_weights, axis=-1, keepdims=True))) * score_scale
    grad_scores = grad_scores.astype(jnp.bfloat16)
    grad_query = jnp.dot(grad_scores, key_rows, preferred_element_type=jnp.float32)
    grad_keys = jnp.dot(grad_scores.T, query, preferred_element_type=jnp.float32)
    return (mixed.astype(jnp.bfloat16), grad_query.astype(jnp.bfloat16), grad_keys.astype(jnp.bfloat16), grad_values.astype(jnp.bfloat16))

def recording(items):
    query, keys, values, grad_mixed, segment, length = items
    position = jnp.arange(LEN, dtype=jnp.int32)
    near = jnp.abs(position[:, None] - position[None, :]) <= CTX
    live_keys = (position[None, :] < length) | (position[:, None] == position[None, :])
    stretch = jnp.abs(segment[:, None] - segment[None, :]) <= 1
    visible = near & live_keys & stretch
    live_rows = (position < length).astype(jnp.float32)

    def one_head(pieces):
        return head_pass(pieces[0], pieces[1], pieces[2], pieces[3], visible, live_rows)
    results = lax.map(one_head, (query.transpose(1, 0, 2), keys.transpose(1, 0, 2), values.transpose(1, 0, 2), grad_mixed.transpose(1, 0, 2)))
    return tuple((item.transpose(1, 0, 2) for item in results))

def reference(tokens, cotangent, norm_gain, norm_bias, qkv_weight, out_weight, lengths, segments):
    scaled, inverse, normed = normalize(tokens, norm_gain, norm_bias)
    qkv = jnp.einsum('rfc,ckd->rfkd', normed.astype(jnp.float32), qkv_weight.astype(jnp.float32)).astype(jnp.bfloat16)
    query = qkv[:, :, 0].reshape(RECS, LEN, HEADS, HEAD)
    keys = qkv[:, :, 1].reshape(RECS, LEN, HEADS, HEAD)
    values = qkv[:, :, 2].reshape(RECS, LEN, HEADS, HEAD)
    live = (jnp.arange(LEN, dtype=jnp.int32)[None, :] < lengths[:, None]).astype(jnp.float32)
    grad_mixed = jnp.einsum('rfc,ac->rfa', cotangent.astype(jnp.float32), out_weight.astype(jnp.float32))
    grad_mixed = (grad_mixed * live[:, :, None]).astype(jnp.bfloat16).reshape(RECS, LEN, HEADS, HEAD)
    mixed, grad_query, grad_keys, grad_values = lax.map(recording, (query, keys, values, grad_mixed, segments, lengths))
    mixed_flat = mixed.reshape(RECS, LEN, D)
    attended = jnp.einsum('rfa,ac->rfc', mixed_flat.astype(jnp.float32), out_weight.astype(jnp.float32))
    output = (tokens.astype(jnp.float32) + attended).astype(jnp.bfloat16)
    grad_qkv = jnp.stack([grad_query, grad_keys, grad_values], axis=2).reshape(RECS, LEN, 3, D)
    back = jnp.einsum('rfkd,ckd->rfc', grad_qkv.astype(jnp.float32), qkv_weight.astype(jnp.float32))
    weighted = back * norm_gain
    first_mean = lax.optimization_barrier(jnp.mean(weighted, axis=-1, keepdims=True))
    second_mean = lax.optimization_barrier(jnp.mean(weighted * scaled, axis=-1, keepdims=True))
    grad_tokens = (inverse * (weighted - first_mean - scaled * second_mean) + cotangent.astype(jnp.float32)).astype(jnp.bfloat16)
    grad_inner = jnp.einsum('rfc,rfkd->ckd', normed.astype(jnp.float32), grad_qkv.astype(jnp.float32))
    grad_outer = jnp.einsum('rfc,rfa->ca', cotangent.astype(jnp.float32), mixed_flat.astype(jnp.float32))
    grad_proj = jnp.concatenate([grad_inner, grad_outer[:, None, :]], axis=1)
    return (output, grad_tokens, grad_proj)
```

```python
import jax
import jax.numpy as jnp
from jax import lax
from jax.experimental import pallas as pl
from jax.experimental.pallas import tpu as pltpu
from jax.sharding import PartitionSpec as P

HEAD = 64
CTX = 256
EPS = 1e-05
NEG = -1e30
VMEM_LIMIT = 50 * 1024 * 1024
SHIFTS = ((1, 0), (3, 0), (0, 1), (1, 1), (3, 1), (2, 0), (2, 1))

F32 = jnp.float32
BF16 = jnp.bfloat16


def params():
    return pltpu.CompilerParams(vmem_limit_bytes=VMEM_LIMIT)


def dot_nn(a, b):
    return lax.dot_general(a, b, (((1,), (0,)), ((), ())), preferred_element_type=F32)


def dot_nt(a, b):
    return lax.dot_general(a, b, (((1,), (1,)), ((), ())), preferred_element_type=F32)


def dot_tn(a, b):
    return lax.dot_general(a, b, (((0,), (0,)), ((), ())), preferred_element_type=F32)


def norm_stats(tokens):
    values = tokens.astype(F32)
    centered = values - jnp.mean(values, axis=-1, keepdims=True)
    inverse = lax.rsqrt(jnp.mean(centered * centered, axis=-1, keepdims=True) + EPS)
    return centered * inverse, inverse


def project_body(tok, cot, gain, bias, weight, out_w, live, normed, q, kv, g, kv_first, kv_last):
    width = q.shape[0]
    scaled, _ = norm_stats(tok[...])
    rows = (scaled * gain[...] + bias[...]).astype(BF16)
    normed[...] = rows
    qkv = dot_nt(weight[...], rows).astype(BF16)
    q[...] = qkv[:width]
    kv[...] = qkv[width:]
    step = pl.program_id(0)

    @pl.when(step % 2 == 0)
    def _():
        kv_first[...] = qkv[width:]

    @pl.when(step % 2 == 1)
    def _():
        kv_last[...] = qkv[width:]

    g[...] = (dot_nt(out_w[...], cot[...]) * live[...]).astype(BF16)


def project(tokens, cotangent, gain, bias, weight, out_w, live):
    rows, model = tokens.shape
    width = out_w.shape[0]
    full = lambda shape: pl.BlockSpec(shape, lambda i: (0, 0))
    by_row = pl.BlockSpec((CTX, model), lambda i: (i, 0))
    by_col = lambda n: pl.BlockSpec((n, CTX), lambda i: (0, i))
    by_half = pl.BlockSpec((2 * width, CTX), lambda i: (0, i // 2))
    return pl.pallas_call(
        project_body,
        grid=(rows // CTX,),
        in_specs=[
            by_row,
            by_row,
            full((1, model)),
            full((1, model)),
            full((3 * width, model)),
            full((width, model)),
            by_col(1),
        ],
        out_specs=[by_row, by_col(width), by_col(2 * width), by_col(width), by_half, by_half],
        out_shape=[
            jax.ShapeDtypeStruct((rows, model), BF16),
            jax.ShapeDtypeStruct((width, rows), BF16),
            jax.ShapeDtypeStruct((2 * width, rows), BF16),
            jax.ShapeDtypeStruct((width, rows), BF16),
            jax.ShapeDtypeStruct((2 * width, rows // 2), BF16),
            jax.ShapeDtypeStruct((2 * width, rows // 2), BF16),
        ],
        compiler_params=params(),
        name="project",
    )(tokens, cotangent, gain, bias, weight, out_w, live)


def attention_body(
    q, kv, before, after, g, seg_keys, seg_rows, live, mixed, dq, dkv, dbefore, dafter, acc, mask
):
    width = q.shape[0]
    span = 3 * CTX
    kv_all = jnp.concatenate([before[...], kv[...], after[...]], axis=1)
    q_small = q[...] * jnp.asarray(HEAD**-0.5, BF16)
    grads = g[...]
    acc[...] = jnp.zeros_like(acc)
    for tile in range(2):
        cols = slice(tile * CTX, (tile + 1) * CTX)
        keys = slice(tile * CTX, tile * CTX + span)
        away = (
            lax.broadcasted_iota(jnp.int32, (span, CTX), 0)
            - CTX
            - lax.broadcasted_iota(jnp.int32, (span, CTX), 1)
        )
        near = jnp.abs(away) <= CTX
        stretch = jnp.abs(seg_keys[0, keys, :] - seg_rows[0, :, cols]) <= 1
        visible = (near & stretch) | (away == 0)
        mask[...] = jnp.where(visible, 0.0, NEG)
        for head in range(width // HEAD):
            d = slice(head * HEAD, (head + 1) * HEAD)
            dv = slice(width + head * HEAD, width + (head + 1) * HEAD)
            k_t, v_t = kv_all[d, keys], kv_all[dv, keys]
            q_t, g_t = q_small[d, cols], grads[d, cols]
            scores = dot_tn(k_t, q_t) + mask[...]
            weights = jnp.exp(scores - jnp.max(scores, axis=0, keepdims=True))
            weights = weights * (1.0 / jnp.sum(weights, axis=0, keepdims=True))
            rounded = weights.astype(BF16)
            mixed[d, cols] = (dot_nn(v_t, rounded) * live[:, cols]).astype(BF16)
            grad_w = dot_tn(v_t, g_t)
            total = jnp.sum(weights * grad_w, axis=0, keepdims=True)
            grad_s = (weights * (grad_w - total)).astype(BF16)
            dq[d, cols] = (dot_nn(k_t, grad_s) * (HEAD**-0.5)).astype(BF16)
            acc[d, keys] += dot_nt(q_t, grad_s)
            acc[dv, keys] += dot_nt(g_t, rounded)
    frames = q.shape[1]
    dkv[...] = acc[:, CTX : CTX + frames]
    dbefore[...] = acc[:, :CTX].astype(BF16)
    dafter[...] = acc[:, CTX + frames :].astype(BF16)


def attention(q, kv, before, after, g, seg_keys, seg_rows, live):
    width, rows = q.shape
    recs, span, _ = seg_keys.shape
    frames = rows // recs
    by_rec = lambda n, m: pl.BlockSpec((n, m), lambda r: (0, r))
    return pl.pallas_call(
        attention_body,
        grid=(recs,),
        in_specs=[
            by_rec(width, frames),
            by_rec(2 * width, frames),
            by_rec(2 * width, CTX),
            by_rec(2 * width, CTX),
            by_rec(width, frames),
            pl.BlockSpec((1, span, 1), lambda r: (r, 0, 0)),
            pl.BlockSpec((1, 1, frames), lambda r: (r, 0, 0)),
            by_rec(1, frames),
        ],
        out_specs=[
            by_rec(width, frames),
            by_rec(width, frames),
            by_rec(2 * width, frames),
            by_rec(2 * width, CTX),
            by_rec(2 * width, CTX),
        ],
        out_shape=[
            jax.ShapeDtypeStruct((width, rows), BF16),
            jax.ShapeDtypeStruct((width, rows), BF16),
            jax.ShapeDtypeStruct((2 * width, rows), F32),
            jax.ShapeDtypeStruct((2 * width, recs * CTX), BF16),
            jax.ShapeDtypeStruct((2 * width, recs * CTX), BF16),
        ],
        scratch_shapes=[pltpu.VMEM((2 * width, span), F32), pltpu.VMEM((3 * CTX, CTX), F32)],
        compiler_params=params(),
        name="attention",
    )(q, kv, before, after, g, seg_keys, seg_rows, live)


def back_body(order, dq, own, left, right, weight, gkv, mine, *parts):
    step = pl.program_id(0)
    chunk = own.shape[1]
    half = CTX // chunk
    place = order[step] % (2 * half)
    beside = jnp.where(place < half, left[...].astype(F32), right[...].astype(F32))
    kv_grads = (own[...] + beside).astype(BF16)
    gkv[...] = kv_grads
    grads = jnp.concatenate([dq[...], kv_grads], axis=0)
    back = dot_tn(grads, weight[...])

    @pl.when(step == 0)
    def _():
        mine[...] = back

    for index, part in enumerate(parts):

        @pl.when(step == index + 1)
        def _(part=part):
            part[...] = back.astype(BF16)


def back_parts(order, dq, own, left, right, weight):
    width, rows = dq.shape
    model = weight.shape[1]
    count = len(SHIFTS) + 1
    chunk = rows // count
    half = CTX // chunk
    by_order = lambda n: pl.BlockSpec((n, chunk), lambda i, o: (0, o[i]))
    whole = pl.BlockSpec((chunk, model), lambda i, o: (0, 0))

    def edge(i, o):
        return (0, (o[i] // (2 * half)) * half + o[i] % half)

    return pl.pallas_call(
        back_body,
        grid_spec=pltpu.PrefetchScalarGridSpec(
            num_scalar_prefetch=1,
            grid=(count,),
            in_specs=[
                by_order(width),
                by_order(2 * width),
                pl.BlockSpec((2 * width, chunk), edge),
                pl.BlockSpec((2 * width, chunk), edge),
                pl.BlockSpec((3 * width, model), lambda i, o: (0, 0)),
            ],
            out_specs=[by_order(2 * width)] + [whole] * count,
        ),
        out_shape=[
            jax.ShapeDtypeStruct((2 * width, rows), BF16),
            jax.ShapeDtypeStruct((chunk, model), F32),
        ]
        + [jax.ShapeDtypeStruct((chunk, model), BF16)] * (count - 1),
        compiler_params=params(),
        name="back",
    )(order, dq, own, left, right, weight)


def finish_body(place, tok, cot, gain, mine, *rest):
    parts, out = rest[:-1], rest[-1]
    back = mine[...]
    for part in parts:
        back = back + part[...].astype(F32)
    scaled, inverse = norm_stats(tok[...])
    weighted = back * gain[...]
    first = jnp.mean(weighted, axis=-1, keepdims=True)
    second = jnp.mean(weighted * scaled, axis=-1, keepdims=True)
    grad = inverse * (weighted - first - scaled * second) + cot[...].astype(F32)
    out[...] = grad.astype(BF16)


def finish(place, tokens, cotangent, gain, mine, parts):
    chunk, model = mine.shape
    here = pl.BlockSpec((chunk, model), lambda i, p: (p[0], 0))
    whole = pl.BlockSpec((chunk, model), lambda i, p: (0, 0))
    return pl.pallas_call(
        finish_body,
        grid_spec=pltpu.PrefetchScalarGridSpec(
            num_scalar_prefetch=1,
            grid=(1,),
            in_specs=[here, here, pl.BlockSpec((1, model), lambda i, p: (0, 0))]
            + [whole] * (1 + len(parts)),
            out_specs=whole,
        ),
        out_shape=jax.ShapeDtypeStruct((chunk, model), BF16),
        compiler_params=params(),
        name="finish",
    )(place, tokens, cotangent, gain, mine, *parts)


def to_peer(array, shift):
    dz, dy = shift
    pairs = [
        (z * 2 + y, ((z + dz) % 4) * 2 + (y + dy) % 2) for z in range(4) for y in range(2)
    ]
    return lax.ppermute(array, "chan", pairs)


def peer_index(me, shift, sign):
    dz, dy = shift
    return ((me // 2 + sign * dz) % 4) * 2 + (me % 2 + dy) % 2


def scatter_grads(grads):
    batch, frame = lax.axis_index("batch"), lax.axis_index("frames")
    core, row = batch % 2, batch // 2
    grads = grads.reshape(2, 2, 4, -1, grads.shape[-1])
    pick = lambda array, index, axis: lax.dynamic_index_in_dim(array, index, axis, keepdims=False)
    sent = pick(grads, 1 - core, 1).astype(BF16)
    got = lax.ppermute(sent, "batch", [(0, 1), (1, 0), (2, 3), (3, 2)])
    pair = pick(grads, core, 1) + got.astype(F32)
    sums = pick(pair, frame, 1)
    for shift in (1, 3, 2):
        sent = pick(pair, (frame + shift) % 4, 1).astype(BF16)
        got = lax.ppermute(sent, "frames", [(i, (i + shift) % 4) for i in range(4)])
        sums = sums + got.astype(F32)
    sent = pick(sums, 1 - row, 0).astype(BF16)
    got = lax.ppermute(sent, "batch", [(0, 2), (1, 3), (2, 0), (3, 1)])
    return pick(sums, row, 0) + got.astype(F32)


def shards(tokens, cotangent, norm_gain, norm_bias, qkv_weight, out_weight, lengths, segments):
    recs, frames, model = tokens.shape
    rows = recs * frames
    width = out_weight.shape[0]
    me = lax.axis_index("chan")
    start = lax.axis_index("frames") * frames

    full_out = lax.all_gather(out_weight, "chan", tiled=True)

    flat_tokens = tokens.reshape(rows, model)
    flat_cot = cotangent.reshape(rows, model)
    gain = norm_gain.reshape(1, model)
    weight = qkv_weight.transpose(1, 2, 0).reshape(3 * width, model)
    position = start + jnp.arange(frames, dtype=jnp.int32)
    reach = start - CTX + jnp.arange(frames + 2 * CTX, dtype=jnp.int32)
    live = (position[None, :] < lengths[:, None]).astype(F32).reshape(1, rows)
    padded = jnp.pad(segments, ((0, 0), (CTX, CTX)), constant_values=-10)
    seg_keys = lax.dynamic_slice_in_dim(padded, start, frames + 2 * CTX, 1)
    seg_keys = jnp.where(reach[None, :] < lengths[:, None], seg_keys, -10)[:, :, None]
    seg_rows = lax.dynamic_slice_in_dim(segments, start, frames, 1)[:, None, :]

    normed, q, kv, g, kv_first, kv_last = project(
        flat_tokens, flat_cot, gain, norm_bias.reshape(1, model), weight, out_weight, live
    )
    size = lax.axis_size("frames")
    up = [(i, i + 1) for i in range(size - 1)]
    down = [(i + 1, i) for i in range(size - 1)]
    before = lax.ppermute(kv_last, "frames", up)
    after = lax.ppermute(kv_first, "frames", down)
    mixed, dq, dkv, dbefore, dafter = attention(
        q, kv, before, after, g, seg_keys, seg_rows, live
    )
    from_right = lax.ppermute(dbefore, "frames", down)
    from_left = lax.ppermute(dafter, "frames", up)

    full_mixed = lax.all_gather(mixed, "chan", tiled=True)

    order = jnp.stack([me] + [peer_index(me, shift, 1) for shift in SHIFTS]).astype(jnp.int32)
    gkv, mine, *parts = back_parts(order, dq, dkv, from_left, from_right, weight)
    got = [to_peer(part, shift) for part, shift in zip(parts, SHIFTS)]
    piece = finish(me.reshape(1).astype(jnp.int32), flat_tokens, flat_cot, gain, mine, got)

    chunk = piece.shape[0]
    grad_tokens = jnp.zeros((rows, model), BF16)
    grad_tokens = lax.dynamic_update_slice_in_dim(grad_tokens, piece, me * chunk, 0)
    for shift in SHIFTS:
        other = to_peer(piece, shift)
        place = peer_index(me, shift, -1) * chunk
        grad_tokens = lax.dynamic_update_slice_in_dim(grad_tokens, other, place, 0)

    inner = lax.dot_general(
        normed,
        jnp.concatenate([dq, gkv], axis=0),
        (((0,), (1,)), ((), ())),
        preferred_element_type=F32,
    )
    outer = lax.dot_general(
        flat_cot, mixed, (((0,), (1,)), ((), ())), preferred_element_type=F32
    )
    grad_proj = scatter_grads(jnp.concatenate([inner, outer], axis=1))
    grad_proj = grad_proj.reshape(-1, 4, width)

    output = (flat_tokens.astype(F32) + dot_tn(full_mixed, full_out)).astype(BF16)
    shape = (recs, frames, model)
    return (output.reshape(shape), grad_tokens.reshape(shape), grad_proj)


def solution(mesh):
    return jax.shard_map(
        shards,
        mesh=mesh,
        in_specs=(
            P("batch", "frames", None),
            P("batch", "frames", None),
            P(),
            P(),
            P(None, None, "chan"),
            P("chan", None),
            P("batch"),
            P("batch", None),
        ),
        out_specs=(
            P("batch", "frames", None),
            P("batch", "frames", None),
            P(("batch", "frames"), None, "chan"),
        ),
        check_vma=False,
    )
```

```python
import jax
import jax.numpy as jnp
from jax import lax
from jax.experimental import pallas as pl
from jax.experimental.pallas import tpu as pltpu
from jax.sharding import PartitionSpec as P

HEAD = 64
CTX = 256
EPS = 1e-05
NEG = -1e30
VMEM_LIMIT = 50 * 1024 * 1024
SHIFTS = ((1, 0), (3, 0), (0, 1), (1, 1), (3, 1), (2, 0), (2, 1))
SPREAD = (0, 1, 2, 3)

F32 = jnp.float32
BF16 = jnp.bfloat16


def params():
    return pltpu.CompilerParams(vmem_limit_bytes=VMEM_LIMIT)


def dot_nn(a, b):
    return lax.dot_general(a, b, (((1,), (0,)), ((), ())), preferred_element_type=F32)


def dot_nt(a, b):
    return lax.dot_general(a, b, (((1,), (1,)), ((), ())), preferred_element_type=F32)


def dot_tn(a, b):
    return lax.dot_general(a, b, (((0,), (0,)), ((), ())), preferred_element_type=F32)


def norm_stats(tokens):
    values = tokens.astype(F32)
    centered = values - jnp.mean(values, axis=-1, keepdims=True)
    inverse = lax.rsqrt(jnp.mean(centered * centered, axis=-1, keepdims=True) + EPS)
    return centered * inverse, inverse


def project_body(
    lengths, tok, cot, gain, bias, weight, out_w, normed, q, kv, g, kv_first, kv_last, live
):
    width = q.shape[0]
    scaled, _ = norm_stats(tok[...])
    rows = (scaled * gain[...][None, :] + bias[...][None, :]).astype(BF16)
    normed[...] = rows
    qkv = dot_nt(weight[...], rows).astype(BF16)
    q[...] = qkv[:width]
    kv[...] = qkv[width:]
    step = pl.program_id(0)

    @pl.when(step % 2 == 0)
    def _():
        kv_first[...] = qkv[width:]

    @pl.when(step % 2 == 1)
    def _():
        kv_last[...] = qkv[width:]

    start = lax.axis_index("frames") * (2 * CTX) + (step % 2) * CTX
    position = start + lax.broadcasted_iota(jnp.int32, (1, CTX), 1)
    alive = jnp.where(position < lengths[step // 2], 1.0, 0.0)
    live[...] = alive
    g[...] = (dot_nt(out_w[...], cot[...]) * alive).astype(BF16)


def project(lengths, tokens, cotangent, gain, bias, weight, out_w):
    rows, model = tokens.shape
    width = out_w.shape[0]
    full = lambda shape: pl.BlockSpec(shape, lambda i: (0,) * len(shape))
    by_row = pl.BlockSpec((CTX, model), lambda i: (i, 0))
    by_col = lambda n: pl.BlockSpec((n, CTX), lambda i: (0, i))
    by_half = pl.BlockSpec((2 * width, CTX), lambda i: (0, i // 2))
    return pl.pallas_call(
        project_body,
        grid=(rows // CTX,),
        in_specs=[
            pl.BlockSpec(memory_space=pltpu.SMEM),
            by_row,
            by_row,
            full((model,)),
            full((model,)),
            full((3 * width, model)),
            full((width, model)),
        ],
        out_specs=[
            by_row,
            by_col(width),
            by_col(2 * width),
            by_col(width),
            by_half,
            by_half,
            by_col(1),
        ],
        out_shape=[
            jax.ShapeDtypeStruct((rows, model), BF16),
            jax.ShapeDtypeStruct((width, rows), BF16),
            jax.ShapeDtypeStruct((2 * width, rows), BF16),
            jax.ShapeDtypeStruct((width, rows), BF16),
            jax.ShapeDtypeStruct((2 * width, rows // 2), BF16),
            jax.ShapeDtypeStruct((2 * width, rows // 2), BF16),
            jax.ShapeDtypeStruct((1, rows), F32),
        ],
        compiler_params=params(),
        cost_estimate=pl.CostEstimate(flops=2400000000, bytes_accessed=15000000, transcendentals=0),
        name="project",
    )(lengths, tokens, cotangent, gain, bias, weight, out_w)


def attention_body(
    q,
    kv,
    before,
    after,
    g,
    seg_keys,
    seg_rows,
    live,
    mixed,
    dq,
    dkv,
    dbefore,
    dafter,
    peer_grads,
    peer_before,
    peer_after,
    acc,
    mask,
):
    width = q.shape[0]
    span = 3 * CTX
    kv_all = jnp.concatenate([before[...], kv[...], after[...]], axis=1)
    q_small = q[...] * jnp.asarray(HEAD**-0.5, BF16)
    grads = g[...]
    acc[...] = jnp.zeros_like(acc)
    for tile in range(2):
        cols = slice(tile * CTX, (tile + 1) * CTX)
        keys = slice(tile * CTX, tile * CTX + span)
        away = (
            lax.broadcasted_iota(jnp.int32, (span, CTX), 0)
            - CTX
            - lax.broadcasted_iota(jnp.int32, (span, CTX), 1)
        )
        near = jnp.abs(away) <= CTX
        stretch = jnp.abs(seg_keys[0, keys, :] - seg_rows[0, :, cols]) <= 1
        visible = (near & stretch) | (away == 0)
        mask[...] = jnp.where(visible, 0.0, NEG)
        for head in range(width // HEAD):
            d = slice(head * HEAD, (head + 1) * HEAD)
            dv = slice(width + head * HEAD, width + (head + 1) * HEAD)
            k_t, v_t = kv_all[d, keys], kv_all[dv, keys]
            q_t, g_t = q_small[d, cols], grads[d, cols]
            scores = dot_tn(k_t, q_t) + mask[...]
            weights = jnp.exp(scores - jnp.max(scores, axis=0, keepdims=True))
            weights = weights * (1.0 / jnp.sum(weights, axis=0, keepdims=True))
            rounded = weights.astype(BF16)
            mixed[d, cols] = (dot_nn(v_t, rounded) * live[:, cols]).astype(BF16)
            grad_w = dot_tn(v_t, g_t)
            total = jnp.sum(weights * grad_w, axis=0, keepdims=True)
            grad_s = (weights * (grad_w - total)).astype(BF16)
            dq[d, cols] = (dot_nn(k_t, grad_s) * (HEAD**-0.5)).astype(BF16)
            acc[d, keys] += dot_nt(q_t, grad_s)
            acc[dv, keys] += dot_nt(g_t, rounded)
    frames = q.shape[1]
    dkv[...] = acc[:, CTX : CTX + frames]
    dbefore[...] = acc[:, :CTX].astype(BF16)
    dafter[...] = acc[:, CTX + frames :].astype(BF16)

    @pl.when(pl.program_id(0) != lax.axis_index("chan") % 2)
    def _():
        peer_grads[:width, :] = dq[...]
        peer_grads[width:, :] = acc[:, CTX : CTX + frames].astype(BF16)
        peer_before[...] = dbefore[...]
        peer_after[...] = dafter[...]


def attention(q, kv, before, after, g, seg_keys, seg_rows, live):
    width, rows = q.shape
    recs, span, _ = seg_keys.shape
    frames = rows // recs
    by_rec = lambda n, m: pl.BlockSpec((n, m), lambda r: (0, r))
    fixed = lambda n, m: pl.BlockSpec((n, m), lambda r: (0, 0))
    return pl.pallas_call(
        attention_body,
        grid=(recs,),
        in_specs=[
            by_rec(width, frames),
            by_rec(2 * width, frames),
            by_rec(2 * width, CTX),
            by_rec(2 * width, CTX),
            by_rec(width, frames),
            pl.BlockSpec((1, span, 1), lambda r: (r, 0, 0)),
            pl.BlockSpec((1, 1, frames), lambda r: (r, 0, 0)),
            by_rec(1, frames),
        ],
        out_specs=[
            by_rec(width, frames),
            by_rec(width, frames),
            by_rec(2 * width, frames),
            by_rec(2 * width, CTX),
            by_rec(2 * width, CTX),
            fixed(3 * width, frames),
            fixed(2 * width, CTX),
            fixed(2 * width, CTX),
        ],
        out_shape=[
            jax.ShapeDtypeStruct((width, rows), BF16),
            jax.ShapeDtypeStruct((width, rows), BF16),
            jax.ShapeDtypeStruct((2 * width, rows), F32),
            jax.ShapeDtypeStruct((2 * width, recs * CTX), BF16),
            jax.ShapeDtypeStruct((2 * width, recs * CTX), BF16),
            jax.ShapeDtypeStruct((3 * width, frames), BF16),
            jax.ShapeDtypeStruct((2 * width, CTX), BF16),
            jax.ShapeDtypeStruct((2 * width, CTX), BF16),
        ],
        scratch_shapes=[pltpu.VMEM((2 * width, span), F32), pltpu.VMEM((3 * CTX, CTX), F32)],
        compiler_params=params(),
        cost_estimate=pl.CostEstimate(flops=2400000000, bytes_accessed=8000000, transcendentals=0),
        name="attention",
    )(q, kv, before, after, g, seg_keys, seg_rows, live)


def back_body(
    here, dq, own, left, right, peer, peer_left, peer_right, weight, peer_weight, mine, *rest
):
    parts, (flipped, sums) = rest[:-2], rest[-2:]
    width = dq.shape[0]
    chunk = mine.shape[0]

    @pl.when(pl.program_id(0) == 0)
    def _():
        beside = jnp.concatenate([left[...], right[...]], axis=1).astype(F32)
        peer_beside = jnp.concatenate([peer_left[...], peer_right[...]], axis=1).astype(F32)
        flipped[:, :width] = dq[...].T
        flipped[:, width : 3 * width] = (own[...] + beside).astype(BF16).T
        flipped[:, 3 * width : 4 * width] = peer[:width, :].T
        flipped[:, 4 * width :] = (peer[width:, :].astype(F32) + peer_beside).astype(BF16).T

    sums[...] = dot_nn(flipped[:, : 3 * width], weight[...]) + dot_nn(
        flipped[:, 3 * width :], peer_weight[...]
    )
    z = here[0] >> 1
    for index, part in enumerate((mine,) + parts):
        rows = pl.ds(pl.multiple_of(((z + index) & 3) * chunk, chunk), chunk)
        part[...] = sums[rows, :].astype(part.dtype)


def back_parts(here, dq, own, left, right, peer, peer_left, peer_right, weight, peer_weight):
    width = dq.shape[0]
    frames = peer.shape[1]
    model = weight.shape[1]
    chunk = frames // 4
    tile = 256
    full = lambda n, m: pl.BlockSpec((n, m), lambda i, h: (0, 0))
    by_rec = lambda n, m: pl.BlockSpec((n, m), lambda i, h: (0, h[0] & 1))
    by_col = lambda n: pl.BlockSpec((n, tile), lambda i, h: (0, i))
    return pl.pallas_call(
        back_body,
        grid_spec=pltpu.PrefetchScalarGridSpec(
            num_scalar_prefetch=1,
            grid=(model // tile,),
            in_specs=[
                by_rec(width, frames),
                by_rec(2 * width, frames),
                by_rec(2 * width, CTX),
                by_rec(2 * width, CTX),
                full(3 * width, frames),
                full(2 * width, CTX),
                full(2 * width, CTX),
                by_col(3 * width),
                by_col(3 * width),
            ],
            out_specs=[by_col(chunk)] * 4,
            scratch_shapes=[
                pltpu.VMEM((frames, 6 * width), BF16),
                pltpu.VMEM((frames, tile), F32),
            ],
        ),
        out_shape=[jax.ShapeDtypeStruct((chunk, model), F32)]
        + [jax.ShapeDtypeStruct((chunk, model), BF16)] * 3,
        compiler_params=params(),
        cost_estimate=pl.CostEstimate(flops=1800000000, bytes_accessed=8000000, transcendentals=0),
        name="back",
    )(here, dq, own, left, right, peer, peer_left, peer_right, weight, peer_weight)


def weight_grads_body(normed, cot, dq, own, left, right, mixed, sent, kept, gkv):
    width = dq.shape[0]

    @pl.when(pl.program_id(0) == 0)
    def _():
        beside = []
        for rec in range(own.shape[1] // (2 * CTX)):
            cols = slice(rec * CTX, (rec + 1) * CTX)
            beside += [left[:, cols], right[:, cols]]
        gkv[...] = (own[...] + jnp.concatenate(beside, axis=1).astype(F32)).astype(BF16)

    turned = normed[...].T
    sums = [
        dot_nt(turned, dq[...]),
        dot_nt(turned, gkv[...]),
        dot_nt(cot[...].T, mixed[...]),
    ]
    offsets = (0, width, 3 * width)

    @pl.when(pl.program_id(0) < 2)
    def _():
        for part, offset in zip(sums, offsets):
            sent[0, :, offset : offset + part.shape[1]] = part.astype(BF16)

    @pl.when(pl.program_id(0) >= 2)
    def _():
        for part, offset in zip(sums, offsets):
            kept[0, :, offset : offset + part.shape[1]] = part


def weight_grads(core, normed, cotangent, dq, own, left, right, mixed):
    rows, model = normed.shape
    width = dq.shape[0]
    block = model // 4

    def by_step(i, c):
        return (0, (i % 2) * 2 + jnp.where(i < 2, 1 - c[0], c[0]))

    full = lambda n: pl.BlockSpec((n, rows), lambda i, c: (0, 0))
    half = pl.BlockSpec((2 * width, rows // 2), lambda i, c: (0, 0))
    return pl.pallas_call(
        lambda c, *refs: weight_grads_body(*refs),
        grid_spec=pltpu.PrefetchScalarGridSpec(
            num_scalar_prefetch=1,
            grid=(4,),
            in_specs=[
                pl.BlockSpec((rows, block), by_step),
                pl.BlockSpec((rows, block), by_step),
                full(width),
                full(2 * width),
                half,
                half,
                full(width),
            ],
            out_specs=[
                pl.BlockSpec((1, block, 4 * width), lambda i, c: (jnp.minimum(i, 1), 0, 0)),
                pl.BlockSpec((1, block, 4 * width), lambda i, c: (jnp.maximum(i, 2) - 2, 0, 0)),
            ],
            scratch_shapes=[pltpu.VMEM((2 * width, rows), BF16)],
        ),
        out_shape=[
            jax.ShapeDtypeStruct((2, block, 4 * width), BF16),
            jax.ShapeDtypeStruct((2, block, 4 * width), F32),
        ],
        compiler_params=params(),
        cost_estimate=pl.CostEstimate(flops=2400000000, bytes_accessed=12000000, transcendentals=0),
        name="weight_grads",
    )(core, normed, cotangent, dq, own, left, right, mixed)


def output_body(tok, near, far, weight, out, stacked):
    me = lax.axis_index("chan")
    depth = weight.shape[0]
    width = depth // (2 * len(SPREAD))
    for index, dz in enumerate(SPREAD):
        rows = slice(index * width, (index + 1) * width)
        for side, source in ((0, near), (1, far)):
            chan = (((me >> 1) - dz) & 3) * 2 + ((me & 1) ^ side)
            place = pl.ds(pl.multiple_of(chan * width, width), width)
            stacked[place, :] = source[rows, :]
    total = tok[...].astype(F32) + dot_nn(stacked[...].T, weight[...])
    out[...] = total.astype(BF16)


def output_rows(tokens, near, far, weight):
    rows, model = tokens.shape
    by_row = pl.BlockSpec((CTX, model), lambda i: (i, 0))
    by_col = pl.BlockSpec((near.shape[0], CTX), lambda i: (0, i))
    return pl.pallas_call(
        output_body,
        grid=(rows // CTX,),
        in_specs=[by_row, by_col, by_col, pl.BlockSpec(weight.shape, lambda i: (0, 0))],
        out_specs=by_row,
        out_shape=jax.ShapeDtypeStruct((rows, model), BF16),
        scratch_shapes=[pltpu.VMEM((weight.shape[0], CTX), BF16)],
        compiler_params=params(),
        cost_estimate=pl.CostEstimate(flops=4800000000, bytes_accessed=14000000, transcendentals=0),
        name="output",
    )(tokens, near, far, weight)


def finish_body(place, tok, cot, gain, mine, *rest):
    parts, out = rest[:-1], rest[-1]
    back = mine[...]
    for part in parts:
        back = back + part[...].astype(F32)
    scaled, inverse = norm_stats(tok[...])
    weighted = back * gain[...][None, :]
    first = jnp.mean(weighted, axis=-1, keepdims=True)
    second = jnp.mean(weighted * scaled, axis=-1, keepdims=True)
    grad = inverse * (weighted - first - scaled * second) + cot[...].astype(F32)
    out[...] = grad.astype(BF16)


def finish(place, tokens, cotangent, gain, mine, parts):
    chunk, model = mine.shape
    here = pl.BlockSpec((chunk, model), lambda i, p: (p[0], 0))
    whole = pl.BlockSpec((chunk, model), lambda i, p: (0, 0))
    return pl.pallas_call(
        finish_body,
        grid_spec=pltpu.PrefetchScalarGridSpec(
            num_scalar_prefetch=1,
            grid=(1,),
            in_specs=[here, here, pl.BlockSpec((model,), lambda i, p: (0,))]
            + [whole] * (1 + len(parts)),
            out_specs=whole,
        ),
        out_shape=jax.ShapeDtypeStruct((chunk, model), BF16),
        compiler_params=params(),
        cost_estimate=pl.CostEstimate(flops=10000000, bytes_accessed=5000000, transcendentals=0),
        name="finish",
    )(place, tokens, cotangent, gain, mine, *parts)


def assemble_body(places, *refs):
    pieces, out, sems = refs[:-2], refs[-2], refs[-1]
    chunk = pieces[0].shape[0]
    copies = []
    for index, piece in enumerate(pieces):
        rows = pl.ds(pl.multiple_of(places[index] * chunk, chunk), chunk)
        copies.append(pltpu.make_async_copy(piece, out.at[rows, :], sems.at[index]))
    for copy in copies:
        copy.start()
    for copy in copies:
        copy.wait()


def assemble(places, pieces):
    chunk, model = pieces[0].shape
    count = len(pieces)
    anywhere = pl.BlockSpec(memory_space=pl.ANY)
    return pl.pallas_call(
        assemble_body,
        in_specs=[pl.BlockSpec(memory_space=pltpu.SMEM)] + [anywhere] * count,
        out_specs=anywhere,
        out_shape=jax.ShapeDtypeStruct((count * chunk, model), BF16),
        scratch_shapes=[pltpu.SemaphoreType.DMA((count,))],
        compiler_params=params(),
        cost_estimate=pl.CostEstimate(flops=0, bytes_accessed=6000000, transcendentals=0),
        name="assemble",
    )(places, *pieces)


def to_peer(array, shift):
    dz, dy = shift
    pairs = [
        (z * 2 + y, ((z + dz) % 4) * 2 + (y + dy) % 2) for z in range(4) for y in range(2)
    ]
    return lax.ppermute(array, "chan", pairs)


def piece_index(me, shift):
    dz, dy = shift
    return ((me & 1) ^ dy) * 4 + (((me >> 1) - dz) & 3)


def pick(array, index, axis):
    return lax.dynamic_index_in_dim(array, index, axis, keepdims=False)


def pair_sums(got, kept):
    frame = lax.axis_index("frames")
    pair = (kept + got.astype(F32)).reshape(2, 4, -1, kept.shape[-1])
    sums = pick(pair, frame, 1)
    for shift in (1, 3, 2):
        sent = pick(pair, (frame + shift) & 3, 1).astype(BF16)
        got = lax.ppermute(sent, "frames", [(i, (i + shift) % 4) for i in range(4)])
        sums = sums + got.astype(F32)
    return sums


def row_sums(sums):
    row = lax.axis_index("batch") >> 1
    sent = pick(sums, 1 - row, 0).astype(BF16)
    got = lax.ppermute(sent, "batch", [(0, 2), (1, 3), (2, 0), (3, 1)])
    return pick(sums, row, 0) + got.astype(F32)


def shards(tokens, cotangent, norm_gain, norm_bias, qkv_weight, out_weight, lengths, segments):
    recs, frames, model = tokens.shape
    rows = recs * frames
    width = out_weight.shape[0]
    me = lax.axis_index("chan")
    start = lax.axis_index("frames") * frames
    scalar = lambda value: value.reshape(1).astype(jnp.int32)

    weight = qkv_weight.transpose(1, 2, 0).reshape(3 * width, model)
    peer_weight = to_peer(weight, (0, 1))
    full_out = lax.all_gather(out_weight, "chan", tiled=True)

    flat_tokens = tokens.reshape(rows, model)
    flat_cot = cotangent.reshape(rows, model)
    reach = start - CTX + jnp.arange(frames + 2 * CTX, dtype=jnp.int32)
    padded = jnp.pad(segments, ((0, 0), (CTX, CTX)), constant_values=-10)
    seg_keys = lax.dynamic_slice_in_dim(padded, start, frames + 2 * CTX, 1)
    seg_keys = jnp.where(reach[None, :] < lengths[:, None], seg_keys, -10)[:, :, None]
    seg_rows = lax.dynamic_slice_in_dim(segments, start, frames, 1)[:, None, :]

    normed, q, kv, g, kv_first, kv_last, live = project(
        lengths, flat_tokens, flat_cot, norm_gain, norm_bias, weight, out_weight
    )
    size = lax.axis_size("frames")
    up = [(i, i + 1) for i in range(size - 1)]
    down = [(i + 1, i) for i in range(size - 1)]
    before = lax.ppermute(kv_last, "frames", up)
    after = lax.ppermute(kv_first, "frames", down)
    mixed, dq, dkv, dbefore, dafter, peer_grads, peer_before, peer_after = attention(
        q, kv, before, after, g, seg_keys, seg_rows, live
    )
    tie = lax.optimization_barrier
    dbefore, dafter, peer_grads, peer_before, peer_after, peer_weight = tie(
        (dbefore, dafter, peer_grads, peer_before, peer_after, peer_weight)
    )
    cross = lambda pairs: [(a * 8 + c, b * 8 + (c ^ 1)) for a, b in pairs for c in range(8)]
    both = ("frames", "chan")
    peer_grads = to_peer(peer_grads, (0, 1))
    peer_right = lax.ppermute(peer_before, both, cross(down))
    peer_left = lax.ppermute(peer_after, both, cross(up))
    from_right = lax.ppermute(dbefore, "frames", down)
    from_left = lax.ppermute(dafter, "frames", up)

    late_mixed, from_left, from_right = tie((mixed, from_left, from_right))
    core = scalar(lax.axis_index("batch") & 1)
    sent, kept = weight_grads(core, normed, flat_cot, dq, dkv, from_left, from_right, mixed)
    sent, peer_grads, peer_left, peer_right = tie((sent, peer_grads, peer_left, peer_right))

    mine, *parts = back_parts(
        scalar(me),
        dq,
        dkv,
        from_left,
        from_right,
        peer_grads,
        peer_left,
        peer_right,
        weight,
        peer_weight,
    )
    near = [to_peer(late_mixed, (dz, 0)) for dz in SPREAD[1:]]
    got = [to_peer(part, (dz, 0)) for part, dz in zip(parts, SPREAD[1:])]
    pair = lax.ppermute(sent, "batch", [(0, 1), (1, 0), (2, 3), (3, 2)])
    near, pair, got[0] = tie((near, pair, got[0]))
    near_mixed = jnp.concatenate([mixed] + near, axis=0)
    sums = pair_sums(pair, kept)
    far_mixed = to_peer(near_mixed, (0, 1))
    sums, full_out = tie((sums, full_out))

    here = piece_index(me, (0, 0))
    piece = finish(scalar(here), flat_tokens, flat_cot, norm_gain, mine, got)

    places = jnp.stack([here] + [piece_index(me, shift) for shift in SHIFTS]).astype(jnp.int32)
    grad_tokens = assemble(places, [piece] + [to_peer(piece, shift) for shift in SHIFTS])
    grad_proj = row_sums(sums).reshape(-1, 4, width)
    output = output_rows(flat_tokens, near_mixed, far_mixed, full_out)
    shape = (recs, frames, model)
    return (output.reshape(shape), grad_tokens.reshape(shape), grad_proj)


def solution(mesh):
    return jax.shard_map(
        shards,
        mesh=mesh,
        in_specs=(
            P("batch", "frames", None),
            P("batch", "frames", None),
            P(),
            P(),
            P(None, None, "chan"),
            P("chan", None),
            P("batch"),
            P("batch", None),
        ),
        out_specs=(
            P("batch", "frames", None),
            P("batch", "frames", None),
            P(("batch", "frames"), None, "chan"),
        ),
        check_vma=False,
    )
```

```python
import jax
import jax.numpy as jnp
from jax import lax
from jax.experimental import pallas as pl
from jax.experimental.pallas import tpu as pltpu
from jax.sharding import PartitionSpec as P

HEAD = 64
CTX = 256
EPS = 1e-05
NEG = -1e30
VMEM_LIMIT = 60 * 1024 * 1024
SHIFTS = ((1, 0), (3, 0), (0, 1), (1, 1), (3, 1), (2, 0), (2, 1))
SPREAD = (0, 1, 2, 3)

F32 = jnp.float32
BF16 = jnp.bfloat16


def params():
    return pltpu.CompilerParams(vmem_limit_bytes=VMEM_LIMIT)


def dot_nn(a, b):
    return lax.dot_general(a, b, (((1,), (0,)), ((), ())), preferred_element_type=F32)


def dot_nt(a, b):
    return lax.dot_general(a, b, (((1,), (1,)), ((), ())), preferred_element_type=F32)


def dot_tn(a, b):
    return lax.dot_general(a, b, (((0,), (0,)), ((), ())), preferred_element_type=F32)


def norm_stats(tokens):
    values = tokens.astype(F32)
    centered = values - jnp.mean(values, axis=-1, keepdims=True)
    inverse = lax.rsqrt(jnp.mean(centered * centered, axis=-1, keepdims=True) + EPS)
    return centered * inverse, inverse


def project_body(
    lengths, tok, cot, gain, bias, weight, out_w, normed, q, kv, g, kv_first, kv_last, live
):
    width = q.shape[0]
    scaled, _ = norm_stats(tok[...])
    rows = (scaled * gain[...][None, :] + bias[...][None, :]).astype(BF16)
    normed[...] = rows
    qkv = dot_nt(weight[...], rows).astype(BF16)
    q[...] = qkv[:width]
    kv[...] = qkv[width:]
    step = pl.program_id(0)

    @pl.when(step % 2 == 0)
    def _():
        kv_first[...] = qkv[width:]

    @pl.when(step % 2 == 1)
    def _():
        kv_last[...] = qkv[width:]

    start = lax.axis_index("frames") * (2 * CTX) + (step % 2) * CTX
    position = start + lax.broadcasted_iota(jnp.int32, (1, CTX), 1)
    alive = jnp.where(position < lengths[step // 2], 1.0, 0.0)
    live[...] = alive
    g[...] = (dot_nt(out_w[...], cot[...]) * alive).astype(BF16)


def project(lengths, tokens, cotangent, gain, bias, weight, out_w):
    rows, model = tokens.shape
    width = out_w.shape[0]
    full = lambda shape: pl.BlockSpec(shape, lambda i: (0,) * len(shape))
    by_row = pl.BlockSpec((CTX, model), lambda i: (i, 0))
    by_col = lambda n: pl.BlockSpec((n, CTX), lambda i: (0, i))
    by_half = pl.BlockSpec((2 * width, CTX), lambda i: (0, i // 2))
    return pl.pallas_call(
        project_body,
        grid=(rows // CTX,),
        in_specs=[
            pl.BlockSpec(memory_space=pltpu.SMEM),
            by_row,
            by_row,
            full((model,)),
            full((model,)),
            full((3 * width, model)),
            full((width, model)),
        ],
        out_specs=[
            by_row,
            by_col(width),
            by_col(2 * width),
            by_col(width),
            by_half,
            by_half,
            by_col(1),
        ],
        out_shape=[
            jax.ShapeDtypeStruct((rows, model), BF16),
            jax.ShapeDtypeStruct((width, rows), BF16),
            jax.ShapeDtypeStruct((2 * width, rows), BF16),
            jax.ShapeDtypeStruct((width, rows), BF16),
            jax.ShapeDtypeStruct((2 * width, rows // 2), BF16),
            jax.ShapeDtypeStruct((2 * width, rows // 2), BF16),
            jax.ShapeDtypeStruct((1, rows), F32),
        ],
        compiler_params=params(),
        cost_estimate=pl.CostEstimate(flops=2400000000, bytes_accessed=15000000, transcendentals=0),
        name="project",
    )(lengths, tokens, cotangent, gain, bias, weight, out_w)


def attention_body(
    q,
    kv,
    before,
    after,
    g,
    seg_keys,
    seg_rows,
    live,
    mixed,
    dq,
    dkv,
    dbefore,
    dafter,
    peer_grads,
    peer_before,
    peer_after,
    acc,
    mask,
):
    width = q.shape[0]
    span = 3 * CTX
    kv_all = jnp.concatenate([before[...], kv[...], after[...]], axis=1)
    q_small = q[...] * jnp.asarray(HEAD**-0.5, BF16)
    grads = g[...]
    acc[...] = jnp.zeros_like(acc)
    for tile in range(2):
        cols = slice(tile * CTX, (tile + 1) * CTX)
        keys = slice(tile * CTX, tile * CTX + span)
        away = (
            lax.broadcasted_iota(jnp.int32, (span, CTX), 0)
            - CTX
            - lax.broadcasted_iota(jnp.int32, (span, CTX), 1)
        )
        near = jnp.abs(away) <= CTX
        stretch = jnp.abs(seg_keys[0, keys, :] - seg_rows[0, :, cols]) <= 1
        visible = (near & stretch) | (away == 0)
        mask[...] = jnp.where(visible, 0.0, NEG)
        for head in range(width // HEAD):
            d = slice(head * HEAD, (head + 1) * HEAD)
            dv = slice(width + head * HEAD, width + (head + 1) * HEAD)
            k_t, v_t = kv_all[d, keys], kv_all[dv, keys]
            q_t, g_t = q_small[d, cols], grads[d, cols]
            scores = dot_tn(k_t, q_t) + mask[...]
            weights = jnp.exp(scores - jnp.max(scores, axis=0, keepdims=True))
            weights = weights * (1.0 / jnp.sum(weights, axis=0, keepdims=True))
            rounded = weights.astype(BF16)
            mixed[d, cols] = (dot_nn(v_t, rounded) * live[:, cols]).astype(BF16)
            grad_w = dot_tn(v_t, g_t)
            total = jnp.sum(weights * grad_w, axis=0, keepdims=True)
            grad_s = (weights * (grad_w - total)).astype(BF16)
            dq[d, cols] = (dot_nn(k_t, grad_s) * (HEAD**-0.5)).astype(BF16)
            acc[d, keys] += dot_nt(q_t, grad_s)
            acc[dv, keys] += dot_nt(g_t, rounded)
    frames = q.shape[1]
    dkv[...] = acc[:, CTX : CTX + frames]
    dbefore[...] = acc[:, :CTX].astype(BF16)
    dafter[...] = acc[:, CTX + frames :].astype(BF16)

    @pl.when(pl.program_id(0) != lax.axis_index("chan") % 2)
    def _():
        peer_grads[:width, :] = dq[...]
        peer_grads[width:, :] = acc[:, CTX : CTX + frames].astype(BF16)
        peer_before[...] = dbefore[...]
        peer_after[...] = dafter[...]


def attention(q, kv, before, after, g, seg_keys, seg_rows, live):
    width, rows = q.shape
    recs, span, _ = seg_keys.shape
    frames = rows // recs
    by_rec = lambda n, m: pl.BlockSpec((n, m), lambda r: (0, r))
    fixed = lambda n, m: pl.BlockSpec((n, m), lambda r: (0, 0))
    return pl.pallas_call(
        attention_body,
        grid=(recs,),
        in_specs=[
            by_rec(width, frames),
            by_rec(2 * width, frames),
            by_rec(2 * width, CTX),
            by_rec(2 * width, CTX),
            by_rec(width, frames),
            pl.BlockSpec((1, span, 1), lambda r: (r, 0, 0)),
            pl.BlockSpec((1, 1, frames), lambda r: (r, 0, 0)),
            by_rec(1, frames),
        ],
        out_specs=[
            by_rec(width, frames),
            by_rec(width, frames),
            by_rec(2 * width, frames),
            by_rec(2 * width, CTX),
            by_rec(2 * width, CTX),
            fixed(3 * width, frames),
            fixed(2 * width, CTX),
            fixed(2 * width, CTX),
        ],
        out_shape=[
            jax.ShapeDtypeStruct((width, rows), BF16),
            jax.ShapeDtypeStruct((width, rows), BF16),
            jax.ShapeDtypeStruct((2 * width, rows), F32),
            jax.ShapeDtypeStruct((2 * width, recs * CTX), BF16),
            jax.ShapeDtypeStruct((2 * width, recs * CTX), BF16),
            jax.ShapeDtypeStruct((3 * width, frames), BF16),
            jax.ShapeDtypeStruct((2 * width, CTX), BF16),
            jax.ShapeDtypeStruct((2 * width, CTX), BF16),
        ],
        scratch_shapes=[pltpu.VMEM((2 * width, span), F32), pltpu.VMEM((3 * CTX, CTX), F32)],
        compiler_params=params(),
        cost_estimate=pl.CostEstimate(flops=2400000000, bytes_accessed=8000000, transcendentals=0),
        name="attention",
    )(q, kv, before, after, g, seg_keys, seg_rows, live)


def back_body(
    here, dq, own, left, right, peer, peer_left, peer_right, weight, peer_weight, mine, *rest
):
    parts, (flipped, sums) = rest[:-2], rest[-2:]
    width = dq.shape[0]
    chunk = mine.shape[0]

    @pl.when(pl.program_id(0) == 0)
    def _():
        beside = jnp.concatenate([left[...], right[...]], axis=1).astype(F32)
        peer_beside = jnp.concatenate([peer_left[...], peer_right[...]], axis=1).astype(F32)
        flipped[:, :width] = dq[...].T
        flipped[:, width : 3 * width] = (own[...] + beside).astype(BF16).T
        flipped[:, 3 * width : 4 * width] = peer[:width, :].T
        flipped[:, 4 * width :] = (peer[width:, :].astype(F32) + peer_beside).astype(BF16).T

    sums[...] = dot_nn(flipped[:, : 3 * width], weight[...]) + dot_nn(
        flipped[:, 3 * width :], peer_weight[...]
    )
    z = here[0] >> 1
    for index, part in enumerate((mine,) + parts):
        rows = pl.ds(pl.multiple_of(((z + index) & 3) * chunk, chunk), chunk)
        part[...] = sums[rows, :].astype(part.dtype)


def back_parts(here, dq, own, left, right, peer, peer_left, peer_right, weight, peer_weight):
    width = dq.shape[0]
    frames = peer.shape[1]
    model = weight.shape[1]
    chunk = frames // 4
    tile = 256
    full = lambda n, m: pl.BlockSpec((n, m), lambda i, h: (0, 0))
    by_rec = lambda n, m: pl.BlockSpec((n, m), lambda i, h: (0, h[0] & 1))
    by_col = lambda n: pl.BlockSpec((n, tile), lambda i, h: (0, i))
    return pl.pallas_call(
        back_body,
        grid_spec=pltpu.PrefetchScalarGridSpec(
            num_scalar_prefetch=1,
            grid=(model // tile,),
            in_specs=[
                by_rec(width, frames),
                by_rec(2 * width, frames),
                by_rec(2 * width, CTX),
                by_rec(2 * width, CTX),
                full(3 * width, frames),
                full(2 * width, CTX),
                full(2 * width, CTX),
                by_col(3 * width),
                by_col(3 * width),
            ],
            out_specs=[by_col(chunk)] * 4,
            scratch_shapes=[
                pltpu.VMEM((frames, 6 * width), BF16),
                pltpu.VMEM((frames, tile), F32),
            ],
        ),
        out_shape=[jax.ShapeDtypeStruct((chunk, model), F32)]
        + [jax.ShapeDtypeStruct((chunk, model), BF16)] * 3,
        compiler_params=params(),
        cost_estimate=pl.CostEstimate(flops=1800000000, bytes_accessed=8000000, transcendentals=0),
        name="back",
    )(here, dq, own, left, right, peer, peer_left, peer_right, weight, peer_weight)


def weight_grads_body(normed, cot, dq, own, left, right, mixed, sent, kept, gkv):
    width = dq.shape[0]

    @pl.when(pl.program_id(0) == 0)
    def _():
        beside = []
        for rec in range(own.shape[1] // (2 * CTX)):
            cols = slice(rec * CTX, (rec + 1) * CTX)
            beside += [left[:, cols], right[:, cols]]
        gkv[...] = (own[...] + jnp.concatenate(beside, axis=1).astype(F32)).astype(BF16)

    turned = normed[...].T
    sums = [
        dot_nt(turned, dq[...]),
        dot_nt(turned, gkv[...]),
        dot_nt(cot[...].T, mixed[...]),
    ]
    offsets = (0, width, 3 * width)

    @pl.when(pl.program_id(0) < 2)
    def _():
        for part, offset in zip(sums, offsets):
            shape = (sent.shape[0], sent.shape[2], part.shape[1])
            sent[:, 0, :, offset : offset + part.shape[1]] = part.astype(BF16).reshape(shape)

    @pl.when(pl.program_id(0) >= 2)
    def _():
        for part, offset in zip(sums, offsets):
            shape = (kept.shape[0], kept.shape[2], part.shape[1])
            kept[:, 0, :, offset : offset + part.shape[1]] = part.reshape(shape)


def weight_grads(core, normed, cotangent, dq, own, left, right, mixed):
    rows, model = normed.shape
    width = dq.shape[0]
    block = model // 4

    def by_step(i, c):
        return (0, (i % 2) * 2 + jnp.where(i < 2, 1 - c[0], c[0]))

    full = lambda n: pl.BlockSpec((n, rows), lambda i, c: (0, 0))
    half = pl.BlockSpec((2 * width, rows // 2), lambda i, c: (0, 0))
    part = (4, 1, block // 4, 4 * width)
    return pl.pallas_call(
        lambda c, *refs: weight_grads_body(*refs),
        grid_spec=pltpu.PrefetchScalarGridSpec(
            num_scalar_prefetch=1,
            grid=(4,),
            in_specs=[
                pl.BlockSpec((rows, block), by_step),
                pl.BlockSpec((rows, block), by_step),
                full(width),
                full(2 * width),
                half,
                half,
                full(width),
            ],
            out_specs=[
                pl.BlockSpec(part, lambda i, c: (0, jnp.minimum(i, 1), 0, 0)),
                pl.BlockSpec(part, lambda i, c: (0, jnp.maximum(i, 2) - 2, 0, 0)),
            ],
            scratch_shapes=[pltpu.VMEM((2 * width, rows), BF16)],
        ),
        out_shape=[
            jax.ShapeDtypeStruct((4, 2, block // 4, 4 * width), BF16),
            jax.ShapeDtypeStruct((4, 2, block // 4, 4 * width), F32),
        ],
        compiler_params=params(),
        cost_estimate=pl.CostEstimate(flops=2400000000, bytes_accessed=12000000, transcendentals=0),
        name="weight_grads",
    )(core, normed, cotangent, dq, own, left, right, mixed)


def output_body(tok, near, far, near_weight, far_weight, out, near_stack, far_stack):
    z = lax.axis_index("chan") >> 1
    width = near.shape[0] // len(SPREAD)
    for index, dz in enumerate(SPREAD):
        rows = slice(index * width, (index + 1) * width)
        place = pl.ds(pl.multiple_of(((z - dz) & 3) * width, width), width)
        near_stack[place, :] = near[rows, :]
        far_stack[place, :] = far[rows, :]
    total = dot_nn(near_stack[...].T, near_weight[...])
    total = total + dot_nn(far_stack[...].T, far_weight[...])
    out[...] = (tok[...].astype(F32) + total).astype(BF16)


def output_rows(tokens, near, far, near_weight, far_weight):
    rows, model = tokens.shape
    depth = near.shape[0]
    by_row = pl.BlockSpec((CTX, model), lambda i: (i, 0))
    by_col = pl.BlockSpec((depth, CTX), lambda i: (0, i))
    full = pl.BlockSpec((depth, model), lambda i: (0, 0))
    return pl.pallas_call(
        output_body,
        grid=(rows // CTX,),
        in_specs=[by_row, by_col, by_col, full, full],
        out_specs=by_row,
        out_shape=jax.ShapeDtypeStruct((rows, model), BF16),
        scratch_shapes=[pltpu.VMEM((depth, CTX), BF16)] * 2,
        compiler_params=params(),
        cost_estimate=pl.CostEstimate(flops=4800000000, bytes_accessed=14000000, transcendentals=0),
        name="output",
    )(tokens, near, far, near_weight, far_weight)


def finish_body(place, tok, cot, gain, mine, *rest):
    parts, out = rest[:-1], rest[-1]
    back = mine[...]
    for part in parts:
        back = back + part[...].astype(F32)
    scaled, inverse = norm_stats(tok[...])
    weighted = back * gain[...][None, :]
    first = jnp.mean(weighted, axis=-1, keepdims=True)
    second = jnp.mean(weighted * scaled, axis=-1, keepdims=True)
    grad = inverse * (weighted - first - scaled * second) + cot[...].astype(F32)
    out[...] = grad.astype(BF16)


def finish(place, tokens, cotangent, gain, mine, parts):
    chunk, model = mine.shape
    here = pl.BlockSpec((chunk, model), lambda i, p: (p[0], 0))
    whole = pl.BlockSpec((chunk, model), lambda i, p: (0, 0))
    return pl.pallas_call(
        finish_body,
        grid_spec=pltpu.PrefetchScalarGridSpec(
            num_scalar_prefetch=1,
            grid=(1,),
            in_specs=[here, here, pl.BlockSpec((model,), lambda i, p: (0,))]
            + [whole] * (1 + len(parts)),
            out_specs=whole,
        ),
        out_shape=jax.ShapeDtypeStruct((chunk, model), BF16),
        compiler_params=params(),
        cost_estimate=pl.CostEstimate(flops=10000000, bytes_accessed=5000000, transcendentals=0),
        name="finish",
    )(place, tokens, cotangent, gain, mine, *parts)


def copy_all(pieces, out, sems, places):
    chunk = pieces[0].shape[0]
    copies = []
    for index, (piece, place) in enumerate(zip(pieces, places)):
        rows = pl.ds(pl.multiple_of(place * chunk, chunk), chunk)
        copies.append(pltpu.make_async_copy(piece, out.at[rows, :], sems.at[index]))
    for copy in copies:
        copy.start()
    for copy in copies:
        copy.wait()


def assemble_body(places, *refs):
    copy_all(refs[:-2], refs[-2], refs[-1], [places[i] for i in range(len(refs) - 2)])


def stack_body(*refs):
    copy_all(refs[:-2], refs[-2], refs[-1], range(len(refs) - 2))


def stack(pieces, places=None):
    chunk, model = pieces[0].shape
    count = len(pieces)
    anywhere = pl.BlockSpec(memory_space=pl.ANY)
    ordered = places is not None
    return pl.pallas_call(
        assemble_body if ordered else stack_body,
        in_specs=[pl.BlockSpec(memory_space=pltpu.SMEM)] * ordered + [anywhere] * count,
        out_specs=anywhere,
        out_shape=jax.ShapeDtypeStruct((count * chunk, model), BF16),
        scratch_shapes=[pltpu.SemaphoreType.DMA((count,))],
        compiler_params=params(),
        cost_estimate=pl.CostEstimate(flops=0, bytes_accessed=6000000, transcendentals=0),
        name="assemble" if ordered else "stack",
    )(*([places] if ordered else []), *pieces)


def to_peer(array, shift):
    dz, dy = shift
    pairs = [
        (z * 2 + y, ((z + dz) % 4) * 2 + (y + dy) % 2) for z in range(4) for y in range(2)
    ]
    return lax.ppermute(array, "chan", pairs)


def piece_index(me, shift):
    dz, dy = shift
    return ((me & 1) ^ dy) * 4 + (((me >> 1) - dz) & 3)


def pick(array, index, axis):
    return lax.dynamic_index_in_dim(array, index, axis, keepdims=False)


def pair_sums(got, kept):
    pair = (kept + got.astype(F32)).astype(BF16)
    return lax.psum_scatter(pair, "frames", scatter_dimension=0)


def row_sums(sums):
    row = lax.axis_index("batch") >> 1
    got = lax.ppermute(pick(sums, 1 - row, 0), "batch", [(0, 2), (1, 3), (2, 0), (3, 1)])
    return pick(sums, row, 0).astype(F32) + got.astype(F32)


def shards(tokens, cotangent, norm_gain, norm_bias, qkv_weight, out_weight, lengths, segments):
    recs, frames, model = tokens.shape
    rows = recs * frames
    width = out_weight.shape[0]
    me = lax.axis_index("chan")
    start = lax.axis_index("frames") * frames
    scalar = lambda value: value.reshape(1).astype(jnp.int32)

    weight = qkv_weight.transpose(1, 2, 0).reshape(3 * width, model)
    over_z = lambda array: lax.all_gather(
        array, "chan", axis_index_groups=[[0, 2, 4, 6], [1, 3, 5, 7]], tiled=True
    )
    near_out = over_z(out_weight)
    peer_out = to_peer(out_weight, (0, 1))
    peer_weight = to_peer(weight, (0, 1))

    flat_tokens = tokens.reshape(rows, model)
    flat_cot = cotangent.reshape(rows, model)
    reach = start - CTX + jnp.arange(frames + 2 * CTX, dtype=jnp.int32)
    padded = jnp.pad(segments, ((0, 0), (CTX, CTX)), constant_values=-10)
    seg_keys = lax.dynamic_slice_in_dim(padded, start, frames + 2 * CTX, 1)
    seg_keys = jnp.where(reach[None, :] < lengths[:, None], seg_keys, -10)[:, :, None]
    seg_rows = lax.dynamic_slice_in_dim(segments, start, frames, 1)[:, None, :]

    normed, q, kv, g, kv_first, kv_last, live = project(
        lengths, flat_tokens, flat_cot, norm_gain, norm_bias, weight, out_weight
    )
    size = lax.axis_size("frames")
    up = [(i, i + 1) for i in range(size - 1)]
    down = [(i + 1, i) for i in range(size - 1)]
    tie = lax.optimization_barrier
    kv_first, kv_last, peer_out = tie((kv_first, kv_last, peer_out))
    far_out = over_z(peer_out)
    before = lax.ppermute(kv_last, "frames", up)
    after = lax.ppermute(kv_first, "frames", down)
    mixed, dq, dkv, dbefore, dafter, peer_grads, peer_before, peer_after = attention(
        q, kv, before, after, g, seg_keys, seg_rows, live
    )
    dbefore, dafter, peer_grads, peer_before, peer_after, peer_weight = tie(
        (dbefore, dafter, peer_grads, peer_before, peer_after, peer_weight)
    )
    cross = lambda pairs: [(a * 8 + c, b * 8 + (c ^ 1)) for a, b in pairs for c in range(8)]
    both = ("frames", "chan")
    peer_grads = to_peer(peer_grads, (0, 1))
    peer_right = lax.ppermute(peer_before, both, cross(down))
    peer_left = lax.ppermute(peer_after, both, cross(up))
    from_right = lax.ppermute(dbefore, "frames", down)
    from_left = lax.ppermute(dafter, "frames", up)

    late_mixed, from_left, from_right, peer_left, peer_right = tie(
        (mixed, from_left, from_right, peer_left, peer_right)
    )
    near = [to_peer(late_mixed, (dz, 0)) for dz in SPREAD[1:]]
    core = scalar(lax.axis_index("batch") & 1)
    sent, kept = weight_grads(core, normed, flat_cot, dq, dkv, from_left, from_right, mixed)
    near_mixed = stack([mixed] + near)
    sent, near_mixed, peer_grads, near_out, far_out = tie(
        (sent, near_mixed, peer_grads, near_out, far_out)
    )

    mine, *parts = back_parts(
        scalar(me),
        dq,
        dkv,
        from_left,
        from_right,
        peer_grads,
        peer_left,
        peer_right,
        weight,
        peer_weight,
    )
    got = [to_peer(part, (dz, 0)) for part, dz in zip(parts, SPREAD[1:])]
    pair = lax.ppermute(sent, "batch", [(0, 1), (1, 0), (2, 3), (3, 2)])
    pair, got = tie((pair, got))
    sums = pair_sums(pair, kept)
    far_mixed = to_peer(near_mixed, (0, 1))

    here = piece_index(me, (0, 0))
    piece = finish(scalar(here), flat_tokens, flat_cot, norm_gain, mine, got)

    places = jnp.stack([here] + [piece_index(me, shift) for shift in SHIFTS]).astype(jnp.int32)
    grad_tokens = stack([piece] + [to_peer(piece, shift) for shift in SHIFTS], places)
    grad_proj = row_sums(sums).reshape(-1, 4, width)
    output = output_rows(flat_tokens, near_mixed, far_mixed, near_out, far_out)
    shape = (recs, frames, model)
    return (output.reshape(shape), grad_tokens.reshape(shape), grad_proj)


def solution(mesh):
    return jax.shard_map(
        shards,
        mesh=mesh,
        in_specs=(
            P("batch", "frames", None),
            P("batch", "frames", None),
            P(),
            P(),
            P(None, None, "chan"),
            P("chan", None),
            P("batch"),
            P("batch", None),
        ),
        out_specs=(
            P("batch", "frames", None),
            P("batch", "frames", None),
            P(("batch", "frames"), None, "chan"),
        ),
        check_vma=False,
    )
```

```python
import jax
import jax.numpy as jnp
from jax import lax
from jax.experimental import pallas as pl
from jax.experimental.pallas import tpu as pltpu
from jax.sharding import PartitionSpec as P

HEAD = 64
CTX = 256
EPS = 1e-05
NEG = -1e30
VMEM_LIMIT = 60 * 1024 * 1024

F32 = jnp.float32
BF16 = jnp.bfloat16


def params():
    return pltpu.CompilerParams(vmem_limit_bytes=VMEM_LIMIT)


def dot_nn(a, b):
    return lax.dot_general(a, b, (((1,), (0,)), ((), ())), preferred_element_type=F32)


def dot_nt(a, b):
    return lax.dot_general(a, b, (((1,), (1,)), ((), ())), preferred_element_type=F32)


def dot_tn(a, b):
    return lax.dot_general(a, b, (((0,), (0,)), ((), ())), preferred_element_type=F32)


def norm_stats(tokens):
    values = tokens.astype(F32)
    centered = values - jnp.mean(values, axis=-1, keepdims=True)
    inverse = lax.rsqrt(jnp.mean(centered * centered, axis=-1, keepdims=True) + EPS)
    return centered * inverse, inverse


def project_body(
    lengths, tok, cot, gain, bias, weight, out_w, normed, q, kv, g, kv_first, kv_last, live
):
    width = q.shape[0]
    scaled, _ = norm_stats(tok[...])
    rows = (scaled * gain[...][None, :] + bias[...][None, :]).astype(BF16)
    normed[...] = rows
    qkv = dot_nt(weight[...], rows).astype(BF16)
    q[...] = qkv[:width]
    kv[...] = qkv[width:]
    step = pl.program_id(0)

    @pl.when(step % 2 == 0)
    def _():
        kv_first[...] = qkv[width:]

    @pl.when(step % 2 == 1)
    def _():
        kv_last[...] = qkv[width:]

    start = lax.axis_index("frames") * (2 * CTX) + (step % 2) * CTX
    position = start + lax.broadcasted_iota(jnp.int32, (1, CTX), 1)
    alive = jnp.where(position < lengths[step // 2], 1.0, 0.0)
    live[...] = alive
    g[...] = (dot_nt(out_w[...], cot[...]) * alive).astype(BF16)


def project(lengths, tokens, cotangent, gain, bias, weight, out_w):
    rows, model = tokens.shape
    width = out_w.shape[0]
    full = lambda shape: pl.BlockSpec(shape, lambda i: (0,) * len(shape))
    by_row = pl.BlockSpec((CTX, model), lambda i: (i, 0))
    by_col = lambda n: pl.BlockSpec((n, CTX), lambda i: (0, i))
    by_half = pl.BlockSpec((2 * width, CTX), lambda i: (0, i // 2))
    return pl.pallas_call(
        project_body,
        grid=(rows // CTX,),
        in_specs=[
            pl.BlockSpec(memory_space=pltpu.SMEM),
            by_row,
            by_row,
            full((model,)),
            full((model,)),
            full((3 * width, model)),
            full((width, model)),
        ],
        out_specs=[
            by_row,
            by_col(width),
            by_col(2 * width),
            by_col(width),
            by_half,
            by_half,
            by_col(1),
        ],
        out_shape=[
            jax.ShapeDtypeStruct((rows, model), BF16),
            jax.ShapeDtypeStruct((width, rows), BF16),
            jax.ShapeDtypeStruct((2 * width, rows), BF16),
            jax.ShapeDtypeStruct((width, rows), BF16),
            jax.ShapeDtypeStruct((2 * width, rows // 2), BF16),
            jax.ShapeDtypeStruct((2 * width, rows // 2), BF16),
            jax.ShapeDtypeStruct((1, rows), F32),
        ],
        compiler_params=params(),
        cost_estimate=pl.CostEstimate(flops=2400000000, bytes_accessed=15000000, transcendentals=0),
        name="project",
    )(lengths, tokens, cotangent, gain, bias, weight, out_w)


def attention_body(
    q, kv, before, after, g, seg_keys, seg_rows, live, mixed, dq, dkv, dbefore, dafter, acc, mask
):
    width = q.shape[0]
    span = 3 * CTX
    kv_all = jnp.concatenate([before[...], kv[...], after[...]], axis=1)
    q_small = q[...] * jnp.asarray(HEAD**-0.5, BF16)
    grads = g[...]
    acc[...] = jnp.zeros_like(acc)
    for tile in range(2):
        cols = slice(tile * CTX, (tile + 1) * CTX)
        keys = slice(tile * CTX, tile * CTX + span)
        away = (
            lax.broadcasted_iota(jnp.int32, (span, CTX), 0)
            - CTX
            - lax.broadcasted_iota(jnp.int32, (span, CTX), 1)
        )
        near = jnp.abs(away) <= CTX
        stretch = jnp.abs(seg_keys[0, keys, :] - seg_rows[0, :, cols]) <= 1
        visible = (near & stretch) | (away == 0)
        mask[...] = jnp.where(visible, 0.0, NEG)
        for head in range(width // HEAD):
            d = slice(head * HEAD, (head + 1) * HEAD)
            dv = slice(width + head * HEAD, width + (head + 1) * HEAD)
            k_t, v_t = kv_all[d, keys], kv_all[dv, keys]
            q_t, g_t = q_small[d, cols], grads[d, cols]
            scores = dot_tn(k_t, q_t) + mask[...]
            weights = jnp.exp(scores - jnp.max(scores, axis=0, keepdims=True))
            weights = weights * (1.0 / jnp.sum(weights, axis=0, keepdims=True))
            rounded = weights.astype(BF16)
            mixed[d, cols] = (dot_nn(v_t, rounded) * live[:, cols]).astype(BF16)
            grad_w = dot_tn(v_t, g_t)
            total = jnp.sum(weights * grad_w, axis=0, keepdims=True)
            grad_s = (weights * (grad_w - total)).astype(BF16)
            dq[d, cols] = (dot_nn(k_t, grad_s) * (HEAD**-0.5)).astype(BF16)
            acc[d, keys] += dot_nt(q_t, grad_s)
            acc[dv, keys] += dot_nt(g_t, rounded)
    frames = q.shape[1]
    dkv[...] = acc[:, CTX : CTX + frames]
    dbefore[...] = acc[:, :CTX].astype(BF16)
    dafter[...] = acc[:, CTX + frames :].astype(BF16)


def attention(q, kv, before, after, g, seg_keys, seg_rows, live):
    width, rows = q.shape
    recs, span, _ = seg_keys.shape
    frames = rows // recs
    by_rec = lambda n, m: pl.BlockSpec((n, m), lambda r: (0, r))
    return pl.pallas_call(
        attention_body,
        grid=(recs,),
        in_specs=[
            by_rec(width, frames),
            by_rec(2 * width, frames),
            by_rec(2 * width, CTX),
            by_rec(2 * width, CTX),
            by_rec(width, frames),
            pl.BlockSpec((1, span, 1), lambda r: (r, 0, 0)),
            pl.BlockSpec((1, 1, frames), lambda r: (r, 0, 0)),
            by_rec(1, frames),
        ],
        out_specs=[
            by_rec(width, frames),
            by_rec(width, frames),
            by_rec(2 * width, frames),
            by_rec(2 * width, CTX),
            by_rec(2 * width, CTX),
        ],
        out_shape=[
            jax.ShapeDtypeStruct((width, rows), BF16),
            jax.ShapeDtypeStruct((width, rows), BF16),
            jax.ShapeDtypeStruct((2 * width, rows), F32),
            jax.ShapeDtypeStruct((2 * width, recs * CTX), BF16),
            jax.ShapeDtypeStruct((2 * width, recs * CTX), BF16),
        ],
        scratch_shapes=[pltpu.VMEM((2 * width, span), F32), pltpu.VMEM((3 * CTX, CTX), F32)],
        compiler_params=params(),
        cost_estimate=pl.CostEstimate(flops=2400000000, bytes_accessed=8000000, transcendentals=0),
        name="attention",
    )(q, kv, before, after, g, seg_keys, seg_rows, live)


def back_body(dq, own, left, right, weight, out, flipped):
    width = dq.shape[0]

    @pl.when(pl.program_id(0) == 0)
    def _():
        beside = []
        for rec in range(own.shape[1] // (2 * CTX)):
            cols = slice(rec * CTX, (rec + 1) * CTX)
            beside += [left[:, cols], right[:, cols]]
        beside = jnp.concatenate(beside, axis=1).astype(F32)
        flipped[:, :width] = dq[...].T
        flipped[:, width:] = (own[...] + beside).astype(BF16).T

    out[...] = dot_nn(flipped[...], weight[...]).astype(BF16)


def back_rows(dq, own, left, right, weight):
    width, rows = dq.shape
    model = weight.shape[1]
    tile = 256
    full = lambda n, m: pl.BlockSpec((n, m), lambda i: (0, 0))
    by_col = lambda n: pl.BlockSpec((n, tile), lambda i: (0, i))
    return pl.pallas_call(
        back_body,
        grid=(model // tile,),
        in_specs=[
            full(width, rows),
            full(2 * width, rows),
            full(2 * width, rows // 2),
            full(2 * width, rows // 2),
            by_col(3 * width),
        ],
        out_specs=by_col(rows),
        out_shape=jax.ShapeDtypeStruct((rows, model), BF16),
        scratch_shapes=[pltpu.VMEM((rows, 3 * width), BF16)],
        compiler_params=params(),
        cost_estimate=pl.CostEstimate(flops=1800000000, bytes_accessed=8000000, transcendentals=0),
        name="back",
    )(dq, own, left, right, weight)


def weight_grads_body(normed, cot, dq, own, left, right, mixed, sent, kept, gkv):
    width = dq.shape[0]

    @pl.when(pl.program_id(0) == 0)
    def _():
        beside = []
        for rec in range(own.shape[1] // (2 * CTX)):
            cols = slice(rec * CTX, (rec + 1) * CTX)
            beside += [left[:, cols], right[:, cols]]
        gkv[...] = (own[...] + jnp.concatenate(beside, axis=1).astype(F32)).astype(BF16)

    turned = normed[...].T
    sums = [
        dot_nt(turned, dq[...]),
        dot_nt(turned, gkv[...]),
        dot_nt(cot[...].T, mixed[...]),
    ]
    offsets = (0, width, 3 * width)

    @pl.when(pl.program_id(0) < 2)
    def _():
        for part, offset in zip(sums, offsets):
            shape = (sent.shape[0], sent.shape[2], part.shape[1])
            sent[:, 0, :, offset : offset + part.shape[1]] = part.astype(BF16).reshape(shape)

    @pl.when(pl.program_id(0) >= 2)
    def _():
        for part, offset in zip(sums, offsets):
            shape = (kept.shape[0], kept.shape[2], part.shape[1])
            kept[:, 0, :, offset : offset + part.shape[1]] = part.reshape(shape)


def weight_grads(core, normed, cotangent, dq, own, left, right, mixed):
    rows, model = normed.shape
    width = dq.shape[0]
    block = model // 4

    def by_step(i, c):
        return (0, (i % 2) * 2 + jnp.where(i < 2, 1 - c[0], c[0]))

    full = lambda n: pl.BlockSpec((n, rows), lambda i, c: (0, 0))
    half = pl.BlockSpec((2 * width, rows // 2), lambda i, c: (0, 0))
    part = (4, 1, block // 4, 4 * width)
    return pl.pallas_call(
        lambda c, *refs: weight_grads_body(*refs),
        grid_spec=pltpu.PrefetchScalarGridSpec(
            num_scalar_prefetch=1,
            grid=(4,),
            in_specs=[
                pl.BlockSpec((rows, block), by_step),
                pl.BlockSpec((rows, block), by_step),
                full(width),
                full(2 * width),
                half,
                half,
                full(width),
            ],
            out_specs=[
                pl.BlockSpec(part, lambda i, c: (0, jnp.minimum(i, 1), 0, 0)),
                pl.BlockSpec(part, lambda i, c: (0, jnp.maximum(i, 2) - 2, 0, 0)),
            ],
            scratch_shapes=[pltpu.VMEM((2 * width, rows), BF16)],
        ),
        out_shape=[
            jax.ShapeDtypeStruct((4, 2, block // 4, 4 * width), BF16),
            jax.ShapeDtypeStruct((4, 2, block // 4, 4 * width), F32),
        ],
        compiler_params=params(),
        cost_estimate=pl.CostEstimate(flops=1000, bytes_accessed=1000, transcendentals=0),
        name="weight_grads",
    )(core, normed, cotangent, dq, own, left, right, mixed)


def output_body(tok, near, far, near_weight, far_weight, out):
    total = dot_nn(near[...].T, near_weight[...]) + dot_nn(far[...].T, far_weight[...])
    out[...] = (tok[...].astype(F32) + total).astype(BF16)


def output_rows(tokens, near, far, near_weight, far_weight):
    rows, model = tokens.shape
    depth = near.shape[0]
    by_row = pl.BlockSpec((CTX, model), lambda i: (i, 0))
    by_col = pl.BlockSpec((depth, CTX), lambda i: (0, i))
    full = pl.BlockSpec((depth, model), lambda i: (0, 0))
    return pl.pallas_call(
        output_body,
        grid=(rows // CTX,),
        in_specs=[by_row, by_col, by_col, full, full],
        out_specs=by_row,
        out_shape=jax.ShapeDtypeStruct((rows, model), BF16),
        compiler_params=params(),
        cost_estimate=pl.CostEstimate(flops=1000, bytes_accessed=1000, transcendentals=0),
        name="output",
    )(tokens, near, far, near_weight, far_weight)


def finish_body(place, tok, cot, gain, parts, out):
    back = jnp.sum(parts[...].astype(F32), axis=0)
    scaled, inverse = norm_stats(tok[...])
    weighted = back * gain[...][None, :]
    first = jnp.mean(weighted, axis=-1, keepdims=True)
    second = jnp.mean(weighted * scaled, axis=-1, keepdims=True)
    grad = inverse * (weighted - first - scaled * second) + cot[...].astype(F32)
    out[...] = jnp.broadcast_to(grad.astype(BF16)[None], out.shape)


def finish(place, tokens, cotangent, gain, parts):
    count, chunk, model = parts.shape
    here = pl.BlockSpec((chunk, model), lambda i, p: (p[0], 0))
    whole = pl.BlockSpec((count, chunk, model), lambda i, p: (0, 0, 0))
    return pl.pallas_call(
        finish_body,
        grid_spec=pltpu.PrefetchScalarGridSpec(
            num_scalar_prefetch=1,
            grid=(1,),
            in_specs=[here, here, pl.BlockSpec((model,), lambda i, p: (0,)), whole],
            out_specs=whole,
        ),
        out_shape=jax.ShapeDtypeStruct((count, chunk, model), BF16),
        compiler_params=params(),
        cost_estimate=pl.CostEstimate(flops=10000000, bytes_accessed=5000000, transcendentals=0),
        name="finish",
    )(place, tokens, cotangent, gain, parts)


def to_peer(array, shift):
    dz, dy = shift
    pairs = [
        (z * 2 + y, ((z + dz) % 4) * 2 + (y + dy) % 2) for z in range(4) for y in range(2)
    ]
    return lax.ppermute(array, "chan", pairs)


def to_all(array):
    return lax.all_to_all(array, "chan", 0, 0, tiled=True)


def over_z(array):
    groups = [[0, 2, 4, 6], [1, 3, 5, 7]]
    return lax.all_gather(array, "chan", axis_index_groups=groups, tiled=True)


def shards(tokens, cotangent, norm_gain, norm_bias, qkv_weight, out_weight, lengths, segments):
    recs, frames, model = tokens.shape
    rows = recs * frames
    width = out_weight.shape[0]
    me = lax.axis_index("chan")
    start = lax.axis_index("frames") * frames
    scalar = lambda value: value.reshape(1).astype(jnp.int32)

    weight = qkv_weight.transpose(1, 2, 0).reshape(3 * width, model)
    near_out = over_z(out_weight)
    peer_out = to_peer(out_weight, (0, 1))

    flat_tokens = tokens.reshape(rows, model)
    flat_cot = cotangent.reshape(rows, model)
    reach = start - CTX + jnp.arange(frames + 2 * CTX, dtype=jnp.int32)
    padded = jnp.pad(segments, ((0, 0), (CTX, CTX)), constant_values=-10)
    seg_keys = lax.dynamic_slice_in_dim(padded, start, frames + 2 * CTX, 1)
    seg_keys = jnp.where(reach[None, :] < lengths[:, None], seg_keys, -10)[:, :, None]
    seg_rows = lax.dynamic_slice_in_dim(segments, start, frames, 1)[:, None, :]

    normed, q, kv, g, kv_first, kv_last, live = project(
        lengths, flat_tokens, flat_cot, norm_gain, norm_bias, weight, out_weight
    )
    size = lax.axis_size("frames")
    up = [(i, i + 1) for i in range(size - 1)]
    down = [(i + 1, i) for i in range(size - 1)]
    tie = lax.optimization_barrier
    kv_first, kv_last, peer_out = tie((kv_first, kv_last, peer_out))
    far_out = over_z(peer_out)
    before = lax.ppermute(kv_last, "frames", up)
    after = lax.ppermute(kv_first, "frames", down)
    mixed, dq, dkv, dbefore, dafter = attention(
        q, kv, before, after, g, seg_keys, seg_rows, live
    )
    from_right = lax.ppermute(dbefore, "frames", down)
    from_left = lax.ppermute(dafter, "frames", up)
    near_mixed = over_z(mixed)
    peer_mixed = to_peer(mixed, (0, 1))
    from_left, from_right, peer_mixed, near_out, far_out = tie(
        (from_left, from_right, peer_mixed, near_out, far_out)
    )
    far_mixed = over_z(peer_mixed)

    back = back_rows(dq, dkv, from_left, from_right, weight)
    parts = to_all(back.reshape(lax.axis_size("chan"), -1, model))

    core = scalar(lax.axis_index("batch") & 1)
    sent, kept = weight_grads(core, normed, flat_cot, dq, dkv, from_left, from_right, mixed)
    pair = lax.ppermute(sent, "batch", [(0, 1), (1, 0), (2, 3), (3, 2)])
    pair = (kept + pair.astype(F32)).astype(BF16)
    pair, near_mixed, parts = tie((pair, near_mixed, parts))
    sums = lax.psum_scatter(pair, "frames", scatter_dimension=0)
    sums = lax.psum_scatter(
        sums, "batch", scatter_dimension=0, axis_index_groups=[[0, 2], [1, 3]]
    )
    grad_proj = sums.astype(F32).reshape(-1, 4, width)

    pieces = finish(scalar(me), flat_tokens, flat_cot, norm_gain, parts)
    grad_tokens = to_all(pieces)
    output = output_rows(flat_tokens, near_mixed, far_mixed, near_out, far_out)
    shape = (recs, frames, model)
    return (output.reshape(shape), grad_tokens.reshape(shape), grad_proj)


def solution(mesh):
    return jax.shard_map(
        shards,
        mesh=mesh,
        in_specs=(
            P("batch", "frames", None),
            P("batch", "frames", None),
            P(),
            P(),
            P(None, None, "chan"),
            P("chan", None),
            P("batch"),
            P("batch", None),
        ),
        out_specs=(
            P("batch", "frames", None),
            P("batch", "frames", None),
            P(("batch", "frames"), None, "chan"),
        ),
        check_vma=False,
    )
```

```python
import jax
import jax.numpy as jnp
from jax import lax
from jax.experimental import pallas as pl
from jax.experimental.pallas import tpu as pltpu
from jax.sharding import PartitionSpec as P

HEAD = 64
CTX = 256
EPS = 1e-05
NEG = -1e30
VMEM_LIMIT = 60 * 1024 * 1024

F32 = jnp.float32
BF16 = jnp.bfloat16


def params():
    return pltpu.CompilerParams(vmem_limit_bytes=VMEM_LIMIT)


def dot_nn(a, b):
    return lax.dot_general(a, b, (((1,), (0,)), ((), ())), preferred_element_type=F32)


def dot_nt(a, b):
    return lax.dot_general(a, b, (((1,), (1,)), ((), ())), preferred_element_type=F32)


def dot_tn(a, b):
    return lax.dot_general(a, b, (((0,), (0,)), ((), ())), preferred_element_type=F32)


def norm_stats(tokens):
    values = tokens.astype(F32)
    centered = values - jnp.mean(values, axis=-1, keepdims=True)
    inverse = lax.rsqrt(jnp.mean(centered * centered, axis=-1, keepdims=True) + EPS)
    return centered * inverse, inverse


def project_body(
    lengths, tok, cot, gain, bias, weight, out_w, normed, q, kv, g, kv_first, kv_last, live
):
    width = q.shape[0]
    scaled, _ = norm_stats(tok[...])
    rows = (scaled * gain[...][None, :] + bias[...][None, :]).astype(BF16)
    normed[...] = rows
    qkv = dot_nt(weight[...], rows).astype(BF16)
    q[...] = qkv[:width]
    kv[...] = qkv[width:]
    step = pl.program_id(0)

    @pl.when(step % 2 == 0)
    def _():
        kv_first[...] = qkv[width:]

    @pl.when(step % 2 == 1)
    def _():
        kv_last[...] = qkv[width:]

    start = lax.axis_index("frames") * (2 * CTX) + (step % 2) * CTX
    position = start + lax.broadcasted_iota(jnp.int32, (1, CTX), 1)
    alive = jnp.where(position < lengths[step // 2], 1.0, 0.0)
    live[...] = alive
    g[...] = (dot_nt(out_w[...], cot[...]) * alive).astype(BF16)


def project(lengths, tokens, cotangent, gain, bias, weight, out_w):
    rows, model = tokens.shape
    width = out_w.shape[0]
    full = lambda shape: pl.BlockSpec(shape, lambda i: (0,) * len(shape))
    by_row = pl.BlockSpec((CTX, model), lambda i: (i, 0))
    by_col = lambda n: pl.BlockSpec((n, CTX), lambda i: (0, i))
    by_half = pl.BlockSpec((2 * width, CTX), lambda i: (0, i // 2))
    return pl.pallas_call(
        project_body,
        grid=(rows // CTX,),
        in_specs=[
            pl.BlockSpec(memory_space=pltpu.SMEM),
            by_row,
            by_row,
            full((model,)),
            full((model,)),
            full((3 * width, model)),
            full((width, model)),
        ],
        out_specs=[
            by_row,
            by_col(width),
            by_col(2 * width),
            by_col(width),
            by_half,
            by_half,
            by_col(1),
        ],
        out_shape=[
            jax.ShapeDtypeStruct((rows, model), BF16),
            jax.ShapeDtypeStruct((width, rows), BF16),
            jax.ShapeDtypeStruct((2 * width, rows), BF16),
            jax.ShapeDtypeStruct((width, rows), BF16),
            jax.ShapeDtypeStruct((2 * width, rows // 2), BF16),
            jax.ShapeDtypeStruct((2 * width, rows // 2), BF16),
            jax.ShapeDtypeStruct((1, rows), F32),
        ],
        compiler_params=params(),
        cost_estimate=pl.CostEstimate(flops=2400000000, bytes_accessed=15000000, transcendentals=0),
        name="project",
    )(lengths, tokens, cotangent, gain, bias, weight, out_w)


def attention_body(
    q, kv, before, after, g, seg_keys, seg_rows, live, mixed, dq, dkv, dbefore, dafter, acc, mask
):
    width = q.shape[0]
    span = 3 * CTX
    kv_all = jnp.concatenate([before[...], kv[...], after[...]], axis=1)
    q_small = q[...] * jnp.asarray(HEAD**-0.5, BF16)
    grads = g[...]
    acc[...] = jnp.zeros_like(acc)
    for tile in range(2):
        cols = slice(tile * CTX, (tile + 1) * CTX)
        keys = slice(tile * CTX, tile * CTX + span)
        away = (
            lax.broadcasted_iota(jnp.int32, (span, CTX), 0)
            - CTX
            - lax.broadcasted_iota(jnp.int32, (span, CTX), 1)
        )
        near = jnp.abs(away) <= CTX
        stretch = jnp.abs(seg_keys[0, keys, :] - seg_rows[0, :, cols]) <= 1
        visible = (near & stretch) | (away == 0)
        mask[...] = jnp.where(visible, 0.0, NEG)
        for head in range(width // HEAD):
            d = slice(head * HEAD, (head + 1) * HEAD)
            dv = slice(width + head * HEAD, width + (head + 1) * HEAD)
            k_t, v_t = kv_all[d, keys], kv_all[dv, keys]
            q_t, g_t = q_small[d, cols], grads[d, cols]
            scores = dot_tn(k_t, q_t) + mask[...]
            weights = jnp.exp(scores - jnp.max(scores, axis=0, keepdims=True))
            weights = weights * (1.0 / jnp.sum(weights, axis=0, keepdims=True))
            rounded = weights.astype(BF16)
            mixed[d, cols] = (dot_nn(v_t, rounded) * live[:, cols]).astype(BF16)
            grad_w = dot_tn(v_t, g_t)
            total = jnp.sum(weights * grad_w, axis=0, keepdims=True)
            grad_s = (weights * (grad_w - total)).astype(BF16)
            dq[d, cols] = (dot_nn(k_t, grad_s) * (HEAD**-0.5)).astype(BF16)
            acc[d, keys] += dot_nt(q_t, grad_s)
            acc[dv, keys] += dot_nt(g_t, rounded)
    frames = q.shape[1]
    dkv[...] = acc[:, CTX : CTX + frames]
    dbefore[...] = acc[:, :CTX].astype(BF16)
    dafter[...] = acc[:, CTX + frames :].astype(BF16)


def attention(rec, q, kv, before, after, g, seg_keys, seg_rows, live):
    width, rows = q.shape
    recs, span, _ = seg_keys.shape
    frames = rows // recs
    by_rec = lambda n, m: pl.BlockSpec((n, m), lambda i: (0, rec))
    whole = lambda n, m: pl.BlockSpec((n, m), lambda i: (0, 0))
    return pl.pallas_call(
        attention_body,
        grid=(1,),
        in_specs=[
            by_rec(width, frames),
            by_rec(2 * width, frames),
            by_rec(2 * width, CTX),
            by_rec(2 * width, CTX),
            by_rec(width, frames),
            pl.BlockSpec((1, span, 1), lambda i: (rec, 0, 0)),
            pl.BlockSpec((1, 1, frames), lambda i: (rec, 0, 0)),
            by_rec(1, frames),
        ],
        out_specs=[
            whole(width, frames),
            whole(width, frames),
            whole(2 * width, frames),
            whole(2 * width, CTX),
            whole(2 * width, CTX),
        ],
        out_shape=[
            jax.ShapeDtypeStruct((width, frames), BF16),
            jax.ShapeDtypeStruct((width, frames), BF16),
            jax.ShapeDtypeStruct((2 * width, frames), F32),
            jax.ShapeDtypeStruct((2 * width, CTX), BF16),
            jax.ShapeDtypeStruct((2 * width, CTX), BF16),
        ],
        scratch_shapes=[pltpu.VMEM((2 * width, span), F32), pltpu.VMEM((3 * CTX, CTX), F32)],
        compiler_params=params(),
        cost_estimate=pl.CostEstimate(flops=1000, bytes_accessed=1000, transcendentals=0),
        name="attention",
    )(q, kv, before, after, g, seg_keys, seg_rows, live)


def kv_grads(own, left, right):
    beside = jnp.concatenate([left[...], right[...]], axis=1).astype(F32)
    return (own[...] + beside).astype(BF16)


def back_body(dq, own, left, right, weight, out, flipped):
    width = dq.shape[0]

    @pl.when(pl.program_id(0) == 0)
    def _():
        flipped[:, :width] = dq[...].T
        flipped[:, width:] = kv_grads(own, left, right).T

    out[...] = dot_nn(flipped[...], weight[...]).astype(BF16)


def back_rows(dq, own, left, right, weight):
    width, rows = dq.shape
    model = weight.shape[1]
    tile = 512
    full = lambda n, m: pl.BlockSpec((n, m), lambda i: (0, 0))
    by_col = lambda n: pl.BlockSpec((n, tile), lambda i: (0, i))
    return pl.pallas_call(
        back_body,
        grid=(model // tile,),
        in_specs=[
            full(width, rows),
            full(2 * width, rows),
            full(2 * width, rows // 2),
            full(2 * width, rows // 2),
            by_col(3 * width),
        ],
        out_specs=by_col(rows),
        out_shape=jax.ShapeDtypeStruct((rows, model), BF16),
        scratch_shapes=[pltpu.VMEM((rows, 3 * width), BF16)],
        compiler_params=params(),
        cost_estimate=pl.CostEstimate(flops=900000000, bytes_accessed=4000000, transcendentals=0),
        name="back",
    )(dq, own, left, right, weight)


def weight_grads_body(core, normed, cot, *rest):
    pieces, (sent, kept, kv, query, mixed) = rest[:-5], rest[-5:]
    width, frames = pieces[0].shape
    del core

    @pl.when(pl.program_id(0) == 0)
    def _():
        for rec in range(2):
            dq, own, left, right, out = pieces[5 * rec : 5 * rec + 5]
            cols = slice(rec * frames, (rec + 1) * frames)
            kv[:, cols] = kv_grads(own, left, right)
            query[:, cols] = dq[...]
            mixed[:, cols] = out[...]

    turned = normed[...].T
    sums = [
        dot_nt(turned, query[...]),
        dot_nt(turned, kv[...]),
        dot_nt(cot[...].T, mixed[...]),
    ]
    offsets = (0, width, 3 * width)

    def write(target):
        for part, offset in zip(sums, offsets):
            shape = (target.shape[0], target.shape[2], part.shape[1])
            cols = slice(offset, offset + part.shape[1])
            target[:, 0, :, cols] = part.reshape(shape).astype(target.dtype)

    @pl.when(pl.program_id(0) < 2)
    def _():
        write(sent)

    @pl.when(pl.program_id(0) >= 2)
    def _():
        write(kept)


def weight_grads(core, normed, cotangent, pieces):
    rows, model = normed.shape
    width = pieces[0].shape[0]
    block = model // 4

    def by_step(i, c):
        return (0, (i % 2) * 2 + jnp.where(i < 2, 1 - c[0], c[0]))

    part = (4, 1, block // 4, 4 * width)
    return pl.pallas_call(
        weight_grads_body,
        grid_spec=pltpu.PrefetchScalarGridSpec(
            num_scalar_prefetch=1,
            grid=(4,),
            in_specs=[pl.BlockSpec((rows, block), by_step)] * 2
            + [pl.BlockSpec(piece.shape, lambda i, c: (0, 0)) for piece in pieces],
            out_specs=[
                pl.BlockSpec(part, lambda i, c: (0, jnp.minimum(i, 1), 0, 0)),
                pl.BlockSpec(part, lambda i, c: (0, jnp.maximum(i, 2) - 2, 0, 0)),
            ],
            scratch_shapes=[
                pltpu.VMEM((2 * width, rows), BF16),
                pltpu.VMEM((width, rows), BF16),
                pltpu.VMEM((width, rows), BF16),
            ],
        ),
        out_shape=[
            jax.ShapeDtypeStruct((4, 2, block // 4, 4 * width), BF16),
            jax.ShapeDtypeStruct((4, 2, block // 4, 4 * width), F32),
        ],
        compiler_params=params(),
        cost_estimate=pl.CostEstimate(flops=1000, bytes_accessed=1000, transcendentals=0),
        name="weight_grads",
    )(core, normed, cotangent, *pieces)


def output_body(tok, near, far, weight, out, stacked):
    side = lax.axis_index("chan") & 1
    width = weight.shape[0] // 8
    for z in range(4):
        rows = slice(z * width, (z + 1) * width)
        for offset, source in ((side, near), (1 - side, far)):
            place = pl.multiple_of((2 * z + offset) * width, width)
            stacked[pl.ds(place, width), :] = source[rows, :]
    total = dot_nn(stacked[...].T, weight[...])
    out[...] = (tok[...].astype(F32) + total).astype(BF16)


def output_rows(tokens, near, far, weight):
    rows, model = tokens.shape
    depth = near.shape[0]
    by_row = pl.BlockSpec((CTX, model), lambda i: (i, 0))
    by_col = pl.BlockSpec((depth, CTX), lambda i: (0, i))
    return pl.pallas_call(
        output_body,
        grid=(rows // CTX,),
        in_specs=[by_row, by_col, by_col, pl.BlockSpec((2 * depth, model), lambda i: (0, 0))],
        out_specs=by_row,
        out_shape=jax.ShapeDtypeStruct((rows, model), BF16),
        scratch_shapes=[pltpu.VMEM((2 * depth, CTX), BF16)],
        compiler_params=params(),
        cost_estimate=pl.CostEstimate(flops=1000, bytes_accessed=1000, transcendentals=0),
        name="output",
    )(tokens, near, far, weight)


def finish_body(place, tok, cot, gain, parts, out):
    back = jnp.sum(parts[...].astype(F32), axis=0)
    scaled, inverse = norm_stats(tok[...])
    weighted = back * gain[...][None, :]
    first = jnp.mean(weighted, axis=-1, keepdims=True)
    second = jnp.mean(weighted * scaled, axis=-1, keepdims=True)
    grad = inverse * (weighted - first - scaled * second) + cot[...].astype(F32)
    out[...] = jnp.broadcast_to(grad.astype(BF16)[None], out.shape)


def finish(place, tokens, cotangent, gain, parts):
    count, chunk, model = parts.shape
    here = pl.BlockSpec((chunk, model), lambda i, p: (p[0], 0))
    whole = pl.BlockSpec((count, chunk, model), lambda i, p: (0, 0, 0))
    return pl.pallas_call(
        finish_body,
        grid_spec=pltpu.PrefetchScalarGridSpec(
            num_scalar_prefetch=1,
            grid=(1,),
            in_specs=[here, here, pl.BlockSpec((model,), lambda i, p: (0,)), whole],
            out_specs=whole,
        ),
        out_shape=jax.ShapeDtypeStruct((count, chunk, model), BF16),
        compiler_params=params(),
        cost_estimate=pl.CostEstimate(flops=10000000, bytes_accessed=5000000, transcendentals=0),
        name="finish",
    )(place, tokens, cotangent, gain, parts)


def to_peer(array, shift):
    dz, dy = shift
    pairs = [
        (z * 2 + y, ((z + dz) % 4) * 2 + (y + dy) % 2) for z in range(4) for y in range(2)
    ]
    return lax.ppermute(array, "chan", pairs)


def to_all(array):
    return lax.all_to_all(array, "chan", 0, 0, tiled=True)


def pick(array, index, axis):
    return lax.dynamic_index_in_dim(array, index, axis, keepdims=False)


def frame_sums(sent, kept):
    frame = lax.axis_index("frames")
    got = lax.ppermute(sent, "batch", [(0, 1), (1, 0), (2, 3), (3, 2)])
    pair = kept + got.astype(F32)
    sums = pick(pair, frame, 0)
    for shift in (1, 3, 2):
        sent = pick(pair, (frame + shift) & 3, 0).astype(BF16)
        got = lax.ppermute(sent, "frames", [(i, (i + shift) % 4) for i in range(4)])
        sums = sums + got.astype(F32)
    return sums


def row_sums(sums):
    row = lax.axis_index("batch") >> 1
    sent = pick(sums, 1 - row, 0).astype(BF16)
    got = lax.ppermute(sent, "batch", [(0, 2), (1, 3), (2, 0), (3, 1)])
    return pick(sums, row, 0) + got.astype(F32)


def over_z(array):
    groups = [[0, 2, 4, 6], [1, 3, 5, 7]]
    return lax.all_gather(array, "chan", axis_index_groups=groups, tiled=True)


def shards(tokens, cotangent, norm_gain, norm_bias, qkv_weight, out_weight, lengths, segments):
    recs, frames, model = tokens.shape
    rows = recs * frames
    width = out_weight.shape[0]
    me = lax.axis_index("chan")
    start = lax.axis_index("frames") * frames
    scalar = lambda value: value.reshape(1).astype(jnp.int32)

    weight = qkv_weight.transpose(1, 2, 0).reshape(3 * width, model)
    tie = lax.optimization_barrier
    full_out = lax.all_gather(out_weight, "chan", tiled=True)

    flat_tokens = tokens.reshape(rows, model)
    flat_cot = cotangent.reshape(rows, model)
    reach = start - CTX + jnp.arange(frames + 2 * CTX, dtype=jnp.int32)
    padded = jnp.pad(segments, ((0, 0), (CTX, CTX)), constant_values=-10)
    seg_keys = lax.dynamic_slice_in_dim(padded, start, frames + 2 * CTX, 1)
    seg_keys = jnp.where(reach[None, :] < lengths[:, None], seg_keys, -10)[:, :, None]
    seg_rows = lax.dynamic_slice_in_dim(segments, start, frames, 1)[:, None, :]

    normed, q, kv, g, kv_first, kv_last, live = project(
        lengths, flat_tokens, flat_cot, norm_gain, norm_bias, weight, out_weight
    )
    size = lax.axis_size("frames")
    up = [(i, i + 1) for i in range(size - 1)]
    down = [(i + 1, i) for i in range(size - 1)]
    before = lax.ppermute(kv_last, "frames", up)
    after = lax.ppermute(kv_first, "frames", down)

    results = []
    for rec in range(recs):
        mixed, dq, dkv, dbefore, dafter = attention(
            rec, q, kv, before, after, g, seg_keys, seg_rows, live
        )
        right = lax.ppermute(dbefore, "frames", down)
        left = lax.ppermute(dafter, "frames", up)
        results.append([dq, dkv, left, right, mixed])

    mixed = jnp.concatenate([result[4] for result in results], axis=1)
    near_mixed = over_z(mixed)
    peer_mixed = to_peer(mixed, (0, 1))
    first = results[0]
    first[0], peer_mixed, _ = tie((first[0], peer_mixed, results[1][0]))
    far_mixed = over_z(peer_mixed)

    count = lax.axis_size("chan")
    backs = [
        back_rows(*result[:4], weight).reshape(count, -1, model) for result in results
    ]
    parts = [to_all(back) for back in backs]
    parts[0], full_out = tie((parts[0], full_out))
    results[1][0], _ = tie((results[1][0], backs[0]))

    core = scalar(lax.axis_index("batch") & 1)
    sent, kept = weight_grads(core, normed, flat_cot, results[0] + results[1])
    sums = frame_sums(sent, kept)
    sums, parts[1] = tie((sums, parts[1]))
    grad_proj = row_sums(sums).reshape(-1, 4, width)

    grad_tokens = []
    for rec in range(recs):
        pieces = finish(
            scalar(rec * count + me), flat_tokens, flat_cot, norm_gain, parts[rec]
        )
        grad_tokens.append(to_all(pieces).reshape(frames, model))
    grad_tokens = jnp.stack(grad_tokens)
    output = output_rows(flat_tokens, near_mixed, far_mixed, full_out)
    shape = (recs, frames, model)
    return (output.reshape(shape), grad_tokens.reshape(shape), grad_proj)


def solution(mesh):
    return jax.shard_map(
        shards,
        mesh=mesh,
        in_specs=(
            P("batch", "frames", None),
            P("batch", "frames", None),
            P(),
            P(),
            P(None, None, "chan"),
            P("chan", None),
            P("batch"),
            P("batch", None),
        ),
        out_specs=(
            P("batch", "frames", None),
            P("batch", "frames", None),
            P(("batch", "frames"), None, "chan"),
        ),
        check_vma=False,
    )
```

```python
import jax
import jax.numpy as jnp
from jax import lax
from jax.experimental import pallas as pl
from jax.experimental.pallas import tpu as pltpu
from jax.sharding import PartitionSpec as P

HEAD = 64
CTX = 256
EPS = 1e-05
NEG = -1e30
VMEM_LIMIT = 60 * 1024 * 1024

SHIFTS = ((1, 0), (3, 0), (0, 1), (1, 1), (3, 1), (2, 0), (2, 1))

F32 = jnp.float32
BF16 = jnp.bfloat16


def params():
    return pltpu.CompilerParams(vmem_limit_bytes=VMEM_LIMIT)


def dot_nn(a, b):
    return lax.dot_general(a, b, (((1,), (0,)), ((), ())), preferred_element_type=F32)


def dot_nt(a, b):
    return lax.dot_general(a, b, (((1,), (1,)), ((), ())), preferred_element_type=F32)


def dot_tn(a, b):
    return lax.dot_general(a, b, (((0,), (0,)), ((), ())), preferred_element_type=F32)


def norm_stats(tokens):
    values = tokens.astype(F32)
    centered = values - jnp.mean(values, axis=-1, keepdims=True)
    inverse = lax.rsqrt(jnp.mean(centered * centered, axis=-1, keepdims=True) + EPS)
    return centered * inverse, inverse


def project_body(
    lengths, tok, cot, gain, bias, weight, out_w, normed, q, kv, g, kv_first, kv_last, live
):
    width = q.shape[0]
    scaled, _ = norm_stats(tok[...])
    rows = (scaled * gain[...][None, :] + bias[...][None, :]).astype(BF16)
    normed[...] = rows
    qkv = dot_nt(weight[...], rows).astype(BF16)
    q[...] = qkv[:width]
    kv[...] = qkv[width:]
    step = pl.program_id(0)

    @pl.when(step % 2 == 0)
    def _():
        kv_first[...] = qkv[width:]

    @pl.when(step % 2 == 1)
    def _():
        kv_last[...] = qkv[width:]

    start = lax.axis_index("frames") * (2 * CTX) + (step % 2) * CTX
    position = start + lax.broadcasted_iota(jnp.int32, (1, CTX), 1)
    alive = jnp.where(position < lengths[step // 2], 1.0, 0.0)
    live[...] = alive
    g[...] = (dot_nt(out_w[...], cot[...]) * alive).astype(BF16)


def project(lengths, tokens, cotangent, gain, bias, weight, out_w):
    rows, model = tokens.shape
    width = out_w.shape[0]
    full = lambda shape: pl.BlockSpec(shape, lambda i: (0,) * len(shape))
    by_row = pl.BlockSpec((CTX, model), lambda i: (i, 0))
    by_col = lambda n: pl.BlockSpec((n, CTX), lambda i: (0, i))
    by_half = pl.BlockSpec((2 * width, CTX), lambda i: (0, i // 2))
    return pl.pallas_call(
        project_body,
        grid=(rows // CTX,),
        in_specs=[
            pl.BlockSpec(memory_space=pltpu.SMEM),
            by_row,
            by_row,
            full((model,)),
            full((model,)),
            full((3 * width, model)),
            full((width, model)),
        ],
        out_specs=[
            by_row,
            by_col(width),
            by_col(2 * width),
            by_col(width),
            by_half,
            by_half,
            by_col(1),
        ],
        out_shape=[
            jax.ShapeDtypeStruct((rows, model), BF16),
            jax.ShapeDtypeStruct((width, rows), BF16),
            jax.ShapeDtypeStruct((2 * width, rows), BF16),
            jax.ShapeDtypeStruct((width, rows), BF16),
            jax.ShapeDtypeStruct((2 * width, rows // 2), BF16),
            jax.ShapeDtypeStruct((2 * width, rows // 2), BF16),
            jax.ShapeDtypeStruct((1, rows), F32),
        ],
        compiler_params=params(),
        cost_estimate=pl.CostEstimate(flops=2400000000, bytes_accessed=15000000, transcendentals=0),
        name="project",
    )(lengths, tokens, cotangent, gain, bias, weight, out_w)


def attention_body(
    q, kv, before, after, g, seg_keys, seg_rows, live, mixed, dq, dkv, dbefore, dafter, acc, mask
):
    width = q.shape[0]
    span = 3 * CTX
    kv_all = jnp.concatenate([before[...], kv[...], after[...]], axis=1)
    q_small = q[...] * jnp.asarray(HEAD**-0.5, BF16)
    grads = g[...]
    acc[...] = jnp.zeros_like(acc)
    for tile in range(2):
        cols = slice(tile * CTX, (tile + 1) * CTX)
        keys = slice(tile * CTX, tile * CTX + span)
        away = (
            lax.broadcasted_iota(jnp.int32, (span, CTX), 0)
            - CTX
            - lax.broadcasted_iota(jnp.int32, (span, CTX), 1)
        )
        near = jnp.abs(away) <= CTX
        stretch = jnp.abs(seg_keys[0, keys, :] - seg_rows[0, :, cols]) <= 1
        visible = (near & stretch) | (away == 0)
        mask[...] = jnp.where(visible, 0.0, NEG)
        for head in range(width // HEAD):
            d = slice(head * HEAD, (head + 1) * HEAD)
            dv = slice(width + head * HEAD, width + (head + 1) * HEAD)
            k_t, v_t = kv_all[d, keys], kv_all[dv, keys]
            q_t, g_t = q_small[d, cols], grads[d, cols]
            scores = dot_tn(k_t, q_t) + mask[...]
            weights = jnp.exp(scores - jnp.max(scores, axis=0, keepdims=True))
            weights = weights * (1.0 / jnp.sum(weights, axis=0, keepdims=True))
            rounded = weights.astype(BF16)
            mixed[d, cols] = (dot_nn(v_t, rounded) * live[:, cols]).astype(BF16)
            grad_w = dot_tn(v_t, g_t)
            total = jnp.sum(weights * grad_w, axis=0, keepdims=True)
            grad_s = (weights * (grad_w - total)).astype(BF16)
            dq[d, cols] = (dot_nn(k_t, grad_s) * (HEAD**-0.5)).astype(BF16)
            acc[d, keys] += dot_nt(q_t, grad_s)
            acc[dv, keys] += dot_nt(g_t, rounded)
    frames = q.shape[1]
    dkv[...] = acc[:, CTX : CTX + frames]
    dbefore[...] = acc[:, :CTX].astype(BF16)
    dafter[...] = acc[:, CTX + frames :].astype(BF16)


def attention(rec, q, kv, before, after, g, seg_keys, seg_rows, live):
    width, rows = q.shape
    recs, span, _ = seg_keys.shape
    frames = rows // recs
    by_rec = lambda n, m: pl.BlockSpec((n, m), lambda i: (0, rec))
    whole = lambda n, m: pl.BlockSpec((n, m), lambda i: (0, 0))
    return pl.pallas_call(
        attention_body,
        grid=(1,),
        in_specs=[
            by_rec(width, frames),
            by_rec(2 * width, frames),
            by_rec(2 * width, CTX),
            by_rec(2 * width, CTX),
            by_rec(width, frames),
            pl.BlockSpec((1, span, 1), lambda i: (rec, 0, 0)),
            pl.BlockSpec((1, 1, frames), lambda i: (rec, 0, 0)),
            by_rec(1, frames),
        ],
        out_specs=[
            whole(width, frames),
            whole(width, frames),
            whole(2 * width, frames),
            whole(2 * width, CTX),
            whole(2 * width, CTX),
        ],
        out_shape=[
            jax.ShapeDtypeStruct((width, frames), BF16),
            jax.ShapeDtypeStruct((width, frames), BF16),
            jax.ShapeDtypeStruct((2 * width, frames), F32),
            jax.ShapeDtypeStruct((2 * width, CTX), BF16),
            jax.ShapeDtypeStruct((2 * width, CTX), BF16),
        ],
        scratch_shapes=[pltpu.VMEM((2 * width, span), F32), pltpu.VMEM((3 * CTX, CTX), F32)],
        compiler_params=params(),
        cost_estimate=pl.CostEstimate(flops=1000, bytes_accessed=1000, transcendentals=0),
        name="attention",
    )(q, kv, before, after, g, seg_keys, seg_rows, live)


def kv_grads(own, left, right):
    beside = jnp.concatenate([left[...], right[...]], axis=1).astype(F32)
    return (own[...] + beside).astype(BF16)


def back_body(dq, own, left, right, weight, out, flipped):
    width = dq.shape[0]

    @pl.when(pl.program_id(0) == 0)
    def _():
        flipped[:, :width] = dq[...].T
        flipped[:, width:] = kv_grads(own, left, right).T

    out[...] = dot_nn(flipped[...], weight[...]).astype(BF16)


def back_rows(dq, own, left, right, weight):
    width, rows = dq.shape
    model = weight.shape[1]
    tile = 512
    full = lambda n, m: pl.BlockSpec((n, m), lambda i: (0, 0))
    by_col = lambda n: pl.BlockSpec((n, tile), lambda i: (0, i))
    return pl.pallas_call(
        back_body,
        grid=(model // tile,),
        in_specs=[
            full(width, rows),
            full(2 * width, rows),
            full(2 * width, rows // 2),
            full(2 * width, rows // 2),
            by_col(3 * width),
        ],
        out_specs=by_col(rows),
        out_shape=jax.ShapeDtypeStruct((rows, model), BF16),
        scratch_shapes=[pltpu.VMEM((rows, 3 * width), BF16)],
        compiler_params=params(),
        cost_estimate=pl.CostEstimate(flops=900000000, bytes_accessed=4000000, transcendentals=0),
        name="back",
    )(dq, own, left, right, weight)


def weight_grads_body(core, normed, cot, *rest):
    pieces, (sent, kept, kv, query, mixed) = rest[:-5], rest[-5:]
    width, frames = pieces[0].shape
    del core

    @pl.when(pl.program_id(0) == 0)
    def _():
        for rec in range(2):
            dq, own, left, right, out = pieces[5 * rec : 5 * rec + 5]
            cols = slice(rec * frames, (rec + 1) * frames)
            kv[:, cols] = kv_grads(own, left, right)
            query[:, cols] = dq[...]
            mixed[:, cols] = out[...]

    turned = normed[...].T
    sums = [
        dot_nt(turned, query[...]),
        dot_nt(turned, kv[...]),
        dot_nt(cot[...].T, mixed[...]),
    ]
    offsets = (0, width, 3 * width)

    def write(target):
        for part, offset in zip(sums, offsets):
            shape = (target.shape[0], target.shape[2], part.shape[1])
            cols = slice(offset, offset + part.shape[1])
            target[:, 0, :, cols] = part.reshape(shape).astype(target.dtype)

    @pl.when(pl.program_id(0) < 2)
    def _():
        write(sent)

    @pl.when(pl.program_id(0) >= 2)
    def _():
        write(kept)


def weight_grads(core, normed, cotangent, pieces):
    rows, model = normed.shape
    width = pieces[0].shape[0]
    block = model // 4

    def by_step(i, c):
        return (0, (i % 2) * 2 + jnp.where(i < 2, 1 - c[0], c[0]))

    part = (4, 1, block // 4, 4 * width)
    return pl.pallas_call(
        weight_grads_body,
        grid_spec=pltpu.PrefetchScalarGridSpec(
            num_scalar_prefetch=1,
            grid=(4,),
            in_specs=[pl.BlockSpec((rows, block), by_step)] * 2
            + [pl.BlockSpec(piece.shape, lambda i, c: (0, 0)) for piece in pieces],
            out_specs=[
                pl.BlockSpec(part, lambda i, c: (0, jnp.minimum(i, 1), 0, 0)),
                pl.BlockSpec(part, lambda i, c: (0, jnp.maximum(i, 2) - 2, 0, 0)),
            ],
            scratch_shapes=[
                pltpu.VMEM((2 * width, rows), BF16),
                pltpu.VMEM((width, rows), BF16),
                pltpu.VMEM((width, rows), BF16),
            ],
        ),
        out_shape=[
            jax.ShapeDtypeStruct((4, 2, block // 4, 4 * width), BF16),
            jax.ShapeDtypeStruct((4, 2, block // 4, 4 * width), F32),
        ],
        compiler_params=params(),
        cost_estimate=pl.CostEstimate(flops=10000000000, bytes_accessed=12000000, transcendentals=0),
        name="weight_grads",
    )(core, normed, cotangent, *pieces)


def output_body(tok, first, second, own_weight, other_weight, out, own, other):
    core = lax.axis_index("batch") & 1
    half = own_weight.shape[0] // 8
    rec = pl.program_id(0) // 2

    def fill(source):
        for chan in range(8):
            rows = slice(chan * half, (chan + 1) * half)
            for offset, target in ((core, own), (1 - core, other)):
                place = pl.multiple_of((2 * chan + offset) * half, half)
                target[rows, :] = source[pl.ds(place, half), :]

    pl.when(rec == 0)(lambda: fill(first))
    pl.when(rec == 1)(lambda: fill(second))
    total = dot_nn(own[...].T, own_weight[...]) + dot_nn(other[...].T, other_weight[...])
    out[...] = (tok[...].astype(F32) + total).astype(BF16)


def output_rows(tokens, mixed, own_weight, other_weight):
    rows, model = tokens.shape
    depth = own_weight.shape[0]
    by_row = pl.BlockSpec((CTX, model), lambda i: (i, 0))
    by_col = pl.BlockSpec((2 * depth, CTX), lambda i: (0, i % 2))
    full = pl.BlockSpec((depth, model), lambda i: (0, 0))
    return pl.pallas_call(
        output_body,
        grid=(rows // CTX,),
        in_specs=[by_row, by_col, by_col, full, full],
        out_specs=by_row,
        out_shape=jax.ShapeDtypeStruct((rows, model), BF16),
        scratch_shapes=[pltpu.VMEM((depth, CTX), BF16)] * 2,
        compiler_params=params(),
        cost_estimate=pl.CostEstimate(flops=10000000000, bytes_accessed=12000000, transcendentals=0),
        name="output",
    )(tokens, *mixed, own_weight, other_weight)


def finish_body(place, gain, *refs):
    out = refs[-1]
    chunk = refs[0].shape[0]
    for rec in range(2):
        tok, cot, parts = refs[3 * rec : 3 * rec + 3]
        back = jnp.sum(parts[...].astype(F32), axis=0)
        scaled, inverse = norm_stats(tok[...])
        weighted = back * gain[...][None, :]
        first = jnp.mean(weighted, axis=-1, keepdims=True)
        second = jnp.mean(weighted * scaled, axis=-1, keepdims=True)
        grad = inverse * (weighted - first - scaled * second) + cot[...].astype(F32)
        out[rec * chunk : (rec + 1) * chunk, :] = grad.astype(BF16)


def finish(place, tokens, cotangent, gain, parts):
    count, chunk, model = parts[0].shape
    at = lambda rec: pl.BlockSpec((chunk, model), lambda i, p: (rec * count + p[0], 0))
    whole = pl.BlockSpec((count, chunk, model), lambda i, p: (0, 0, 0))
    return pl.pallas_call(
        finish_body,
        grid_spec=pltpu.PrefetchScalarGridSpec(
            num_scalar_prefetch=1,
            grid=(1,),
            in_specs=[pl.BlockSpec((model,), lambda i, p: (0,))]
            + [at(0), at(0), whole, at(1), at(1), whole],
            out_specs=pl.BlockSpec((2 * chunk, model), lambda i, p: (0, 0)),
        ),
        out_shape=jax.ShapeDtypeStruct((2 * chunk, model), BF16),
        compiler_params=params(),
        cost_estimate=pl.CostEstimate(flops=10000000, bytes_accessed=5000000, transcendentals=0),
        name="finish",
    )(place, gain, tokens, cotangent, parts[0], tokens, cotangent, parts[1])


def assemble_body(places, *refs):
    pieces, out = refs[:-1], refs[-1]
    chunk = pieces[0].shape[0] // 2
    half = out.shape[0] // 2
    for index, piece in enumerate(pieces):
        for rec in range(2):
            place = pl.multiple_of(rec * half + places[index] * chunk, chunk)
            out[pl.ds(place, chunk), :] = piece[rec * chunk : (rec + 1) * chunk, :]


def assemble(places, pieces):
    chunk, model = pieces[0].shape
    count = len(pieces)
    tile = 512
    by_col = lambda n: pl.BlockSpec((n, tile), lambda i: (0, i))
    return pl.pallas_call(
        assemble_body,
        grid=(model // tile,),
        in_specs=[pl.BlockSpec(memory_space=pltpu.SMEM)] + [by_col(chunk)] * count,
        out_specs=by_col(count * chunk),
        out_shape=jax.ShapeDtypeStruct((count * chunk, model), BF16),
        compiler_params=params(),
        cost_estimate=pl.CostEstimate(flops=0, bytes_accessed=6000000, transcendentals=0),
        name="assemble",
    )(places, *pieces)


def to_peer(array, shift):
    dz, dy = shift
    pairs = [
        (z * 2 + y, ((z + dz) % 4) * 2 + (y + dy) % 2) for z in range(4) for y in range(2)
    ]
    return lax.ppermute(array, "chan", pairs)


def peer_index(me, shift, sign):
    dz, dy = shift
    return (((me >> 1) + sign * dz) & 3) * 2 + ((me & 1) ^ dy)


def to_all(array):
    return lax.all_to_all(array, "chan", 0, 0, tiled=True)


def pick(array, index, axis):
    return lax.dynamic_index_in_dim(array, index, axis, keepdims=False)


def core_swap(array):
    return lax.ppermute(array, "batch", [(0, 1), (1, 0), (2, 3), (3, 2)])


def frame_sums(pair):
    frame = lax.axis_index("frames")
    sums = pick(pair, frame, 0)
    for shift in (1, 3, 2):
        sent = pick(pair, (frame + shift) & 3, 0).astype(BF16)
        got = lax.ppermute(sent, "frames", [(i, (i + shift) % 4) for i in range(4)])
        sums = sums + got.astype(F32)
    return sums


def row_sums(sums):
    row = lax.axis_index("batch") >> 1
    sent = pick(sums, 1 - row, 0).astype(BF16)
    got = lax.ppermute(sent, "batch", [(0, 2), (1, 3), (2, 0), (3, 1)])
    return pick(sums, row, 0) + got.astype(F32)


def shards(tokens, cotangent, norm_gain, norm_bias, qkv_weight, out_weight, lengths, segments):
    recs, frames, model = tokens.shape
    rows = recs * frames
    width = out_weight.shape[0]
    me = lax.axis_index("chan")
    start = lax.axis_index("frames") * frames
    scalar = lambda value: value.reshape(1).astype(jnp.int32)

    weight = qkv_weight.transpose(1, 2, 0).reshape(3 * width, model)
    tie = lax.optimization_barrier
    core = lax.axis_index("batch") & 1
    half_out = lax.dynamic_slice_in_dim(out_weight, core * (width // 2), width // 2, 0)
    own_out = lax.all_gather(half_out, "chan", tiled=True)

    flat_tokens = tokens.reshape(rows, model)
    flat_cot = cotangent.reshape(rows, model)
    reach = start - CTX + jnp.arange(frames + 2 * CTX, dtype=jnp.int32)
    padded = jnp.pad(segments, ((0, 0), (CTX, CTX)), constant_values=-10)
    seg_keys = lax.dynamic_slice_in_dim(padded, start, frames + 2 * CTX, 1)
    seg_keys = jnp.where(reach[None, :] < lengths[:, None], seg_keys, -10)[:, :, None]
    seg_rows = lax.dynamic_slice_in_dim(segments, start, frames, 1)[:, None, :]

    normed, q, kv, g, kv_first, kv_last, live = project(
        lengths, flat_tokens, flat_cot, norm_gain, norm_bias, weight, out_weight
    )
    size = lax.axis_size("frames")
    up = [(i, i + 1) for i in range(size - 1)]
    down = [(i + 1, i) for i in range(size - 1)]
    before = lax.ppermute(kv_last, "frames", up)
    after = lax.ppermute(kv_first, "frames", down)

    results = []
    for rec in range(recs):
        mixed, dq, dkv, dbefore, dafter = attention(
            rec, q, kv, before, after, g, seg_keys, seg_rows, live
        )
        right = lax.ppermute(dbefore, "frames", down)
        left = lax.ppermute(dafter, "frames", up)
        results.append([dq, dkv, left, right, mixed])

    first, second = results
    count = lax.axis_size("chan")
    mixed = [lax.all_gather(result[4], "chan", tiled=True) for result in results]
    own_out, first[0] = tie((own_out, first[0]))
    other_out = core_swap(own_out)
    second[0], _ = tie((second[0], first[0]))

    split = lambda back: back.reshape(count, -1, model)
    second_back = split(back_rows(*second[:4], weight))
    first[0], second_back = tie((first[0], second_back))
    first_back = split(back_rows(*first[:4], weight))
    parts = [to_all(first_back), to_all(second_back)]

    first[0], first_back, mixed[1], parts[1] = tie((first[0], first_back, mixed[1], parts[1]))
    sent, kept = weight_grads(scalar(core), normed, flat_cot, first + second)
    sums = frame_sums(kept + core_swap(sent).astype(F32))
    sums, parts[0], mixed[0], other_out = tie((sums, parts[0], mixed[0], other_out))
    grad_proj = row_sums(sums).reshape(-1, 4, width)

    piece = finish(scalar(me), flat_tokens, flat_cot, norm_gain, parts)
    places = jnp.stack([me] + [peer_index(me, shift, -1) for shift in SHIFTS]).astype(jnp.int32)
    output = output_rows(flat_tokens, mixed, own_out, other_out)
    pieces = [to_peer(piece, shift) for shift in SHIFTS]
    pieces[0], output = tie((pieces[0], output))
    grad_tokens = assemble(places, [piece] + pieces)
    shape = (recs, frames, model)
    return (output.reshape(shape), grad_tokens.reshape(shape), grad_proj)


def solution(mesh):
    return jax.shard_map(
        shards,
        mesh=mesh,
        in_specs=(
            P("batch", "frames", None),
            P("batch", "frames", None),
            P(),
            P(),
            P(None, None, "chan"),
            P("chan", None),
            P("batch"),
            P("batch", None),
        ),
        out_specs=(
            P("batch", "frames", None),
            P("batch", "frames", None),
            P(("batch", "frames"), None, "chan"),
        ),
        check_vma=False,
    )
```

```python
import jax
import jax.numpy as jnp
from jax import lax
from jax.experimental import pallas as pl
from jax.experimental.pallas import tpu as pltpu
from jax.sharding import PartitionSpec as P

HEAD = 64
CTX = 256
EPS = 1e-05
NEG = -1e30

SHIFTS = ((1, 0), (3, 0), (0, 1), (1, 1), (3, 1), (2, 0), (2, 1))

F32 = jnp.float32
BF16 = jnp.bfloat16


def params(mebibytes=60):
    return pltpu.CompilerParams(vmem_limit_bytes=mebibytes * 1024 * 1024)


def dot_nn(a, b):
    return lax.dot_general(a, b, (((1,), (0,)), ((), ())), preferred_element_type=F32)


def dot_nt(a, b):
    return lax.dot_general(a, b, (((1,), (1,)), ((), ())), preferred_element_type=F32)


def dot_tn(a, b):
    return lax.dot_general(a, b, (((0,), (0,)), ((), ())), preferred_element_type=F32)


def norm_stats(tokens):
    values = tokens.astype(F32)
    centered = values - jnp.mean(values, axis=-1, keepdims=True)
    inverse = lax.rsqrt(jnp.mean(centered * centered, axis=-1, keepdims=True) + EPS)
    return centered * inverse, inverse


def project_body(
    lengths, tok, cot, gain, bias, weight, out_w, normed, q, kv, g, kv_first, kv_last, live
):
    width = q.shape[0]
    scaled, _ = norm_stats(tok[...])
    rows = (scaled * gain[...][None, :] + bias[...][None, :]).astype(BF16)
    normed[...] = rows
    qkv = dot_nt(weight[...], rows).astype(BF16)
    q[...] = qkv[:width]
    kv[...] = qkv[width:]
    step = pl.program_id(0)

    @pl.when(step % 2 == 0)
    def _():
        kv_first[...] = qkv[width:]

    @pl.when(step % 2 == 1)
    def _():
        kv_last[...] = qkv[width:]

    start = lax.axis_index("frames") * (2 * CTX) + (step % 2) * CTX
    position = start + lax.broadcasted_iota(jnp.int32, (1, CTX), 1)
    alive = jnp.where(position < lengths[step // 2], 1.0, 0.0)
    live[...] = alive
    g[...] = (dot_nt(out_w[...], cot[...]) * alive).astype(BF16)


def project(lengths, tokens, cotangent, gain, bias, weight, out_w):
    rows, model = tokens.shape
    width = out_w.shape[0]
    full = lambda shape: pl.BlockSpec(shape, lambda i: (0,) * len(shape))
    by_row = pl.BlockSpec((CTX, model), lambda i: (i, 0))
    by_col = lambda n: pl.BlockSpec((n, CTX), lambda i: (0, i))
    by_half = pl.BlockSpec((2 * width, CTX), lambda i: (0, i // 2))
    return pl.pallas_call(
        project_body,
        grid=(rows // CTX,),
        in_specs=[
            pl.BlockSpec(memory_space=pltpu.SMEM),
            by_row,
            by_row,
            full((model,)),
            full((model,)),
            full((3 * width, model)),
            full((width, model)),
        ],
        out_specs=[
            by_row,
            by_col(width),
            by_col(2 * width),
            by_col(width),
            by_half,
            by_half,
            by_col(1),
        ],
        out_shape=[
            jax.ShapeDtypeStruct((rows, model), BF16),
            jax.ShapeDtypeStruct((width, rows), BF16),
            jax.ShapeDtypeStruct((2 * width, rows), BF16),
            jax.ShapeDtypeStruct((width, rows), BF16),
            jax.ShapeDtypeStruct((2 * width, rows // 2), BF16),
            jax.ShapeDtypeStruct((2 * width, rows // 2), BF16),
            jax.ShapeDtypeStruct((1, rows), F32),
        ],
        compiler_params=params(),
        cost_estimate=pl.CostEstimate(flops=2400000000, bytes_accessed=15000000, transcendentals=0),
        name="project",
    )(lengths, tokens, cotangent, gain, bias, weight, out_w)


def attention_body(
    q, kv, before, after, g, seg_keys, seg_rows, live, mixed, dq, dkv, dbefore, dafter, acc, mask
):
    width = q.shape[0]
    span = 3 * CTX
    kv_all = jnp.concatenate([before[...], kv[...], after[...]], axis=1)
    q_small = q[...] * jnp.asarray(HEAD**-0.5, BF16)
    grads = g[...]
    acc[...] = jnp.zeros_like(acc)
    for tile in range(2):
        cols = slice(tile * CTX, (tile + 1) * CTX)
        keys = slice(tile * CTX, tile * CTX + span)
        away = (
            lax.broadcasted_iota(jnp.int32, (span, CTX), 0)
            - CTX
            - lax.broadcasted_iota(jnp.int32, (span, CTX), 1)
        )
        near = jnp.abs(away) <= CTX
        stretch = jnp.abs(seg_keys[0, keys, :] - seg_rows[0, :, cols]) <= 1
        visible = (near & stretch) | (away == 0)
        mask[...] = jnp.where(visible, 0.0, NEG)
        for head in range(width // HEAD):
            d = slice(head * HEAD, (head + 1) * HEAD)
            dv = slice(width + head * HEAD, width + (head + 1) * HEAD)
            k_t, v_t = kv_all[d, keys], kv_all[dv, keys]
            q_t, g_t = q_small[d, cols], grads[d, cols]
            scores = dot_tn(k_t, q_t) + mask[...]
            weights = jnp.exp(scores - jnp.max(scores, axis=0, keepdims=True))
            weights = weights * (1.0 / jnp.sum(weights, axis=0, keepdims=True))
            rounded = weights.astype(BF16)
            out = (dot_nn(v_t, rounded) * live[:, cols]).astype(BF16)
            mixed[:, d, cols] = jnp.broadcast_to(out[None], (mixed.shape[0],) + out.shape)
            grad_w = dot_tn(v_t, g_t)
            total = jnp.sum(weights * grad_w, axis=0, keepdims=True)
            grad_s = (weights * (grad_w - total)).astype(BF16)
            dq[d, cols] = (dot_nn(k_t, grad_s) * (HEAD**-0.5)).astype(BF16)
            acc[d, keys] += dot_nt(q_t, grad_s)
            acc[dv, keys] += dot_nt(g_t, rounded)
    frames = q.shape[1]
    dkv[...] = acc[:, CTX : CTX + frames]
    dbefore[...] = acc[:, :CTX].astype(BF16)
    dafter[...] = acc[:, CTX + frames :].astype(BF16)


def attention(rec, q, kv, before, after, g, seg_keys, seg_rows, live):
    width, rows = q.shape
    recs, span, _ = seg_keys.shape
    frames = rows // recs
    by_rec = lambda n, m: pl.BlockSpec((n, m), lambda i: (0, rec))
    whole = lambda n, m: pl.BlockSpec((n, m), lambda i: (0, 0))
    return pl.pallas_call(
        attention_body,
        grid=(1,),
        in_specs=[
            by_rec(width, frames),
            by_rec(2 * width, frames),
            by_rec(2 * width, CTX),
            by_rec(2 * width, CTX),
            by_rec(width, frames),
            pl.BlockSpec((1, span, 1), lambda i: (rec, 0, 0)),
            pl.BlockSpec((1, 1, frames), lambda i: (rec, 0, 0)),
            by_rec(1, frames),
        ],
        out_specs=[
            pl.BlockSpec((8, width, frames), lambda i: (0, 0, 0)),
            whole(width, frames),
            whole(2 * width, frames),
            whole(2 * width, CTX),
            whole(2 * width, CTX),
        ],
        out_shape=[
            jax.ShapeDtypeStruct((8, width, frames), BF16),
            jax.ShapeDtypeStruct((width, frames), BF16),
            jax.ShapeDtypeStruct((2 * width, frames), F32),
            jax.ShapeDtypeStruct((2 * width, CTX), BF16),
            jax.ShapeDtypeStruct((2 * width, CTX), BF16),
        ],
        scratch_shapes=[pltpu.VMEM((2 * width, span), F32), pltpu.VMEM((3 * CTX, CTX), F32)],
        compiler_params=params(),
        cost_estimate=pl.CostEstimate(flops=1000, bytes_accessed=1000, transcendentals=0),
        name="attention",
    )(q, kv, before, after, g, seg_keys, seg_rows, live)


def kv_grads(own, left, right):
    beside = jnp.concatenate([left[...], right[...]], axis=1).astype(F32)
    return (own[...] + beside).astype(BF16)


def back_body(dq, own, left, right, weight, out, flipped):
    width = dq.shape[0]

    @pl.when(pl.program_id(0) == 0)
    def _():
        flipped[:, :width] = dq[...].T
        flipped[:, width:] = kv_grads(own, left, right).T

    out[...] = dot_nn(flipped[...], weight[...]).astype(BF16)


def back_rows(dq, own, left, right, weight):
    width, rows = dq.shape
    model = weight.shape[1]
    tile = 512
    full = lambda n, m: pl.BlockSpec((n, m), lambda i: (0, 0))
    by_col = lambda n: pl.BlockSpec((n, tile), lambda i: (0, i))
    return pl.pallas_call(
        back_body,
        grid=(model // tile,),
        in_specs=[
            full(width, rows),
            full(2 * width, rows),
            full(2 * width, rows // 2),
            full(2 * width, rows // 2),
            by_col(3 * width),
        ],
        out_specs=by_col(rows),
        out_shape=jax.ShapeDtypeStruct((rows, model), BF16),
        scratch_shapes=[pltpu.VMEM((rows, 3 * width), BF16)],
        compiler_params=params(),
        cost_estimate=pl.CostEstimate(flops=900000000, bytes_accessed=4000000, transcendentals=0),
        name="back",
    )(dq, own, left, right, weight)


def weight_grads_body(core, normed, cot, *rest):
    pieces, (sent, kept, kv, query, mixed) = rest[:-5], rest[-5:]
    width, frames = pieces[0].shape
    del core

    @pl.when(pl.program_id(0) == 0)
    def _():
        for rec in range(2):
            dq, own, left, right, out = pieces[5 * rec : 5 * rec + 5]
            cols = slice(rec * frames, (rec + 1) * frames)
            kv[:, cols] = kv_grads(own, left, right)
            query[:, cols] = dq[...]
            mixed[:, cols] = out[0]

    turned = normed[...].T
    sums = [
        dot_nt(turned, query[...]),
        dot_nt(turned, kv[...]),
        dot_nt(cot[...].T, mixed[...]),
    ]
    offsets = (0, width, 3 * width)

    def write(target):
        for part, offset in zip(sums, offsets):
            shape = (target.shape[0], target.shape[2], part.shape[1])
            cols = slice(offset, offset + part.shape[1])
            target[:, 0, :, cols] = part.reshape(shape).astype(target.dtype)

    @pl.when(pl.program_id(0) < 2)
    def _():
        write(sent)

    @pl.when(pl.program_id(0) >= 2)
    def _():
        write(kept)


def weight_grads(core, normed, cotangent, pieces):
    rows, model = normed.shape
    width = pieces[0].shape[0]
    block = model // 4

    def by_step(i, c):
        return (0, (i % 2) * 2 + jnp.where(i < 2, 1 - c[0], c[0]))

    def first_block(piece):
        if piece.ndim == 2:
            return pl.BlockSpec(piece.shape, lambda i, c: (0, 0))
        return pl.BlockSpec((1,) + piece.shape[1:], lambda i, c: (0, 0, 0))

    part = (4, 1, block // 4, 4 * width)
    return pl.pallas_call(
        weight_grads_body,
        grid_spec=pltpu.PrefetchScalarGridSpec(
            num_scalar_prefetch=1,
            grid=(4,),
            in_specs=[pl.BlockSpec((rows, block), by_step)] * 2
            + [first_block(piece) for piece in pieces],
            out_specs=[
                pl.BlockSpec(part, lambda i, c: (0, jnp.minimum(i, 1), 0, 0)),
                pl.BlockSpec(part, lambda i, c: (0, jnp.maximum(i, 2) - 2, 0, 0)),
            ],
            scratch_shapes=[
                pltpu.VMEM((2 * width, rows), BF16),
                pltpu.VMEM((width, rows), BF16),
                pltpu.VMEM((width, rows), BF16),
            ],
        ),
        out_shape=[
            jax.ShapeDtypeStruct((4, 2, block // 4, 4 * width), BF16),
            jax.ShapeDtypeStruct((4, 2, block // 4, 4 * width), F32),
        ],
        compiler_params=params(),
        cost_estimate=pl.CostEstimate(flops=10000000000, bytes_accessed=12000000, transcendentals=0),
        name="weight_grads",
    )(core, normed, cotangent, *pieces)


def output_body(tok, first, second, own_weight, other_weight, out, own, other):
    core = lax.axis_index("batch") & 1
    half = own_weight.shape[0] // 8
    rec = pl.program_id(0) // 2

    def fill(source):
        for chan in range(8):
            rows = slice(chan * half, (chan + 1) * half)
            for offset, target in ((core, own), (1 - core, other)):
                place = pl.multiple_of((2 * chan + offset) * half, half)
                target[rows, :] = source[pl.ds(place, half), :]

    pl.when(rec == 0)(lambda: fill(first))
    pl.when(rec == 1)(lambda: fill(second))
    total = dot_nn(own[...].T, own_weight[...]) + dot_nn(other[...].T, other_weight[...])
    out[...] = (tok[...].astype(F32) + total).astype(BF16)


def output_rows(tokens, mixed, own_weight, other_weight):
    rows, model = tokens.shape
    depth = own_weight.shape[0]
    by_row = pl.BlockSpec((CTX, model), lambda i: (i, 0))
    by_col = pl.BlockSpec((2 * depth, CTX), lambda i: (0, i % 2))
    full = pl.BlockSpec((depth, model), lambda i: (0, 0))
    return pl.pallas_call(
        output_body,
        grid=(rows // CTX,),
        in_specs=[by_row, by_col, by_col, full, full],
        out_specs=by_row,
        out_shape=jax.ShapeDtypeStruct((rows, model), BF16),
        scratch_shapes=[pltpu.VMEM((depth, CTX), BF16)] * 2,
        compiler_params=params(28),
        cost_estimate=pl.CostEstimate(flops=10000000000, bytes_accessed=12000000, transcendentals=0),
        name="output",
    )(tokens, *mixed, own_weight, other_weight)


def finish_body(place, gain, *refs):
    out = refs[-1]
    chunk = refs[0].shape[0]
    for rec in range(2):
        tok, cot, parts = refs[3 * rec : 3 * rec + 3]
        back = jnp.sum(parts[...].astype(F32), axis=0)
        scaled, inverse = norm_stats(tok[...])
        weighted = back * gain[...][None, :]
        first = jnp.mean(weighted, axis=-1, keepdims=True)
        second = jnp.mean(weighted * scaled, axis=-1, keepdims=True)
        grad = inverse * (weighted - first - scaled * second) + cot[...].astype(F32)
        out[rec * chunk : (rec + 1) * chunk, :] = grad.astype(BF16)


def finish(place, tokens, cotangent, gain, parts):
    count, chunk, model = parts[0].shape
    at = lambda rec: pl.BlockSpec((chunk, model), lambda i, p: (rec * count + p[0], 0))
    whole = pl.BlockSpec((count, chunk, model), lambda i, p: (0, 0, 0))
    return pl.pallas_call(
        finish_body,
        grid_spec=pltpu.PrefetchScalarGridSpec(
            num_scalar_prefetch=1,
            grid=(1,),
            in_specs=[pl.BlockSpec((model,), lambda i, p: (0,))]
            + [at(0), at(0), whole, at(1), at(1), whole],
            out_specs=pl.BlockSpec((2 * chunk, model), lambda i, p: (0, 0)),
        ),
        out_shape=jax.ShapeDtypeStruct((2 * chunk, model), BF16),
        compiler_params=params(),
        cost_estimate=pl.CostEstimate(flops=10000000, bytes_accessed=5000000, transcendentals=0),
        name="finish",
    )(place, gain, tokens, cotangent, parts[0], tokens, cotangent, parts[1])


def assemble_body(places, *refs):
    pieces, out = refs[:-1], refs[-1]
    chunk = pieces[0].shape[0] // 2
    half = out.shape[0] // 2
    for index, piece in enumerate(pieces):
        for rec in range(2):
            place = pl.multiple_of(rec * half + places[index] * chunk, chunk)
            out[pl.ds(place, chunk), :] = piece[rec * chunk : (rec + 1) * chunk, :]


def assemble(places, pieces):
    chunk, model = pieces[0].shape
    count = len(pieces)
    tile = 512
    by_col = lambda n: pl.BlockSpec((n, tile), lambda i: (0, i))
    return pl.pallas_call(
        assemble_body,
        grid=(model // tile,),
        in_specs=[pl.BlockSpec(memory_space=pltpu.SMEM)] + [by_col(chunk)] * count,
        out_specs=by_col(count * chunk),
        out_shape=jax.ShapeDtypeStruct((count * chunk, model), BF16),
        compiler_params=params(16),
        cost_estimate=pl.CostEstimate(flops=0, bytes_accessed=6000000, transcendentals=0),
        name="assemble",
    )(places, *pieces)


def to_peer(array, shift):
    dz, dy = shift
    pairs = [
        (z * 2 + y, ((z + dz) % 4) * 2 + (y + dy) % 2) for z in range(4) for y in range(2)
    ]
    return lax.ppermute(array, "chan", pairs)


def peer_index(me, shift, sign):
    dz, dy = shift
    return (((me >> 1) + sign * dz) & 3) * 2 + ((me & 1) ^ dy)


def to_all(array):
    return lax.all_to_all(array, "chan", 0, 0, tiled=True)


def pick(array, index, axis):
    return lax.dynamic_index_in_dim(array, index, axis, keepdims=False)


def core_swap(array):
    return lax.ppermute(array, "batch", [(0, 1), (1, 0), (2, 3), (3, 2)])


def frame_sums(pair):
    frame = lax.axis_index("frames")
    sums = pick(pair, frame, 0)
    for shift in (1, 3, 2):
        sent = pick(pair, (frame + shift) & 3, 0).astype(BF16)
        got = lax.ppermute(sent, "frames", [(i, (i + shift) % 4) for i in range(4)])
        sums = sums + got.astype(F32)
    return sums


def row_sums(sums):
    row = lax.axis_index("batch") >> 1
    sent = pick(sums, 1 - row, 0).astype(BF16)
    got = lax.ppermute(sent, "batch", [(0, 2), (1, 3), (2, 0), (3, 1)])
    return pick(sums, row, 0) + got.astype(F32)


def shards(tokens, cotangent, norm_gain, norm_bias, qkv_weight, out_weight, lengths, segments):
    recs, frames, model = tokens.shape
    rows = recs * frames
    width = out_weight.shape[0]
    me = lax.axis_index("chan")
    start = lax.axis_index("frames") * frames
    scalar = lambda value: value.reshape(1).astype(jnp.int32)

    weight = qkv_weight.transpose(1, 2, 0).reshape(3 * width, model)
    tie = lax.optimization_barrier
    core = lax.axis_index("batch") & 1
    half_out = lax.dynamic_slice_in_dim(out_weight, core * (width // 2), width // 2, 0)
    own_out = lax.all_gather(half_out, "chan", tiled=True)

    flat_tokens = tokens.reshape(rows, model)
    flat_cot = cotangent.reshape(rows, model)
    reach = start - CTX + jnp.arange(frames + 2 * CTX, dtype=jnp.int32)
    padded = jnp.pad(segments, ((0, 0), (CTX, CTX)), constant_values=-10)
    seg_keys = lax.dynamic_slice_in_dim(padded, start, frames + 2 * CTX, 1)
    seg_keys = jnp.where(reach[None, :] < lengths[:, None], seg_keys, -10)[:, :, None]
    seg_rows = lax.dynamic_slice_in_dim(segments, start, frames, 1)[:, None, :]

    normed, q, kv, g, kv_first, kv_last, live = project(
        lengths, flat_tokens, flat_cot, norm_gain, norm_bias, weight, out_weight
    )
    size = lax.axis_size("frames")
    up = [(i, i + 1) for i in range(size - 1)]
    down = [(i + 1, i) for i in range(size - 1)]
    before = lax.ppermute(kv_last, "frames", up)
    after = lax.ppermute(kv_first, "frames", down)

    results = []
    for rec in range(recs):
        mixed, dq, dkv, dbefore, dafter = attention(
            rec, q, kv, before, after, g, seg_keys, seg_rows, live
        )
        right = lax.ppermute(dbefore, "frames", down)
        left = lax.ppermute(dafter, "frames", up)
        results.append([dq, dkv, left, right, mixed])

    first, second = results
    count = lax.axis_size("chan")
    mixed = [to_all(result[4]).reshape(count * width, frames) for result in results]
    second[0], _ = tie((second[0], first[0]))

    split = lambda back: back.reshape(count, -1, model)
    second[0], mixed[0], mixed[1] = tie((second[0], mixed[0], mixed[1]))
    second_back = split(back_rows(*second[:4], weight))
    first[0], second_back, own_out = tie((first[0], second_back, own_out))
    first_back = split(back_rows(*first[:4], weight))
    parts = [to_all(first_back), to_all(second_back)]

    first[0], first_back, parts[1] = tie((first[0], first_back, parts[1]))
    other_out = core_swap(own_out)
    sent, kept = weight_grads(scalar(core), normed, flat_cot, first + second)
    sums = frame_sums(kept + core_swap(sent).astype(F32))
    sums, parts[0] = tie((sums, parts[0]))
    grad_proj = row_sums(sums).reshape(-1, 4, width)

    piece = finish(scalar(me), flat_tokens, flat_cot, norm_gain, parts)
    places = jnp.stack([me] + [peer_index(me, shift, -1) for shift in SHIFTS]).astype(jnp.int32)
    output = output_rows(flat_tokens, mixed, own_out, other_out)
    pieces = [to_peer(piece, shift) for shift in SHIFTS]
    pieces[0], output = tie((pieces[0], output))
    grad_tokens = assemble(places, [piece] + pieces)
    shape = (recs, frames, model)
    return (output.reshape(shape), grad_tokens.reshape(shape), grad_proj)


def solution(mesh):
    return jax.shard_map(
        shards,
        mesh=mesh,
        in_specs=(
            P("batch", "frames", None),
            P("batch", "frames", None),
            P(),
            P(),
            P(None, None, "chan"),
            P("chan", None),
            P("batch"),
            P("batch", None),
        ),
        out_specs=(
            P("batch", "frames", None),
            P("batch", "frames", None),
            P(("batch", "frames"), None, "chan"),
        ),
        check_vma=False,
    )
```

```python
import jax
import jax.numpy as jnp
from jax import lax
from jax.experimental import pallas as pl
from jax.experimental.pallas import tpu as pltpu
from jax.sharding import PartitionSpec as P

HEAD = 64
CTX = 256
EPS = 1e-05
NEG = -1e30

SHIFTS = ((1, 0), (3, 0), (0, 1), (1, 1), (3, 1), (2, 0), (2, 1))

F32 = jnp.float32
BF16 = jnp.bfloat16


def params(mebibytes=60):
    return pltpu.CompilerParams(vmem_limit_bytes=mebibytes * 1024 * 1024)


def dot_nn(a, b):
    return lax.dot_general(a, b, (((1,), (0,)), ((), ())), preferred_element_type=F32)


def dot_nt(a, b):
    return lax.dot_general(a, b, (((1,), (1,)), ((), ())), preferred_element_type=F32)


def dot_tn(a, b):
    return lax.dot_general(a, b, (((0,), (0,)), ((), ())), preferred_element_type=F32)


def norm_stats(tokens):
    values = tokens.astype(F32)
    centered = values - jnp.mean(values, axis=-1, keepdims=True)
    inverse = lax.rsqrt(jnp.mean(centered * centered, axis=-1, keepdims=True) + EPS)
    return centered * inverse, inverse


def project_body(
    lengths, tok, cot, gain, bias, weight, out_w, normed, q, kv, g, kv_first, kv_last, live
):
    width = q.shape[0]
    scaled, _ = norm_stats(tok[...])
    rows = (scaled * gain[...][None, :] + bias[...][None, :]).astype(BF16)
    normed[...] = rows
    qkv = dot_nt(weight[...], rows).astype(BF16)
    q[...] = qkv[:width]
    kv[...] = qkv[width:]
    step = pl.program_id(0)

    @pl.when(step % 2 == 0)
    def _():
        kv_first[...] = qkv[width:]

    @pl.when(step % 2 == 1)
    def _():
        kv_last[...] = qkv[width:]

    start = lax.axis_index("frames") * (2 * CTX) + (step % 2) * CTX
    position = start + lax.broadcasted_iota(jnp.int32, (1, CTX), 1)
    alive = jnp.where(position < lengths[step // 2], 1.0, 0.0)
    live[...] = alive
    g[...] = (dot_nt(out_w[...], cot[...]) * alive).astype(BF16)


def project(lengths, tokens, cotangent, gain, bias, weight, out_w):
    rows, model = tokens.shape
    width = out_w.shape[0]
    full = lambda shape: pl.BlockSpec(shape, lambda i: (0,) * len(shape))
    by_row = pl.BlockSpec((CTX, model), lambda i: (i, 0))
    by_col = lambda n: pl.BlockSpec((n, CTX), lambda i: (0, i))
    by_half = pl.BlockSpec((2 * width, CTX), lambda i: (0, i // 2))
    return pl.pallas_call(
        project_body,
        grid=(rows // CTX,),
        in_specs=[
            pl.BlockSpec(memory_space=pltpu.SMEM),
            by_row,
            by_row,
            full((model,)),
            full((model,)),
            full((3 * width, model)),
            full((width, model)),
        ],
        out_specs=[
            by_row,
            by_col(width),
            by_col(2 * width),
            by_col(width),
            by_half,
            by_half,
            by_col(1),
        ],
        out_shape=[
            jax.ShapeDtypeStruct((rows, model), BF16),
            jax.ShapeDtypeStruct((width, rows), BF16),
            jax.ShapeDtypeStruct((2 * width, rows), BF16),
            jax.ShapeDtypeStruct((width, rows), BF16),
            jax.ShapeDtypeStruct((2 * width, rows // 2), BF16),
            jax.ShapeDtypeStruct((2 * width, rows // 2), BF16),
            jax.ShapeDtypeStruct((1, rows), F32),
        ],
        compiler_params=params(),
        cost_estimate=pl.CostEstimate(flops=2400000000, bytes_accessed=15000000, transcendentals=0),
        name="project",
    )(lengths, tokens, cotangent, gain, bias, weight, out_w)


def attention_body(
    q, kv, before, after, g, seg_keys, seg_rows, live, mixed, dq, dkv, dbefore, dafter, acc, mask
):
    width = q.shape[0]
    span = 3 * CTX
    kv_all = jnp.concatenate([before[...], kv[...], after[...]], axis=1)
    q_small = q[...] * jnp.asarray(HEAD**-0.5, BF16)
    grads = g[...]
    acc[...] = jnp.zeros_like(acc)
    for tile in range(2):
        cols = slice(tile * CTX, (tile + 1) * CTX)
        keys = slice(tile * CTX, tile * CTX + span)
        away = (
            lax.broadcasted_iota(jnp.int32, (span, CTX), 0)
            - CTX
            - lax.broadcasted_iota(jnp.int32, (span, CTX), 1)
        )
        near = jnp.abs(away) <= CTX
        stretch = jnp.abs(seg_keys[0, keys, :] - seg_rows[0, :, cols]) <= 1
        visible = (near & stretch) | (away == 0)
        mask[...] = jnp.where(visible, 0.0, NEG)
        for head in range(width // HEAD):
            d = slice(head * HEAD, (head + 1) * HEAD)
            dv = slice(width + head * HEAD, width + (head + 1) * HEAD)
            k_t, v_t = kv_all[d, keys], kv_all[dv, keys]
            q_t, g_t = q_small[d, cols], grads[d, cols]
            scores = dot_tn(k_t, q_t) + mask[...]
            weights = jnp.exp(scores - jnp.max(scores, axis=0, keepdims=True))
            weights = weights * (1.0 / jnp.sum(weights, axis=0, keepdims=True))
            rounded = weights.astype(BF16)
            mixed[d, cols] = (dot_nn(v_t, rounded) * live[:, cols]).astype(BF16)
            grad_w = dot_tn(v_t, g_t)
            total = jnp.sum(weights * grad_w, axis=0, keepdims=True)
            grad_s = (weights * (grad_w - total)).astype(BF16)
            dq[d, cols] = (dot_nn(k_t, grad_s) * (HEAD**-0.5)).astype(BF16)
            acc[d, keys] += dot_nt(q_t, grad_s)
            acc[dv, keys] += dot_nt(g_t, rounded)
    frames = q.shape[1]
    dkv[...] = acc[:, CTX : CTX + frames]
    dbefore[...] = acc[:, :CTX].astype(BF16)
    dafter[...] = acc[:, CTX + frames :].astype(BF16)


def attention(rec, q, kv, before, after, g, seg_keys, seg_rows, live):
    width, rows = q.shape
    recs, span, _ = seg_keys.shape
    frames = rows // recs
    by_rec = lambda n, m: pl.BlockSpec((n, m), lambda i: (0, rec))
    whole = lambda n, m: pl.BlockSpec((n, m), lambda i: (0, 0))
    return pl.pallas_call(
        attention_body,
        grid=(1,),
        in_specs=[
            by_rec(width, frames),
            by_rec(2 * width, frames),
            by_rec(2 * width, CTX),
            by_rec(2 * width, CTX),
            by_rec(width, frames),
            pl.BlockSpec((1, span, 1), lambda i: (rec, 0, 0)),
            pl.BlockSpec((1, 1, frames), lambda i: (rec, 0, 0)),
            by_rec(1, frames),
        ],
        out_specs=[
            whole(width, frames),
            whole(width, frames),
            whole(2 * width, frames),
            whole(2 * width, CTX),
            whole(2 * width, CTX),
        ],
        out_shape=[
            jax.ShapeDtypeStruct((width, frames), BF16),
            jax.ShapeDtypeStruct((width, frames), BF16),
            jax.ShapeDtypeStruct((2 * width, frames), F32),
            jax.ShapeDtypeStruct((2 * width, CTX), BF16),
            jax.ShapeDtypeStruct((2 * width, CTX), BF16),
        ],
        scratch_shapes=[pltpu.VMEM((2 * width, span), F32), pltpu.VMEM((3 * CTX, CTX), F32)],
        compiler_params=params(),
        cost_estimate=pl.CostEstimate(flops=1000, bytes_accessed=1000, transcendentals=0),
        name="attention",
    )(q, kv, before, after, g, seg_keys, seg_rows, live)


def kv_grads(own, left, right):
    beside = jnp.concatenate([left[...], right[...]], axis=1).astype(F32)
    return (own[...] + beside).astype(BF16)


def back_body(dq, own, left, right, weight, out, flipped):
    width = dq.shape[0]

    @pl.when(pl.program_id(0) == 0)
    def _():
        flipped[:, :width] = dq[...].T
        flipped[:, width:] = kv_grads(own, left, right).T

    out[...] = dot_nn(flipped[...], weight[...]).astype(BF16)


def back_rows(dq, own, left, right, weight):
    width, rows = dq.shape
    model = weight.shape[1]
    tile = 512
    full = lambda n, m: pl.BlockSpec((n, m), lambda i: (0, 0))
    by_col = lambda n: pl.BlockSpec((n, tile), lambda i: (0, i))
    return pl.pallas_call(
        back_body,
        grid=(model // tile,),
        in_specs=[
            full(width, rows),
            full(2 * width, rows),
            full(2 * width, rows // 2),
            full(2 * width, rows // 2),
            by_col(3 * width),
        ],
        out_specs=by_col(rows),
        out_shape=jax.ShapeDtypeStruct((rows, model), BF16),
        scratch_shapes=[pltpu.VMEM((rows, 3 * width), BF16)],
        compiler_params=params(),
        cost_estimate=pl.CostEstimate(flops=900000000, bytes_accessed=4000000, transcendentals=0),
        name="back",
    )(dq, own, left, right, weight)


def weight_grads_body(core, normed, cot, *rest):
    pieces, (sent, kept, kv, query, mixed) = rest[:-5], rest[-5:]
    width, frames = pieces[0].shape
    del core

    @pl.when(pl.program_id(0) == 0)
    def _():
        for rec in range(2):
            dq, own, left, right, out = pieces[5 * rec : 5 * rec + 5]
            cols = slice(rec * frames, (rec + 1) * frames)
            kv[:, cols] = kv_grads(own, left, right)
            query[:, cols] = dq[...]
            mixed[:, cols] = out[...]

    turned = normed[...].T
    sums = [
        dot_nt(turned, query[...]),
        dot_nt(turned, kv[...]),
        dot_nt(cot[...].T, mixed[...]),
    ]
    offsets = (0, width, 3 * width)

    def write(target):
        for part, offset in zip(sums, offsets):
            shape = (target.shape[0], target.shape[2], part.shape[1])
            cols = slice(offset, offset + part.shape[1])
            target[:, 0, :, cols] = part.reshape(shape).astype(target.dtype)

    @pl.when(pl.program_id(0) < 2)
    def _():
        write(sent)

    @pl.when(pl.program_id(0) >= 2)
    def _():
        write(kept)


def weight_grads(core, normed, cotangent, pieces):
    rows, model = normed.shape
    width = pieces[0].shape[0]
    block = model // 4

    def by_step(i, c):
        return (0, (i % 2) * 2 + jnp.where(i < 2, 1 - c[0], c[0]))

    part = (4, 1, block // 4, 4 * width)
    return pl.pallas_call(
        weight_grads_body,
        grid_spec=pltpu.PrefetchScalarGridSpec(
            num_scalar_prefetch=1,
            grid=(4,),
            in_specs=[pl.BlockSpec((rows, block), by_step)] * 2
            + [pl.BlockSpec(piece.shape, lambda i, c: (0, 0)) for piece in pieces],
            out_specs=[
                pl.BlockSpec(part, lambda i, c: (0, jnp.minimum(i, 1), 0, 0)),
                pl.BlockSpec(part, lambda i, c: (0, jnp.maximum(i, 2) - 2, 0, 0)),
            ],
            scratch_shapes=[
                pltpu.VMEM((2 * width, rows), BF16),
                pltpu.VMEM((width, rows), BF16),
                pltpu.VMEM((width, rows), BF16),
            ],
        ),
        out_shape=[
            jax.ShapeDtypeStruct((4, 2, block // 4, 4 * width), BF16),
            jax.ShapeDtypeStruct((4, 2, block // 4, 4 * width), F32),
        ],
        compiler_params=params(),
        cost_estimate=pl.CostEstimate(flops=10000000000, bytes_accessed=12000000, transcendentals=0),
        name="weight_grads",
    )(core, normed, cotangent, *pieces)


def output_body(tok, near, far, *refs):
    weights, (out, stacks) = refs[:4], refs[4:]
    core = lax.axis_index("batch") & 1
    half = weights[0].shape[0] // 4
    total = tok[...].astype(F32)
    for index, weight in enumerate(weights):
        offset = core if index < 2 else 1 - core
        source = (near, far)[index % 2]
        for z in range(4):
            place = pl.multiple_of((2 * z + offset) * half, half)
            stacks[index, z * half : (z + 1) * half, :] = source[pl.ds(place, half), :]
        total = total + dot_nn(stacks[index].T, weight[...])
    out[...] = total.astype(BF16)


def output_rows(tokens, near, far, weights):
    rows, model = tokens.shape
    depth = weights[0].shape[0]
    by_row = pl.BlockSpec((CTX, model), lambda i: (i, 0))
    by_col = pl.BlockSpec((2 * depth, CTX), lambda i: (0, i))
    full = pl.BlockSpec((depth, model), lambda i: (0, 0))
    return pl.pallas_call(
        output_body,
        grid=(rows // CTX,),
        in_specs=[by_row, by_col, by_col] + [full] * 4,
        out_specs=by_row,
        out_shape=jax.ShapeDtypeStruct((rows, model), BF16),
        scratch_shapes=[pltpu.VMEM((4, depth, CTX), BF16)],
        compiler_params=params(28),
        cost_estimate=pl.CostEstimate(
            flops=10000000000, bytes_accessed=12000000, transcendentals=0
        ),
        name="output",
    )(tokens, near, far, *weights)


def finish_body(place, gain, *refs):
    out = refs[-1]
    chunk = refs[0].shape[0]
    for rec in range(2):
        tok, cot, parts = refs[3 * rec : 3 * rec + 3]
        back = jnp.sum(parts[...].astype(F32), axis=0)
        scaled, inverse = norm_stats(tok[...])
        weighted = back * gain[...][None, :]
        first = jnp.mean(weighted, axis=-1, keepdims=True)
        second = jnp.mean(weighted * scaled, axis=-1, keepdims=True)
        grad = inverse * (weighted - first - scaled * second) + cot[...].astype(F32)
        out[rec * chunk : (rec + 1) * chunk, :] = grad.astype(BF16)


def finish(place, tokens, cotangent, gain, parts):
    count, chunk, model = parts[0].shape
    at = lambda rec: pl.BlockSpec((chunk, model), lambda i, p: (rec * count + p[0], 0))
    whole = pl.BlockSpec((count, chunk, model), lambda i, p: (0, 0, 0))
    return pl.pallas_call(
        finish_body,
        grid_spec=pltpu.PrefetchScalarGridSpec(
            num_scalar_prefetch=1,
            grid=(1,),
            in_specs=[pl.BlockSpec((model,), lambda i, p: (0,))]
            + [at(0), at(0), whole, at(1), at(1), whole],
            out_specs=pl.BlockSpec((2 * chunk, model), lambda i, p: (0, 0)),
        ),
        out_shape=jax.ShapeDtypeStruct((2 * chunk, model), BF16),
        compiler_params=params(),
        cost_estimate=pl.CostEstimate(flops=10000000, bytes_accessed=5000000, transcendentals=0),
        name="finish",
    )(place, gain, tokens, cotangent, parts[0], tokens, cotangent, parts[1])


def assemble_body(places, *refs):
    pieces, out = refs[:-1], refs[-1]
    chunk = pieces[0].shape[0] // 2
    half = out.shape[0] // 2
    for index, piece in enumerate(pieces):
        for rec in range(2):
            place = pl.multiple_of(rec * half + places[index] * chunk, chunk)
            out[pl.ds(place, chunk), :] = piece[rec * chunk : (rec + 1) * chunk, :]


def assemble(places, pieces):
    chunk, model = pieces[0].shape
    count = len(pieces)
    tile = 512
    by_col = lambda n: pl.BlockSpec((n, tile), lambda i: (0, i))
    return pl.pallas_call(
        assemble_body,
        grid=(model // tile,),
        in_specs=[pl.BlockSpec(memory_space=pltpu.SMEM)] + [by_col(chunk)] * count,
        out_specs=by_col(count * chunk),
        out_shape=jax.ShapeDtypeStruct((count * chunk, model), BF16),
        compiler_params=params(16),
        cost_estimate=pl.CostEstimate(flops=0, bytes_accessed=6000000, transcendentals=0),
        name="assemble",
    )(places, *pieces)


def to_peer(array, shift):
    dz, dy = shift
    pairs = [
        (z * 2 + y, ((z + dz) % 4) * 2 + (y + dy) % 2) for z in range(4) for y in range(2)
    ]
    return lax.ppermute(array, "chan", pairs)


def peer_index(me, shift, sign):
    dz, dy = shift
    return (((me >> 1) + sign * dz) & 3) * 2 + ((me & 1) ^ dy)


def to_all(array):
    return lax.all_to_all(array, "chan", 0, 0, tiled=True)


def pick(array, index, axis):
    return lax.dynamic_index_in_dim(array, index, axis, keepdims=False)


def core_swap(array):
    return lax.ppermute(array, "batch", [(0, 1), (1, 0), (2, 3), (3, 2)])


def frame_sums(pair):
    frame = lax.axis_index("frames")
    sums = pick(pair, frame, 0)
    for shift in (1, 3, 2):
        sent = pick(pair, (frame + shift) & 3, 0).astype(BF16)
        got = lax.ppermute(sent, "frames", [(i, (i + shift) % 4) for i in range(4)])
        sums = sums + got.astype(F32)
    return sums


def row_sums(sums):
    row = lax.axis_index("batch") >> 1
    sent = pick(sums, 1 - row, 0).astype(BF16)
    got = lax.ppermute(sent, "batch", [(0, 2), (1, 3), (2, 0), (3, 1)])
    return pick(sums, row, 0) + got.astype(F32)


def over_z(array):
    groups = [[0, 2, 4, 6], [1, 3, 5, 7]]
    return lax.all_gather(array, "chan", axis_index_groups=groups, tiled=True)


def shards(tokens, cotangent, norm_gain, norm_bias, qkv_weight, out_weight, lengths, segments):
    recs, frames, model = tokens.shape
    rows = recs * frames
    width = out_weight.shape[0]
    me = lax.axis_index("chan")
    start = lax.axis_index("frames") * frames
    scalar = lambda value: value.reshape(1).astype(jnp.int32)

    weight = qkv_weight.transpose(1, 2, 0).reshape(3 * width, model)
    tie = lax.optimization_barrier
    core = lax.axis_index("batch") & 1
    half_out = lax.dynamic_slice_in_dim(out_weight, core * (width // 2), width // 2, 0)
    near_out = over_z(half_out)

    flat_tokens = tokens.reshape(rows, model)
    flat_cot = cotangent.reshape(rows, model)
    reach = start - CTX + jnp.arange(frames + 2 * CTX, dtype=jnp.int32)
    padded = jnp.pad(segments, ((0, 0), (CTX, CTX)), constant_values=-10)
    seg_keys = lax.dynamic_slice_in_dim(padded, start, frames + 2 * CTX, 1)
    seg_keys = jnp.where(reach[None, :] < lengths[:, None], seg_keys, -10)[:, :, None]
    seg_rows = lax.dynamic_slice_in_dim(segments, start, frames, 1)[:, None, :]

    normed, q, kv, g, kv_first, kv_last, live = project(
        lengths, flat_tokens, flat_cot, norm_gain, norm_bias, weight, out_weight
    )
    size = lax.axis_size("frames")
    up = [(i, i + 1) for i in range(size - 1)]
    down = [(i + 1, i) for i in range(size - 1)]
    before = lax.ppermute(kv_last, "frames", up)
    after = lax.ppermute(kv_first, "frames", down)
    before, after, near_out = tie((before, after, near_out))
    far_out = to_peer(near_out, (0, 1))

    results = []
    for rec in range(recs):
        mixed, dq, dkv, dbefore, dafter = attention(
            rec, q, kv, before, after, g, seg_keys, seg_rows, live
        )
        right = lax.ppermute(dbefore, "frames", down)
        left = lax.ppermute(dafter, "frames", up)
        results.append([dq, dkv, left, right, mixed])

    first, second = results
    count = lax.axis_size("chan")
    mixed = jnp.concatenate([first[4], second[4]], axis=1)
    near_mixed = over_z(mixed)
    peer_mixed = to_peer(mixed, (0, 1))
    far_mixed = over_z(peer_mixed)
    second[0], _ = tie((second[0], first[0]))

    split = lambda back: back.reshape(count, -1, model)
    second_back = split(back_rows(*second[:4], weight))
    first[0], second_back, far_out = tie((first[0], second_back, far_out))
    first_back = split(back_rows(*first[:4], weight))
    parts = [to_all(first_back), to_all(second_back)]

    first[0], first_back, parts[1] = tie((first[0], first_back, parts[1]))
    sent, kept = weight_grads(scalar(core), normed, flat_cot, first + second)
    sums = frame_sums(kept + core_swap(sent).astype(F32))
    sums, parts[0], near_mixed = tie((sums, parts[0], near_mixed))
    grad_proj = row_sums(sums).reshape(-1, 4, width)

    piece = finish(scalar(me), flat_tokens, flat_cot, norm_gain, parts)
    places = jnp.stack([me] + [peer_index(me, shift, -1) for shift in SHIFTS]).astype(jnp.int32)
    own = [near_out, far_out]
    output = output_rows(
        flat_tokens, near_mixed, far_mixed, own + [core_swap(array) for array in own]
    )
    pieces = [to_peer(piece, shift) for shift in SHIFTS]
    pieces[0], output = tie((pieces[0], output))
    grad_tokens = assemble(places, [piece] + pieces)
    shape = (recs, frames, model)
    return (output.reshape(shape), grad_tokens.reshape(shape), grad_proj)


def solution(mesh):
    return jax.shard_map(
        shards,
        mesh=mesh,
        in_specs=(
            P("batch", "frames", None),
            P("batch", "frames", None),
            P(),
            P(),
            P(None, None, "chan"),
            P("chan", None),
            P("batch"),
            P("batch", None),
        ),
        out_specs=(
            P("batch", "frames", None),
            P("batch", "frames", None),
            P(("batch", "frames"), None, "chan"),
        ),
        check_vma=False,
    )
```

```python
import jax
import jax.numpy as jnp
from jax import lax
from jax.experimental import pallas as pl
from jax.experimental.pallas import tpu as pltpu
from jax.sharding import PartitionSpec as P

HEAD = 64
CTX = 256
EPS = 1e-05
NEG = -1e30

SHIFTS = ((2, 1), (2, 0), (3, 1), (1, 1), (0, 1), (3, 0), (1, 0))

F32 = jnp.float32
BF16 = jnp.bfloat16


def params(mebibytes=60):
    return pltpu.CompilerParams(vmem_limit_bytes=mebibytes * 1024 * 1024)


def dot_nn(a, b):
    return lax.dot_general(a, b, (((1,), (0,)), ((), ())), preferred_element_type=F32)


def dot_nt(a, b):
    return lax.dot_general(a, b, (((1,), (1,)), ((), ())), preferred_element_type=F32)


def dot_tn(a, b):
    return lax.dot_general(a, b, (((0,), (0,)), ((), ())), preferred_element_type=F32)


def norm_stats(tokens):
    values = tokens.astype(F32)
    centered = values - jnp.mean(values, axis=-1, keepdims=True)
    inverse = lax.rsqrt(jnp.mean(centered * centered, axis=-1, keepdims=True) + EPS)
    return centered * inverse, inverse


def project_body(
    lengths, tok, cot, gain, bias, weight, out_w, normed, q, kv, g, kv_first, kv_last, live
):
    width = q.shape[0]
    scaled, _ = norm_stats(tok[...])
    rows = (scaled * gain[...][None, :] + bias[...][None, :]).astype(BF16)
    normed[...] = rows
    qkv = dot_nt(weight[...], rows).astype(BF16)
    q[...] = qkv[:width]
    kv[...] = qkv[width:]
    step = pl.program_id(0)

    @pl.when(step % 2 == 0)
    def _():
        kv_first[...] = qkv[width:]

    @pl.when(step % 2 == 1)
    def _():
        kv_last[...] = qkv[width:]

    start = lax.axis_index("frames") * (2 * CTX) + (step % 2) * CTX
    position = start + lax.broadcasted_iota(jnp.int32, (1, CTX), 1)
    alive = jnp.where(position < lengths[step // 2], 1.0, 0.0)
    live[...] = alive
    g[...] = (dot_nt(out_w[...], cot[...]) * alive).astype(BF16)


def project(lengths, tokens, cotangent, gain, bias, weight, out_w):
    rows, model = tokens.shape
    width = out_w.shape[0]
    full = lambda shape: pl.BlockSpec(shape, lambda i: (0,) * len(shape))
    by_row = pl.BlockSpec((CTX, model), lambda i: (i, 0))
    by_col = lambda n: pl.BlockSpec((n, CTX), lambda i: (0, i))
    by_half = pl.BlockSpec((2 * width, CTX), lambda i: (0, i // 2))
    return pl.pallas_call(
        project_body,
        grid=(rows // CTX,),
        in_specs=[
            pl.BlockSpec(memory_space=pltpu.SMEM),
            by_row,
            by_row,
            full((model,)),
            full((model,)),
            full((3 * width, model)),
            full((width, model)),
        ],
        out_specs=[
            by_row,
            by_col(width),
            by_col(2 * width),
            by_col(width),
            by_half,
            by_half,
            by_col(1),
        ],
        out_shape=[
            jax.ShapeDtypeStruct((rows, model), BF16),
            jax.ShapeDtypeStruct((width, rows), BF16),
            jax.ShapeDtypeStruct((2 * width, rows), BF16),
            jax.ShapeDtypeStruct((width, rows), BF16),
            jax.ShapeDtypeStruct((2 * width, rows // 2), BF16),
            jax.ShapeDtypeStruct((2 * width, rows // 2), BF16),
            jax.ShapeDtypeStruct((1, rows), F32),
        ],
        compiler_params=params(),
        cost_estimate=pl.CostEstimate(flops=2400000000, bytes_accessed=15000000, transcendentals=0),
        name="project",
    )(lengths, tokens, cotangent, gain, bias, weight, out_w)


def attention_body(
    q, kv, before, after, g, seg_keys, seg_rows, live, mixed, dq, dkv, dbefore, dafter, acc, mask
):
    width = q.shape[0]
    span = 3 * CTX
    kv_all = jnp.concatenate([before[...], kv[...], after[...]], axis=1)
    q_small = q[...] * jnp.asarray(HEAD**-0.5, BF16)
    grads = g[...]
    acc[...] = jnp.zeros_like(acc)
    for tile in range(2):
        cols = slice(tile * CTX, (tile + 1) * CTX)
        keys = slice(tile * CTX, tile * CTX + span)
        away = (
            lax.broadcasted_iota(jnp.int32, (span, CTX), 0)
            - CTX
            - lax.broadcasted_iota(jnp.int32, (span, CTX), 1)
        )
        near = jnp.abs(away) <= CTX
        stretch = jnp.abs(seg_keys[0, keys, :] - seg_rows[0, :, cols]) <= 1
        visible = (near & stretch) | (away == 0)
        mask[...] = jnp.where(visible, 0.0, NEG)
        for head in range(width // HEAD):
            d = slice(head * HEAD, (head + 1) * HEAD)
            dv = slice(width + head * HEAD, width + (head + 1) * HEAD)
            k_t, v_t = kv_all[d, keys], kv_all[dv, keys]
            q_t, g_t = q_small[d, cols], grads[d, cols]
            scores = dot_tn(k_t, q_t) + mask[...]
            weights = jnp.exp(scores - jnp.max(scores, axis=0, keepdims=True))
            weights = weights * (1.0 / jnp.sum(weights, axis=0, keepdims=True))
            rounded = weights.astype(BF16)
            mixed[d, cols] = (dot_nn(v_t, rounded) * live[:, cols]).astype(BF16)
            grad_w = dot_tn(v_t, g_t)
            total = jnp.sum(weights * grad_w, axis=0, keepdims=True)
            grad_s = (weights * (grad_w - total)).astype(BF16)
            dq[d, cols] = (dot_nn(k_t, grad_s) * (HEAD**-0.5)).astype(BF16)
            acc[d, keys] += dot_nt(q_t, grad_s)
            acc[dv, keys] += dot_nt(g_t, rounded)
    frames = q.shape[1]
    dkv[...] = acc[:, CTX : CTX + frames]
    dbefore[...] = acc[:, :CTX].astype(BF16)
    dafter[...] = acc[:, CTX + frames :].astype(BF16)


def attention(rec, q, kv, before, after, g, seg_keys, seg_rows, live):
    width, rows = q.shape
    recs, span, _ = seg_keys.shape
    frames = rows // recs
    by_rec = lambda n, m: pl.BlockSpec((n, m), lambda i: (0, rec))
    whole = lambda n, m: pl.BlockSpec((n, m), lambda i: (0, 0))
    return pl.pallas_call(
        attention_body,
        grid=(1,),
        in_specs=[
            by_rec(width, frames),
            by_rec(2 * width, frames),
            by_rec(2 * width, CTX),
            by_rec(2 * width, CTX),
            by_rec(width, frames),
            pl.BlockSpec((1, span, 1), lambda i: (rec, 0, 0)),
            pl.BlockSpec((1, 1, frames), lambda i: (rec, 0, 0)),
            by_rec(1, frames),
        ],
        out_specs=[
            whole(width, frames),
            whole(width, frames),
            whole(2 * width, frames),
            whole(2 * width, CTX),
            whole(2 * width, CTX),
        ],
        out_shape=[
            jax.ShapeDtypeStruct((width, frames), BF16),
            jax.ShapeDtypeStruct((width, frames), BF16),
            jax.ShapeDtypeStruct((2 * width, frames), F32),
            jax.ShapeDtypeStruct((2 * width, CTX), BF16),
            jax.ShapeDtypeStruct((2 * width, CTX), BF16),
        ],
        scratch_shapes=[pltpu.VMEM((2 * width, span), F32), pltpu.VMEM((3 * CTX, CTX), F32)],
        compiler_params=params(),
        cost_estimate=pl.CostEstimate(flops=1000, bytes_accessed=1000, transcendentals=0),
        name="attention",
    )(q, kv, before, after, g, seg_keys, seg_rows, live)


def kv_grads(own, left, right):
    beside = jnp.concatenate([left[...], right[...]], axis=1).astype(F32)
    return (own[...] + beside).astype(BF16)


def back_body(dq, own, left, right, weight, out, flipped):
    width = dq.shape[0]

    @pl.when(pl.program_id(0) == 0)
    def _():
        flipped[:, :width] = dq[...].T
        flipped[:, width:] = kv_grads(own, left, right).T

    out[...] = dot_nn(flipped[...], weight[...]).astype(BF16)


def back_rows(dq, own, left, right, weight):
    width, rows = dq.shape
    model = weight.shape[1]
    tile = 512
    full = lambda n, m: pl.BlockSpec((n, m), lambda i: (0, 0))
    by_col = lambda n: pl.BlockSpec((n, tile), lambda i: (0, i))
    return pl.pallas_call(
        back_body,
        grid=(model // tile,),
        in_specs=[
            full(width, rows),
            full(2 * width, rows),
            full(2 * width, rows // 2),
            full(2 * width, rows // 2),
            by_col(3 * width),
        ],
        out_specs=by_col(rows),
        out_shape=jax.ShapeDtypeStruct((rows, model), BF16),
        scratch_shapes=[pltpu.VMEM((rows, 3 * width), BF16)],
        compiler_params=params(),
        cost_estimate=pl.CostEstimate(flops=900000000, bytes_accessed=4000000, transcendentals=0),
        name="back",
    )(dq, own, left, right, weight)


def weight_grads_body(core, normed, cot, *rest):
    pieces, (sent, kept, grads, mixed) = rest[:-4], rest[-4:]
    width, frames = pieces[0].shape
    del core

    @pl.when(pl.program_id(0) == 0)
    def _():
        for rec in range(2):
            dq, own, left, right, out = pieces[5 * rec : 5 * rec + 5]
            rows = slice(rec * frames, (rec + 1) * frames)
            stacked = jnp.concatenate([dq[...], kv_grads(own, left, right)], axis=0)
            grads[rows, :] = stacked.T
            mixed[rows, :] = out[...].T

    sums = [dot_nn(normed[...].T, grads[...]), dot_nn(cot[...].T, mixed[...])]

    def write(target):
        for part, offset in zip(sums, (0, 3 * width)):
            shape = (target.shape[0], target.shape[2], part.shape[1])
            cols = slice(offset, offset + part.shape[1])
            target[:, 0, :, cols] = part.reshape(shape).astype(target.dtype)

    @pl.when(pl.program_id(0) < 2)
    def _():
        write(sent)

    @pl.when(pl.program_id(0) >= 2)
    def _():
        write(kept)


def weight_grads(core, normed, cotangent, pieces):
    rows, model = normed.shape
    width = pieces[0].shape[0]
    block = model // 4

    def by_step(i, c):
        return (0, (i % 2) * 2 + jnp.where(i < 2, 1 - c[0], c[0]))

    part = (4, 1, block // 4, 4 * width)
    return pl.pallas_call(
        weight_grads_body,
        grid_spec=pltpu.PrefetchScalarGridSpec(
            num_scalar_prefetch=1,
            grid=(4,),
            in_specs=[pl.BlockSpec((rows, block), by_step)] * 2
            + [pl.BlockSpec(piece.shape, lambda i, c: (0, 0)) for piece in pieces],
            out_specs=[
                pl.BlockSpec(part, lambda i, c: (0, jnp.minimum(i, 1), 0, 0)),
                pl.BlockSpec(part, lambda i, c: (0, jnp.maximum(i, 2) - 2, 0, 0)),
            ],
            scratch_shapes=[
                pltpu.VMEM((rows, 3 * width), BF16),
                pltpu.VMEM((rows, width), BF16),
            ],
        ),
        out_shape=[
            jax.ShapeDtypeStruct((4, 2, block // 4, 4 * width), BF16),
            jax.ShapeDtypeStruct((4, 2, block // 4, 4 * width), BF16),
        ],
        compiler_params=params(),
        cost_estimate=pl.CostEstimate(flops=10000000000, bytes_accessed=12000000, transcendentals=0),
        name="weight_grads",
    )(core, normed, cotangent, *pieces)


def output_body(tok, near, far, *refs):
    weights, (out, stacks) = refs[:4], refs[4:]
    core = lax.axis_index("batch") & 1
    half = weights[0].shape[0] // 4
    total = tok[...].astype(F32)
    for index, weight in enumerate(weights):
        offset = core if index < 2 else 1 - core
        source = (near, far)[index % 2]
        for z in range(4):
            place = pl.multiple_of((2 * z + offset) * half, half)
            stacks[index, z * half : (z + 1) * half, :] = source[pl.ds(place, half), :]
        total = total + dot_nn(stacks[index].T, weight[...])
    out[...] = total.astype(BF16)


def output_rows(tokens, near, far, weights):
    rows, model = tokens.shape
    depth = weights[0].shape[0]
    by_row = pl.BlockSpec((CTX, model), lambda i: (i, 0))
    by_col = pl.BlockSpec((2 * depth, CTX), lambda i: (0, i))
    full = pl.BlockSpec((depth, model), lambda i: (0, 0))
    return pl.pallas_call(
        output_body,
        grid=(rows // CTX,),
        in_specs=[by_row, by_col, by_col] + [full] * 4,
        out_specs=by_row,
        out_shape=jax.ShapeDtypeStruct((rows, model), BF16),
        scratch_shapes=[pltpu.VMEM((4, depth, CTX), BF16)],
        compiler_params=params(28),
        cost_estimate=pl.CostEstimate(
            flops=10000000000, bytes_accessed=12000000, transcendentals=0
        ),
        name="output",
    )(tokens, near, far, *weights)


def finish_body(place, gain, *refs):
    out = refs[-1]
    chunk = refs[0].shape[0]
    for rec in range(2):
        tok, cot, parts = refs[3 * rec : 3 * rec + 3]
        back = jnp.sum(parts[...].astype(F32), axis=0)
        scaled, inverse = norm_stats(tok[...])
        weighted = back * gain[...][None, :]
        first = jnp.mean(weighted, axis=-1, keepdims=True)
        second = jnp.mean(weighted * scaled, axis=-1, keepdims=True)
        grad = inverse * (weighted - first - scaled * second) + cot[...].astype(F32)
        out[rec * chunk : (rec + 1) * chunk, :] = grad.astype(BF16)


def finish(place, tokens, cotangent, gain, parts):
    count, chunk, model = parts[0].shape
    at = lambda rec: pl.BlockSpec((chunk, model), lambda i, p: (rec * count + p[0], 0))
    whole = pl.BlockSpec((count, chunk, model), lambda i, p: (0, 0, 0))
    return pl.pallas_call(
        finish_body,
        grid_spec=pltpu.PrefetchScalarGridSpec(
            num_scalar_prefetch=1,
            grid=(1,),
            in_specs=[pl.BlockSpec((model,), lambda i, p: (0,))]
            + [at(0), at(0), whole, at(1), at(1), whole],
            out_specs=pl.BlockSpec((2 * chunk, model), lambda i, p: (0, 0)),
        ),
        out_shape=jax.ShapeDtypeStruct((2 * chunk, model), BF16),
        compiler_params=params(),
        cost_estimate=pl.CostEstimate(flops=10000000, bytes_accessed=5000000, transcendentals=0),
        name="finish",
    )(place, gain, tokens, cotangent, parts[0], tokens, cotangent, parts[1])


def assemble_body(places, *refs):
    pieces, out = refs[:-1], refs[-1]
    chunk = pieces[0].shape[0] // 2
    half = out.shape[0] // 2
    for index, piece in enumerate(pieces):
        for rec in range(2):
            place = pl.multiple_of(rec * half + places[index] * chunk, chunk)
            out[pl.ds(place, chunk), :] = piece[rec * chunk : (rec + 1) * chunk, :]


def assemble(places, pieces):
    chunk, model = pieces[0].shape
    count = len(pieces)
    tile = 512
    by_col = lambda n: pl.BlockSpec((n, tile), lambda i: (0, i))
    return pl.pallas_call(
        assemble_body,
        grid=(model // tile,),
        in_specs=[pl.BlockSpec(memory_space=pltpu.SMEM)] + [by_col(chunk)] * count,
        out_specs=by_col(count * chunk),
        out_shape=jax.ShapeDtypeStruct((count * chunk, model), BF16),
        compiler_params=params(16),
        cost_estimate=pl.CostEstimate(flops=0, bytes_accessed=6000000, transcendentals=0),
        name="assemble",
    )(places, *pieces)


def to_peer(array, shift):
    dz, dy = shift
    pairs = [
        (z * 2 + y, ((z + dz) % 4) * 2 + (y + dy) % 2) for z in range(4) for y in range(2)
    ]
    return lax.ppermute(array, "chan", pairs)


def peer_index(me, shift, sign):
    dz, dy = shift
    return (((me >> 1) + sign * dz) & 3) * 2 + ((me & 1) ^ dy)


def to_all(array):
    return lax.all_to_all(array, "chan", 0, 0, tiled=True)


def pick(array, index, axis):
    return lax.dynamic_index_in_dim(array, index, axis, keepdims=False)


def core_swap(array):
    return lax.ppermute(array, "batch", [(0, 1), (1, 0), (2, 3), (3, 2)])


def frame_sums(pair):
    frame = lax.axis_index("frames")
    sums = pick(pair, frame, 0)
    for shift in (1, 3, 2):
        sent = pick(pair, (frame + shift) & 3, 0).astype(BF16)
        got = lax.ppermute(sent, "frames", [(i, (i + shift) % 4) for i in range(4)])
        sums = sums + got.astype(F32)
    return sums


def row_sums(sums):
    row = lax.axis_index("batch") >> 1
    sent = pick(sums, 1 - row, 0).astype(BF16)
    got = lax.ppermute(sent, "batch", [(0, 2), (1, 3), (2, 0), (3, 1)])
    return pick(sums, row, 0) + got.astype(F32)


def over_z(array):
    groups = [[0, 2, 4, 6], [1, 3, 5, 7]]
    return lax.all_gather(array, "chan", axis_index_groups=groups, tiled=True)


def shards(tokens, cotangent, norm_gain, norm_bias, qkv_weight, out_weight, lengths, segments):
    recs, frames, model = tokens.shape
    rows = recs * frames
    width = out_weight.shape[0]
    me = lax.axis_index("chan")
    start = lax.axis_index("frames") * frames
    scalar = lambda value: value.reshape(1).astype(jnp.int32)

    weight = qkv_weight.transpose(1, 2, 0).reshape(3 * width, model)
    tie = lax.optimization_barrier
    core = lax.axis_index("batch") & 1
    half_out = lax.dynamic_slice_in_dim(out_weight, core * (width // 2), width // 2, 0)
    near_out = over_z(half_out)

    flat_tokens = tokens.reshape(rows, model)
    flat_cot = cotangent.reshape(rows, model)
    reach = start - CTX + jnp.arange(frames + 2 * CTX, dtype=jnp.int32)
    padded = jnp.pad(segments, ((0, 0), (CTX, CTX)), constant_values=-10)
    seg_keys = lax.dynamic_slice_in_dim(padded, start, frames + 2 * CTX, 1)
    seg_keys = jnp.where(reach[None, :] < lengths[:, None], seg_keys, -10)[:, :, None]
    seg_rows = lax.dynamic_slice_in_dim(segments, start, frames, 1)[:, None, :]

    normed, q, kv, g, kv_first, kv_last, live = project(
        lengths, flat_tokens, flat_cot, norm_gain, norm_bias, weight, out_weight
    )
    size = lax.axis_size("frames")
    up = [(i, i + 1) for i in range(size - 1)]
    down = [(i + 1, i) for i in range(size - 1)]
    before = lax.ppermute(kv_last, "frames", up)
    after = lax.ppermute(kv_first, "frames", down)
    half_out, kv_first = tie((half_out, kv_first))
    peer_out = to_peer(half_out, (0, 1))
    before, after, peer_out = tie((before, after, peer_out))
    far_out = over_z(peer_out)

    results = [None] * recs
    for rec in reversed(range(recs)):
        mixed, dq, dkv, dbefore, dafter = attention(
            rec, q, kv, before, after, g, seg_keys, seg_rows, live
        )
        right = lax.ppermute(dbefore, "frames", down)
        left = lax.ppermute(dafter, "frames", up)
        mixed, q = tie((mixed, q))
        results[rec] = [dq, dkv, left, right, mixed]

    first, second = results
    count = lax.axis_size("chan")
    second[0], _ = tie((second[0], first[0]))

    split = lambda back: back.reshape(count, -1, model)
    second_back = split(back_rows(*second[:4], weight))
    mixed, second_back = tie((jnp.concatenate([first[4], second[4]], axis=1), second_back))
    near_mixed = over_z(mixed)
    peer_mixed = to_peer(mixed, (0, 1))
    first[0], second_back, far_out, near_out = tie((first[0], second_back, far_out, near_out))
    sent, kept = weight_grads(scalar(core), normed, flat_cot, first + second)
    second_parts = to_all(second_back)
    first[0], sent, second_parts = tie((first[0], sent, second_parts))
    first_back = split(back_rows(*first[:4], weight))
    first_back, peer_mixed = tie((first_back, peer_mixed))
    far_mixed = over_z(peer_mixed)
    parts = [to_all(first_back), second_parts]

    sums = frame_sums(kept.astype(F32) + core_swap(sent).astype(F32))
    sums, parts[0] = tie((sums, parts[0]))
    grad_proj = row_sums(sums).reshape(-1, 4, width)

    piece = finish(scalar(me), flat_tokens, flat_cot, norm_gain, parts)
    places = jnp.stack([me] + [peer_index(me, shift, -1) for shift in SHIFTS]).astype(jnp.int32)
    own = [near_out, far_out]
    output = output_rows(
        flat_tokens, near_mixed, far_mixed, own + [core_swap(array) for array in own]
    )
    pieces = [to_peer(piece, shift) for shift in SHIFTS]
    pieces[0], output = tie((pieces[0], output))
    grad_tokens = assemble(places, [piece] + pieces)
    shape = (recs, frames, model)
    return (output.reshape(shape), grad_tokens.reshape(shape), grad_proj)


def solution(mesh):
    return jax.shard_map(
        shards,
        mesh=mesh,
        in_specs=(
            P("batch", "frames", None),
            P("batch", "frames", None),
            P(),
            P(),
            P(None, None, "chan"),
            P("chan", None),
            P("batch"),
            P("batch", None),
        ),
        out_specs=(
            P("batch", "frames", None),
            P("batch", "frames", None),
            P(("batch", "frames"), None, "chan"),
        ),
        check_vma=False,
    )
```

```python
import jax
import jax.numpy as jnp
from jax import lax
from jax.experimental import pallas as pl
from jax.experimental.pallas import tpu as pltpu
from jax.sharding import PartitionSpec as P

HEAD = 64
CTX = 256
EPS = 1e-05
NEG = -1e30

SHIFTS = ((1, 0), (3, 0), (0, 1), (1, 1), (3, 1), (2, 0), (2, 1))

F32 = jnp.float32
BF16 = jnp.bfloat16


def params(mebibytes=60):
    return pltpu.CompilerParams(vmem_limit_bytes=mebibytes * 1024 * 1024)


def dot_nn(a, b):
    return lax.dot_general(a, b, (((1,), (0,)), ((), ())), preferred_element_type=F32)


def dot_nt(a, b):
    return lax.dot_general(a, b, (((1,), (1,)), ((), ())), preferred_element_type=F32)


def dot_tn(a, b):
    return lax.dot_general(a, b, (((0,), (0,)), ((), ())), preferred_element_type=F32)


def norm_stats(tokens):
    values = tokens.astype(F32)
    centered = values - jnp.mean(values, axis=-1, keepdims=True)
    inverse = lax.rsqrt(jnp.mean(centered * centered, axis=-1, keepdims=True) + EPS)
    return centered * inverse, inverse


def project_body(
    lengths, tok, cot, gain, bias, weight, out_w, normed, q, kv, g, kv_first, kv_last, live
):
    width = q.shape[0]
    scaled, _ = norm_stats(tok[...])
    rows = (scaled * gain[...][None, :] + bias[...][None, :]).astype(BF16)
    normed[...] = rows
    qkv = dot_nt(weight[...], rows).astype(BF16)
    q[...] = qkv[:width]
    kv[...] = qkv[width:]
    step = pl.program_id(0)

    @pl.when(step % 2 == 0)
    def _():
        kv_first[...] = qkv[width:]

    @pl.when(step % 2 == 1)
    def _():
        kv_last[...] = qkv[width:]

    start = lax.axis_index("frames") * (2 * CTX) + (step % 2) * CTX
    position = start + lax.broadcasted_iota(jnp.int32, (1, CTX), 1)
    alive = jnp.where(position < lengths[step // 2], 1.0, 0.0)
    live[...] = alive
    g[...] = (dot_nt(out_w[...], cot[...]) * alive).astype(BF16)


def project(lengths, tokens, cotangent, gain, bias, weight, out_w):
    rows, model = tokens.shape
    width = out_w.shape[0]
    full = lambda shape: pl.BlockSpec(shape, lambda i: (0,) * len(shape))
    by_row = pl.BlockSpec((CTX, model), lambda i: (i, 0))
    by_col = lambda n: pl.BlockSpec((n, CTX), lambda i: (0, i))
    by_half = pl.BlockSpec((2 * width, CTX), lambda i: (0, i // 2))
    return pl.pallas_call(
        project_body,
        grid=(rows // CTX,),
        in_specs=[
            pl.BlockSpec(memory_space=pltpu.SMEM),
            by_row,
            by_row,
            full((model,)),
            full((model,)),
            full((3 * width, model)),
            full((width, model)),
        ],
        out_specs=[
            by_row,
            by_col(width),
            by_col(2 * width),
            by_col(width),
            by_half,
            by_half,
            by_col(1),
        ],
        out_shape=[
            jax.ShapeDtypeStruct((rows, model), BF16),
            jax.ShapeDtypeStruct((width, rows), BF16),
            jax.ShapeDtypeStruct((2 * width, rows), BF16),
            jax.ShapeDtypeStruct((width, rows), BF16),
            jax.ShapeDtypeStruct((2 * width, rows // 2), BF16),
            jax.ShapeDtypeStruct((2 * width, rows // 2), BF16),
            jax.ShapeDtypeStruct((1, rows), F32),
        ],
        compiler_params=params(),
        cost_estimate=pl.CostEstimate(flops=2400000000, bytes_accessed=15000000, transcendentals=0),
        name="project",
    )(lengths, tokens, cotangent, gain, bias, weight, out_w)


def attention_body(
    q, kv, before, after, g, seg_keys, seg_rows, live, mixed, dq, dkv, dbefore, dafter, acc, mask
):
    width = q.shape[0]
    span = 3 * CTX
    kv_all = jnp.concatenate([before[...], kv[...], after[...]], axis=1)
    q_small = q[...] * jnp.asarray(HEAD**-0.5, BF16)
    grads = g[...]
    acc[...] = jnp.zeros_like(acc)
    for tile in range(2):
        cols = slice(tile * CTX, (tile + 1) * CTX)
        keys = slice(tile * CTX, tile * CTX + span)
        away = (
            lax.broadcasted_iota(jnp.int32, (span, CTX), 0)
            - CTX
            - lax.broadcasted_iota(jnp.int32, (span, CTX), 1)
        )
        near = jnp.abs(away) <= CTX
        stretch = jnp.abs(seg_keys[0, keys, :] - seg_rows[0, :, cols]) <= 1
        visible = (near & stretch) | (away == 0)
        mask[...] = jnp.where(visible, 0.0, NEG)
        for head in range(width // HEAD):
            d = slice(head * HEAD, (head + 1) * HEAD)
            dv = slice(width + head * HEAD, width + (head + 1) * HEAD)
            k_t, v_t = kv_all[d, keys], kv_all[dv, keys]
            q_t, g_t = q_small[d, cols], grads[d, cols]
            scores = dot_tn(k_t, q_t) + mask[...]
            weights = jnp.exp(scores - jnp.max(scores, axis=0, keepdims=True))
            weights = weights * (1.0 / jnp.sum(weights, axis=0, keepdims=True))
            rounded = weights.astype(BF16)
            mixed[d, cols] = (dot_nn(v_t, rounded) * live[:, cols]).astype(BF16)
            grad_w = dot_tn(v_t, g_t)
            total = jnp.sum(weights * grad_w, axis=0, keepdims=True)
            grad_s = (weights * (grad_w - total)).astype(BF16)
            dq[d, cols] = (dot_nn(k_t, grad_s) * (HEAD**-0.5)).astype(BF16)
            acc[d, keys] += dot_nt(q_t, grad_s)
            acc[dv, keys] += dot_nt(g_t, rounded)
    frames = q.shape[1]
    dkv[...] = acc[:, CTX : CTX + frames]
    dbefore[...] = acc[:, :CTX].astype(BF16)
    dafter[...] = acc[:, CTX + frames :].astype(BF16)


def attention(rec, q, kv, before, after, g, seg_keys, seg_rows, live):
    width, rows = q.shape
    recs, span, _ = seg_keys.shape
    frames = rows // recs
    by_rec = lambda n, m: pl.BlockSpec((n, m), lambda i: (0, rec))
    whole = lambda n, m: pl.BlockSpec((n, m), lambda i: (0, 0))
    return pl.pallas_call(
        attention_body,
        grid=(1,),
        in_specs=[
            by_rec(width, frames),
            by_rec(2 * width, frames),
            by_rec(2 * width, CTX),
            by_rec(2 * width, CTX),
            by_rec(width, frames),
            pl.BlockSpec((1, span, 1), lambda i: (rec, 0, 0)),
            pl.BlockSpec((1, 1, frames), lambda i: (rec, 0, 0)),
            by_rec(1, frames),
        ],
        out_specs=[
            whole(width, frames),
            whole(width, frames),
            whole(2 * width, frames),
            whole(2 * width, CTX),
            whole(2 * width, CTX),
        ],
        out_shape=[
            jax.ShapeDtypeStruct((width, frames), BF16),
            jax.ShapeDtypeStruct((width, frames), BF16),
            jax.ShapeDtypeStruct((2 * width, frames), F32),
            jax.ShapeDtypeStruct((2 * width, CTX), BF16),
            jax.ShapeDtypeStruct((2 * width, CTX), BF16),
        ],
        scratch_shapes=[pltpu.VMEM((2 * width, span), F32), pltpu.VMEM((3 * CTX, CTX), F32)],
        compiler_params=params(),
        cost_estimate=pl.CostEstimate(flops=1000, bytes_accessed=1000, transcendentals=0),
        name="attention",
    )(q, kv, before, after, g, seg_keys, seg_rows, live)


def kv_grads(own, left, right):
    beside = jnp.concatenate([left[...], right[...]], axis=1).astype(F32)
    return (own[...] + beside).astype(BF16)


def back_body(dq, own, left, right, weight, out, flipped):
    width = dq.shape[0]

    @pl.when(pl.program_id(0) == 0)
    def _():
        flipped[:, :width] = dq[...].T
        flipped[:, width:] = kv_grads(own, left, right).T

    out[...] = dot_nn(flipped[...], weight[...]).astype(BF16)


def back_rows(dq, own, left, right, weight):
    width, rows = dq.shape
    model = weight.shape[1]
    tile = 512
    full = lambda n, m: pl.BlockSpec((n, m), lambda i: (0, 0))
    by_col = lambda n: pl.BlockSpec((n, tile), lambda i: (0, i))
    return pl.pallas_call(
        back_body,
        grid=(model // tile,),
        in_specs=[
            full(width, rows),
            full(2 * width, rows),
            full(2 * width, rows // 2),
            full(2 * width, rows // 2),
            by_col(3 * width),
        ],
        out_specs=by_col(rows),
        out_shape=jax.ShapeDtypeStruct((rows, model), BF16),
        scratch_shapes=[pltpu.VMEM((rows, 3 * width), BF16)],
        compiler_params=params(),
        cost_estimate=pl.CostEstimate(flops=900000000, bytes_accessed=4000000, transcendentals=0),
        name="back",
    )(dq, own, left, right, weight)


def weight_grads_body(core, normed, cot, *rest):
    pieces, (sent, kept, grads, mixed) = rest[:-4], rest[-4:]
    width, frames = pieces[0].shape
    del core

    @pl.when(pl.program_id(0) == 0)
    def _():
        for rec in range(2):
            dq, own, left, right, out = pieces[5 * rec : 5 * rec + 5]
            rows = slice(rec * frames, (rec + 1) * frames)
            stacked = jnp.concatenate([dq[...], kv_grads(own, left, right)], axis=0)
            grads[rows, :] = stacked.T
            mixed[rows, :] = out[...].T

    sums = [dot_nn(normed[...].T, grads[...]), dot_nn(cot[...].T, mixed[...])]

    def write(target):
        for part, offset in zip(sums, (0, 3 * width)):
            shape = (target.shape[0], target.shape[2], part.shape[1])
            cols = slice(offset, offset + part.shape[1])
            target[:, 0, :, cols] = part.reshape(shape).astype(target.dtype)

    @pl.when(pl.program_id(0) < 2)
    def _():
        write(sent)

    @pl.when(pl.program_id(0) >= 2)
    def _():
        write(kept)


def weight_grads(core, normed, cotangent, pieces):
    rows, model = normed.shape
    width = pieces[0].shape[0]
    block = model // 4

    def by_step(i, c):
        return (0, (i % 2) * 2 + jnp.where(i < 2, 1 - c[0], c[0]))

    part = (4, 1, block // 4, 4 * width)
    return pl.pallas_call(
        weight_grads_body,
        grid_spec=pltpu.PrefetchScalarGridSpec(
            num_scalar_prefetch=1,
            grid=(4,),
            in_specs=[pl.BlockSpec((rows, block), by_step)] * 2
            + [pl.BlockSpec(piece.shape, lambda i, c: (0, 0)) for piece in pieces],
            out_specs=[
                pl.BlockSpec(part, lambda i, c: (0, jnp.minimum(i, 1), 0, 0)),
                pl.BlockSpec(part, lambda i, c: (0, jnp.maximum(i, 2) - 2, 0, 0)),
            ],
            scratch_shapes=[
                pltpu.VMEM((rows, 3 * width), BF16),
                pltpu.VMEM((rows, width), BF16),
            ],
        ),
        out_shape=[
            jax.ShapeDtypeStruct((4, 2, block // 4, 4 * width), BF16),
            jax.ShapeDtypeStruct((4, 2, block // 4, 4 * width), BF16),
        ],
        compiler_params=params(),
        cost_estimate=pl.CostEstimate(flops=10000000000, bytes_accessed=12000000, transcendentals=0),
        name="weight_grads",
    )(core, normed, cotangent, *pieces)


def output_body(tok, near, far, *refs):
    weights, (out, stacks) = refs[:4], refs[4:]
    core = lax.axis_index("batch") & 1
    half = weights[0].shape[0] // 4
    total = tok[...].astype(F32)
    for index, weight in enumerate(weights):
        offset = core if index < 2 else 1 - core
        source = (near, far)[index % 2]
        for z in range(4):
            place = pl.multiple_of((2 * z + offset) * half, half)
            stacks[index, z * half : (z + 1) * half, :] = source[pl.ds(place, half), :]
        total = total + dot_nn(stacks[index].T, weight[...])
    out[...] = total.astype(BF16)


def output_rows(tokens, near, far, weights):
    rows, model = tokens.shape
    depth = weights[0].shape[0]
    by_row = pl.BlockSpec((CTX, model), lambda i: (i, 0))
    by_col = pl.BlockSpec((2 * depth, CTX), lambda i: (0, i))
    full = pl.BlockSpec((depth, model), lambda i: (0, 0))
    return pl.pallas_call(
        output_body,
        grid=(rows // CTX,),
        in_specs=[by_row, by_col, by_col] + [full] * 4,
        out_specs=by_row,
        out_shape=jax.ShapeDtypeStruct((rows, model), BF16),
        scratch_shapes=[pltpu.VMEM((4, depth, CTX), BF16)],
        compiler_params=params(28),
        cost_estimate=pl.CostEstimate(flops=1000, bytes_accessed=1000, transcendentals=0),
        name="output",
    )(tokens, near, far, *weights)


def finish_body(place, gain, tok, cot, parts, out):
    back = jnp.sum(parts[...].astype(F32), axis=0)
    scaled, inverse = norm_stats(tok[...])
    weighted = back * gain[...][None, :]
    first = jnp.mean(weighted, axis=-1, keepdims=True)
    second = jnp.mean(weighted * scaled, axis=-1, keepdims=True)
    grad = inverse * (weighted - first - scaled * second) + cot[...].astype(F32)
    out[...] = jnp.broadcast_to(grad.astype(BF16)[None], out.shape)


def finish(place, tokens, cotangent, gain, parts, copies):
    count, chunk, model = parts.shape
    here = pl.BlockSpec((chunk, model), lambda i, p: (p[0], 0))
    whole = lambda n: pl.BlockSpec((n, chunk, model), lambda i, p: (0, 0, 0))
    return pl.pallas_call(
        finish_body,
        grid_spec=pltpu.PrefetchScalarGridSpec(
            num_scalar_prefetch=1,
            grid=(1,),
            in_specs=[pl.BlockSpec((model,), lambda i, p: (0,)), here, here, whole(count)],
            out_specs=whole(copies),
        ),
        out_shape=jax.ShapeDtypeStruct((copies, chunk, model), BF16),
        compiler_params=params(),
        cost_estimate=pl.CostEstimate(flops=10000000, bytes_accessed=3000000, transcendentals=0),
        name="finish",
    )(place, gain, tokens, cotangent, parts)


def assemble_body(places, gathered, *refs):
    pieces, out = refs[:-1], refs[-1]
    chunk = pieces[0].shape[0]
    half = gathered.shape[0]
    out[:half, :] = gathered[...]
    for index, piece in enumerate(pieces):
        place = pl.multiple_of(half + places[index] * chunk, chunk)
        out[pl.ds(place, chunk), :] = piece[...]


def assemble(places, gathered, pieces):
    half, model = gathered.shape
    tile = 512
    by_col = lambda n: pl.BlockSpec((n, tile), lambda i: (0, i))
    return pl.pallas_call(
        assemble_body,
        grid=(model // tile,),
        in_specs=[pl.BlockSpec(memory_space=pltpu.SMEM), by_col(half)]
        + [by_col(piece.shape[0]) for piece in pieces],
        out_specs=by_col(2 * half),
        out_shape=jax.ShapeDtypeStruct((2 * half, model), BF16),
        compiler_params=params(16),
        cost_estimate=pl.CostEstimate(flops=0, bytes_accessed=6000000, transcendentals=0),
        name="assemble",
    )(places, gathered, *pieces)


def to_peer(array, shift):
    dz, dy = shift
    pairs = [
        (z * 2 + y, ((z + dz) % 4) * 2 + (y + dy) % 2) for z in range(4) for y in range(2)
    ]
    return lax.ppermute(array, "chan", pairs)


def peer_index(me, shift, sign):
    dz, dy = shift
    return (((me >> 1) + sign * dz) & 3) * 2 + ((me & 1) ^ dy)


def to_all(array):
    return lax.all_to_all(array, "chan", 0, 0, tiled=True)


def pick(array, index, axis):
    return lax.dynamic_index_in_dim(array, index, axis, keepdims=False)


def core_swap(array):
    return lax.ppermute(array, "batch", [(0, 1), (1, 0), (2, 3), (3, 2)])


def frame_sums(pair):
    frame = lax.axis_index("frames")
    sums = pick(pair, frame, 0)
    for shift in (1, 3, 2):
        sent = pick(pair, (frame + shift) & 3, 0).astype(BF16)
        got = lax.ppermute(sent, "frames", [(i, (i + shift) % 4) for i in range(4)])
        sums = sums + got.astype(F32)
    return sums


def row_sums(sums):
    row = lax.axis_index("batch") >> 1
    sent = pick(sums, 1 - row, 0).astype(BF16)
    got = lax.ppermute(sent, "batch", [(0, 2), (1, 3), (2, 0), (3, 1)])
    return pick(sums, row, 0) + got.astype(F32)


def over_z(array):
    groups = [[0, 2, 4, 6], [1, 3, 5, 7]]
    return lax.all_gather(array, "chan", axis_index_groups=groups, tiled=True)


def shards(tokens, cotangent, norm_gain, norm_bias, qkv_weight, out_weight, lengths, segments):
    recs, frames, model = tokens.shape
    rows = recs * frames
    width = out_weight.shape[0]
    me = lax.axis_index("chan")
    start = lax.axis_index("frames") * frames
    scalar = lambda value: value.reshape(1).astype(jnp.int32)

    weight = qkv_weight.transpose(1, 2, 0).reshape(3 * width, model)
    tie = lax.optimization_barrier
    core = lax.axis_index("batch") & 1
    half_out = lax.dynamic_slice_in_dim(out_weight, core * (width // 2), width // 2, 0)
    near_out = over_z(half_out)

    flat_tokens = tokens.reshape(rows, model)
    flat_cot = cotangent.reshape(rows, model)
    reach = start - CTX + jnp.arange(frames + 2 * CTX, dtype=jnp.int32)
    padded = jnp.pad(segments, ((0, 0), (CTX, CTX)), constant_values=-10)
    seg_keys = lax.dynamic_slice_in_dim(padded, start, frames + 2 * CTX, 1)
    seg_keys = jnp.where(reach[None, :] < lengths[:, None], seg_keys, -10)[:, :, None]
    seg_rows = lax.dynamic_slice_in_dim(segments, start, frames, 1)[:, None, :]

    normed, q, kv, g, kv_first, kv_last, live = project(
        lengths, flat_tokens, flat_cot, norm_gain, norm_bias, weight, out_weight
    )
    size = lax.axis_size("frames")
    up = [(i, i + 1) for i in range(size - 1)]
    down = [(i + 1, i) for i in range(size - 1)]
    before = lax.ppermute(kv_last, "frames", up)
    after = lax.ppermute(kv_first, "frames", down)
    half_out, kv_first = tie((half_out, kv_first))
    peer_out = to_peer(half_out, (0, 1))
    before, after, peer_out = tie((before, after, peer_out))
    far_out = over_z(peer_out)

    results = [None] * recs
    for rec in reversed(range(recs)):
        mixed, dq, dkv, dbefore, dafter = attention(
            rec, q, kv, before, after, g, seg_keys, seg_rows, live
        )
        right = lax.ppermute(dbefore, "frames", down)
        left = lax.ppermute(dafter, "frames", up)
        mixed, q = tie((mixed, q))
        results[rec] = [dq, dkv, left, right, mixed]

    first, second = results
    count = lax.axis_size("chan")
    second[0], _ = tie((second[0], first[0]))

    split = lambda back: back.reshape(count, -1, model)
    second_back = split(back_rows(*second[:4], weight))
    mixed, second_back = tie((jnp.concatenate([first[4], second[4]], axis=1), second_back))
    near_mixed = over_z(mixed)
    peer_mixed = to_peer(mixed, (0, 1))
    first[0], second_back, far_out, near_out = tie((first[0], second_back, far_out, near_out))
    sent, kept = weight_grads(scalar(core), normed, flat_cot, first + second)
    second_parts = to_all(second_back)
    first[0], sent, second_parts = tie((first[0], sent, second_parts))
    first_back = split(back_rows(*first[:4], weight))
    first_back, peer_mixed = tie((first_back, peer_mixed))
    far_mixed = over_z(peer_mixed)
    first_parts = to_all(first_back)

    ending = lambda rec, parts, copies: finish(
        scalar(rec * count + me), flat_tokens, flat_cot, norm_gain, parts, copies
    )
    second_parts, first_back = tie((second_parts, first_back))
    piece = ending(1, second_parts, 1)[0]
    pieces = [to_peer(piece, shift) for shift in SHIFTS]

    pair = core_swap(sent)
    pieces, pair, first_parts = tie((pieces, pair, first_parts))
    copies = ending(0, first_parts, count)
    copies, pair = tie((copies, pair))
    gathered = to_all(copies).reshape(frames, model)
    sums = frame_sums(kept.astype(F32) + pair.astype(F32))
    grad_proj = row_sums(sums).reshape(-1, 4, width)
    own = [near_out, far_out]
    output = output_rows(
        flat_tokens, near_mixed, far_mixed, own + [core_swap(array) for array in own]
    )
    gathered, output = tie((gathered, output))
    places = jnp.stack([me] + [peer_index(me, shift, -1) for shift in SHIFTS]).astype(jnp.int32)
    grad_tokens = assemble(places, gathered, [piece] + pieces)
    shape = (recs, frames, model)
    return (output.reshape(shape), grad_tokens.reshape(shape), grad_proj)


def solution(mesh):
    return jax.shard_map(
        shards,
        mesh=mesh,
        in_specs=(
            P("batch", "frames", None),
            P("batch", "frames", None),
            P(),
            P(),
            P(None, None, "chan"),
            P("chan", None),
            P("batch"),
            P("batch", None),
        ),
        out_specs=(
            P("batch", "frames", None),
            P("batch", "frames", None),
            P(("batch", "frames"), None, "chan"),
        ),
        check_vma=False,
    )
```

```python
import jax
import jax.numpy as jnp
from jax import lax
from jax.experimental import pallas as pl
from jax.experimental.pallas import tpu as pltpu
from jax.sharding import PartitionSpec as P

HEAD = 64
CTX = 256
EPS = 1e-05
NEG = -1e30

SHIFTS = ((2, 1), (2, 0), (3, 1), (1, 1), (0, 1), (3, 0), (1, 0))

F32 = jnp.float32
BF16 = jnp.bfloat16


def params(mebibytes=60):
    return pltpu.CompilerParams(vmem_limit_bytes=mebibytes * 1024 * 1024)


def dot_nn(a, b):
    return lax.dot_general(a, b, (((1,), (0,)), ((), ())), preferred_element_type=F32)


def dot_nt(a, b):
    return lax.dot_general(a, b, (((1,), (1,)), ((), ())), preferred_element_type=F32)


def dot_tn(a, b):
    return lax.dot_general(a, b, (((0,), (0,)), ((), ())), preferred_element_type=F32)


def norm_stats(tokens):
    values = tokens.astype(F32)
    centered = values - jnp.mean(values, axis=-1, keepdims=True)
    inverse = lax.rsqrt(jnp.mean(centered * centered, axis=-1, keepdims=True) + EPS)
    return centered * inverse, inverse


def project_body(
    lengths, tok, cot, gain, bias, weight, out_w, normed, q, kv, g, kv_first, kv_last, live
):
    width = q.shape[0]
    scaled, _ = norm_stats(tok[...])
    rows = (scaled * gain[...][None, :] + bias[...][None, :]).astype(BF16)
    normed[...] = rows
    qkv = dot_nt(weight[...], rows).astype(BF16)
    q[...] = qkv[:width]
    kv[...] = qkv[width:]
    step = pl.program_id(0)

    @pl.when(step % 2 == 0)
    def _():
        kv_first[...] = qkv[width:]

    @pl.when(step % 2 == 1)
    def _():
        kv_last[...] = qkv[width:]

    start = lax.axis_index("frames") * (2 * CTX) + (step % 2) * CTX
    position = start + lax.broadcasted_iota(jnp.int32, (1, CTX), 1)
    alive = jnp.where(position < lengths[step // 2], 1.0, 0.0)
    live[...] = alive
    g[...] = (dot_nt(out_w[...], cot[...]) * alive).astype(BF16)


def project(lengths, tokens, cotangent, gain, bias, weight, out_w):
    rows, model = tokens.shape
    width = out_w.shape[0]
    full = lambda shape: pl.BlockSpec(shape, lambda i: (0,) * len(shape))
    by_row = pl.BlockSpec((CTX, model), lambda i: (i, 0))
    by_col = lambda n: pl.BlockSpec((n, CTX), lambda i: (0, i))
    by_half = pl.BlockSpec((2 * width, CTX), lambda i: (0, i // 2))
    return pl.pallas_call(
        project_body,
        grid=(rows // CTX,),
        in_specs=[
            pl.BlockSpec(memory_space=pltpu.SMEM),
            by_row,
            by_row,
            full((model,)),
            full((model,)),
            full((3 * width, model)),
            full((width, model)),
        ],
        out_specs=[
            by_row,
            by_col(width),
            by_col(2 * width),
            by_col(width),
            by_half,
            by_half,
            by_col(1),
        ],
        out_shape=[
            jax.ShapeDtypeStruct((rows, model), BF16),
            jax.ShapeDtypeStruct((width, rows), BF16),
            jax.ShapeDtypeStruct((2 * width, rows), BF16),
            jax.ShapeDtypeStruct((width, rows), BF16),
            jax.ShapeDtypeStruct((2 * width, rows // 2), BF16),
            jax.ShapeDtypeStruct((2 * width, rows // 2), BF16),
            jax.ShapeDtypeStruct((1, rows), F32),
        ],
        compiler_params=params(),
        cost_estimate=pl.CostEstimate(flops=2400000000, bytes_accessed=15000000, transcendentals=0),
        name="project",
    )(lengths, tokens, cotangent, gain, bias, weight, out_w)


def attention_body(q, kv, before, after, g, seg_keys, seg_rows, live, *refs):
    mixed, dq, dkv, dbefore, dafter, acc, mask = refs[-7:]
    if len(refs) > 7:
        mixed[:, q.shape[1] :] = refs[0][...]
    width = q.shape[0]
    span = 3 * CTX
    kv_all = jnp.concatenate([before[...], kv[...], after[...]], axis=1)
    q_small = q[...] * jnp.asarray(HEAD**-0.5, BF16)
    grads = g[...]
    acc[...] = jnp.zeros_like(acc)
    for tile in range(2):
        cols = slice(tile * CTX, (tile + 1) * CTX)
        keys = slice(tile * CTX, tile * CTX + span)
        away = (
            lax.broadcasted_iota(jnp.int32, (span, CTX), 0)
            - CTX
            - lax.broadcasted_iota(jnp.int32, (span, CTX), 1)
        )
        near = jnp.abs(away) <= CTX
        stretch = jnp.abs(seg_keys[0, keys, :] - seg_rows[0, :, cols]) <= 1
        visible = (near & stretch) | (away == 0)
        mask[...] = jnp.where(visible, 0.0, NEG)
        for head in range(width // HEAD):
            d = slice(head * HEAD, (head + 1) * HEAD)
            dv = slice(width + head * HEAD, width + (head + 1) * HEAD)
            k_t, v_t = kv_all[d, keys], kv_all[dv, keys]
            q_t, g_t = q_small[d, cols], grads[d, cols]
            scores = dot_tn(k_t, q_t) + mask[...]
            weights = jnp.exp(scores - jnp.max(scores, axis=0, keepdims=True))
            weights = weights * (1.0 / jnp.sum(weights, axis=0, keepdims=True))
            rounded = weights.astype(BF16)
            mixed[d, cols] = (dot_nn(v_t, rounded) * live[:, cols]).astype(BF16)
            grad_w = dot_tn(v_t, g_t)
            total = jnp.sum(weights * grad_w, axis=0, keepdims=True)
            grad_s = (weights * (grad_w - total)).astype(BF16)
            dq[d, cols] = (dot_nn(k_t, grad_s) * (HEAD**-0.5)).astype(BF16)
            acc[d, keys] += dot_nt(q_t, grad_s)
            acc[dv, keys] += dot_nt(g_t, rounded)
    frames = q.shape[1]
    dkv[...] = acc[:, CTX : CTX + frames]
    dbefore[...] = acc[:, :CTX].astype(BF16)
    dafter[...] = acc[:, CTX + frames :].astype(BF16)


def attention(rec, q, kv, before, after, g, seg_keys, seg_rows, live, *later):
    width, rows = q.shape
    recs, span, _ = seg_keys.shape
    frames = rows // recs
    by_rec = lambda n, m: pl.BlockSpec((n, m), lambda i: (0, rec))
    whole = lambda n, m: pl.BlockSpec((n, m), lambda i: (0, 0))
    return pl.pallas_call(
        attention_body,
        grid=(1,),
        in_specs=[
            by_rec(width, frames),
            by_rec(2 * width, frames),
            by_rec(2 * width, CTX),
            by_rec(2 * width, CTX),
            by_rec(width, frames),
            pl.BlockSpec((1, span, 1), lambda i: (rec, 0, 0)),
            pl.BlockSpec((1, 1, frames), lambda i: (rec, 0, 0)),
            by_rec(1, frames),
        ]
        + [whole(width, frames)] * len(later),
        out_specs=[
            whole(width, frames * (1 + len(later))),
            whole(width, frames),
            whole(2 * width, frames),
            whole(2 * width, CTX),
            whole(2 * width, CTX),
        ],
        out_shape=[
            jax.ShapeDtypeStruct((width, frames * (1 + len(later))), BF16),
            jax.ShapeDtypeStruct((width, frames), BF16),
            jax.ShapeDtypeStruct((2 * width, frames), F32),
            jax.ShapeDtypeStruct((2 * width, CTX), BF16),
            jax.ShapeDtypeStruct((2 * width, CTX), BF16),
        ],
        scratch_shapes=[pltpu.VMEM((2 * width, span), F32), pltpu.VMEM((3 * CTX, CTX), F32)],
        compiler_params=params(),
        cost_estimate=pl.CostEstimate(flops=1000, bytes_accessed=1000, transcendentals=0),
        name="attention",
    )(q, kv, before, after, g, seg_keys, seg_rows, live, *later)


def kv_grads(own, left, right):
    beside = jnp.concatenate([left[...], right[...]], axis=1).astype(F32)
    return (own[...] + beside).astype(BF16)


def back_body(dq, own, left, right, weight, out, flipped):
    width = dq.shape[0]

    @pl.when(pl.program_id(0) == 0)
    def _():
        flipped[:, :width] = dq[...].T
        flipped[:, width:] = kv_grads(own, left, right).T

    out[...] = dot_nn(flipped[...], weight[...]).astype(BF16)


def back_rows(dq, own, left, right, weight):
    width, rows = dq.shape
    model = weight.shape[1]
    tile = 512
    full = lambda n, m: pl.BlockSpec((n, m), lambda i: (0, 0))
    by_col = lambda n: pl.BlockSpec((n, tile), lambda i: (0, i))
    return pl.pallas_call(
        back_body,
        grid=(model // tile,),
        in_specs=[
            full(width, rows),
            full(2 * width, rows),
            full(2 * width, rows // 2),
            full(2 * width, rows // 2),
            by_col(3 * width),
        ],
        out_specs=by_col(rows),
        out_shape=jax.ShapeDtypeStruct((rows, model), BF16),
        scratch_shapes=[pltpu.VMEM((rows, 3 * width), BF16)],
        compiler_params=params(),
        cost_estimate=pl.CostEstimate(flops=900000000, bytes_accessed=4000000, transcendentals=0),
        name="back",
    )(dq, own, left, right, weight)


def weight_grads_body(core, normed, cot, *rest):
    pieces, (sent, kept, grads, mixed) = rest[:-4], rest[-4:]
    width, frames = pieces[0].shape
    del core

    @pl.when(pl.program_id(0) == 0)
    def _():
        for rec in range(2):
            dq, own, left, right = pieces[4 * rec : 4 * rec + 4]
            rows = slice(rec * frames, (rec + 1) * frames)
            stacked = jnp.concatenate([dq[...], kv_grads(own, left, right)], axis=0)
            grads[rows, :] = stacked.T
            mixed[rows, :] = pieces[-1][:, rows].T

    sums = [dot_nn(normed[...].T, grads[...]), dot_nn(cot[...].T, mixed[...])]

    def write(target):
        for part, offset in zip(sums, (0, 3 * width)):
            shape = (target.shape[0], target.shape[2], part.shape[1])
            cols = slice(offset, offset + part.shape[1])
            target[:, 0, :, cols] = part.reshape(shape).astype(target.dtype)

    @pl.when(pl.program_id(0) < 2)
    def _():
        write(sent)

    @pl.when(pl.program_id(0) >= 2)
    def _():
        write(kept)


def weight_grads(core, normed, cotangent, pieces):
    rows, model = normed.shape
    width = pieces[0].shape[0]
    block = model // 4

    def by_step(i, c):
        return (0, (i % 2) * 2 + jnp.where(i < 2, 1 - c[0], c[0]))

    part = (4, 1, block // 4, 4 * width)
    return pl.pallas_call(
        weight_grads_body,
        grid_spec=pltpu.PrefetchScalarGridSpec(
            num_scalar_prefetch=1,
            grid=(4,),
            in_specs=[pl.BlockSpec((rows, block), by_step)] * 2
            + [pl.BlockSpec(piece.shape, lambda i, c: (0, 0)) for piece in pieces],
            out_specs=[
                pl.BlockSpec(part, lambda i, c: (0, jnp.minimum(i, 1), 0, 0)),
                pl.BlockSpec(part, lambda i, c: (0, jnp.maximum(i, 2) - 2, 0, 0)),
            ],
            scratch_shapes=[
                pltpu.VMEM((rows, 3 * width), BF16),
                pltpu.VMEM((rows, width), BF16),
            ],
        ),
        out_shape=[
            jax.ShapeDtypeStruct((4, 2, block // 4, 4 * width), BF16),
            jax.ShapeDtypeStruct((4, 2, block // 4, 4 * width), BF16),
        ],
        compiler_params=params(),
        cost_estimate=pl.CostEstimate(flops=10000000000, bytes_accessed=12000000, transcendentals=0),
        name="weight_grads",
    )(core, normed, cotangent, *pieces)


def output_body(tok, near, far, near_weight, far_weight, out):
    total = dot_nn(near[...].T, near_weight[...]) + dot_nn(far[...].T, far_weight[...])
    out[...] = (tok[...].astype(F32) + total).astype(BF16)


def output_rows(tokens, near, far, near_weight, far_weight):
    rows, model = tokens.shape
    depth = near.shape[0]
    block = 2 * CTX
    by_row = pl.BlockSpec((block, model), lambda i: (i, 0))
    by_col = pl.BlockSpec((depth, block), lambda i: (0, i))
    full = pl.BlockSpec((depth, model), lambda i: (0, 0))
    return pl.pallas_call(
        output_body,
        grid=(rows // block,),
        in_specs=[by_row, by_col, by_col, full, full],
        out_specs=by_row,
        out_shape=jax.ShapeDtypeStruct((rows, model), BF16),
        compiler_params=params(),
        cost_estimate=pl.CostEstimate(
            flops=10000000000, bytes_accessed=12000000, transcendentals=0
        ),
        name="output",
    )(tokens, near, far, near_weight, far_weight)


def finish_body(place, gain, tok, cot, parts, *refs):
    out = refs[-1]
    chunk = tok.shape[0]
    back = jnp.sum(parts[...].astype(F32), axis=0)
    scaled, inverse = norm_stats(tok[...])
    weighted = back * gain[...][None, :]
    first = jnp.mean(weighted, axis=-1, keepdims=True)
    second = jnp.mean(weighted * scaled, axis=-1, keepdims=True)
    grad = inverse * (weighted - first - scaled * second) + cot[...].astype(F32)
    out[:chunk, :] = grad.astype(BF16)
    if len(refs) > 1:
        out[chunk:, :] = refs[0][...]


def finish(place, tokens, cotangent, gain, parts, *later):
    count, chunk, model = parts.shape
    here = pl.BlockSpec((chunk, model), lambda i, p: (p[0], 0))
    whole = lambda n: pl.BlockSpec((n, model), lambda i, p: (0, 0))
    rows = chunk * (1 + len(later))
    return pl.pallas_call(
        finish_body,
        grid_spec=pltpu.PrefetchScalarGridSpec(
            num_scalar_prefetch=1,
            grid=(1,),
            in_specs=[
                pl.BlockSpec((model,), lambda i, p: (0,)),
                here,
                here,
                pl.BlockSpec((count, chunk, model), lambda i, p: (0, 0, 0)),
            ]
            + [whole(chunk)] * len(later),
            out_specs=whole(rows),
        ),
        out_shape=jax.ShapeDtypeStruct((rows, model), BF16),
        compiler_params=params(),
        cost_estimate=pl.CostEstimate(flops=10000000, bytes_accessed=3000000, transcendentals=0),
        name="finish",
    )(place, gain, tokens, cotangent, parts, *later)


def assemble_body(places, *refs):
    pieces, out = refs[:-1], refs[-1]
    chunk = pieces[0].shape[0] // 2
    half = out.shape[0] // 2
    for index, piece in enumerate(pieces):
        for rec in range(2):
            place = pl.multiple_of(rec * half + places[index] * chunk, chunk)
            out[pl.ds(place, chunk), :] = piece[rec * chunk : (rec + 1) * chunk, :]


def assemble(places, pieces):
    chunk, model = pieces[0].shape
    count = len(pieces)
    tile = 512
    by_col = lambda n: pl.BlockSpec((n, tile), lambda i: (0, i))
    return pl.pallas_call(
        assemble_body,
        grid=(model // tile,),
        in_specs=[pl.BlockSpec(memory_space=pltpu.SMEM)] + [by_col(chunk)] * count,
        out_specs=by_col(count * chunk),
        out_shape=jax.ShapeDtypeStruct((count * chunk, model), BF16),
        compiler_params=params(16),
        cost_estimate=pl.CostEstimate(flops=0, bytes_accessed=6000000, transcendentals=0),
        name="assemble",
    )(places, *pieces)


def to_peer(array, shift):
    dz, dy = shift
    pairs = [
        (z * 2 + y, ((z + dz) % 4) * 2 + (y + dy) % 2) for z in range(4) for y in range(2)
    ]
    return lax.ppermute(array, "chan", pairs)


def peer_index(me, shift, sign):
    dz, dy = shift
    return (((me >> 1) + sign * dz) & 3) * 2 + ((me & 1) ^ dy)


def to_all(array):
    return lax.all_to_all(array, "chan", 0, 0, tiled=True)


def pick(array, index, axis):
    return lax.dynamic_index_in_dim(array, index, axis, keepdims=False)


def core_swap(array):
    return lax.ppermute(array, "batch", [(0, 1), (1, 0), (2, 3), (3, 2)])


def frame_sums(pair):
    frame = lax.axis_index("frames")
    sums = pick(pair, frame, 0)
    for shift in (1, 3, 2):
        sent = pick(pair, (frame + shift) & 3, 0).astype(BF16)
        got = lax.ppermute(sent, "frames", [(i, (i + shift) % 4) for i in range(4)])
        sums = sums + got.astype(F32)
    return sums


def row_sums(sums):
    row = lax.axis_index("batch") >> 1
    sent = pick(sums, 1 - row, 0).astype(BF16)
    got = lax.ppermute(sent, "batch", [(0, 2), (1, 3), (2, 0), (3, 1)])
    return pick(sums, row, 0), got


def over_z(array):
    groups = [[0, 2, 4, 6], [1, 3, 5, 7]]
    return lax.all_gather(array, "chan", axis_index_groups=groups, tiled=True)


def shards(tokens, cotangent, norm_gain, norm_bias, qkv_weight, out_weight, lengths, segments):
    recs, frames, model = tokens.shape
    rows = recs * frames
    width = out_weight.shape[0]
    me = lax.axis_index("chan")
    start = lax.axis_index("frames") * frames
    scalar = lambda value: value.reshape(1).astype(jnp.int32)

    weight = qkv_weight.transpose(1, 2, 0).reshape(3 * width, model)
    tie = lax.optimization_barrier
    core = lax.axis_index("batch") & 1
    near_out = over_z(out_weight)

    flat_tokens = tokens.reshape(rows, model)
    flat_cot = cotangent.reshape(rows, model)
    reach = start - CTX + jnp.arange(frames + 2 * CTX, dtype=jnp.int32)
    padded = jnp.pad(segments, ((0, 0), (CTX, CTX)), constant_values=-10)
    seg_keys = lax.dynamic_slice_in_dim(padded, start, frames + 2 * CTX, 1)
    seg_keys = jnp.where(reach[None, :] < lengths[:, None], seg_keys, -10)[:, :, None]
    seg_rows = lax.dynamic_slice_in_dim(segments, start, frames, 1)[:, None, :]

    normed, q, kv, g, kv_first, kv_last, live = project(
        lengths, flat_tokens, flat_cot, norm_gain, norm_bias, weight, out_weight
    )
    size = lax.axis_size("frames")
    up = [(i, i + 1) for i in range(size - 1)]
    down = [(i + 1, i) for i in range(size - 1)]
    before = lax.ppermute(kv_last, "frames", up)
    after = lax.ppermute(kv_first, "frames", down)
    late_out, _ = tie((out_weight, kv_first))
    peer_out = to_peer(late_out, (0, 1))
    before, after, peer_out = tie((before, after, peer_out))
    far_out = over_z(peer_out)

    results, mixed = [None] * recs, []
    for rec in reversed(range(recs)):
        out, dq, dkv, dbefore, dafter = attention(
            rec, q, kv, before, after, g, seg_keys, seg_rows, live, *mixed
        )
        right = lax.ppermute(dbefore, "frames", down)
        left = lax.ppermute(dafter, "frames", up)
        mixed = [out]
        results[rec] = [dq, dkv, left, right]

    first, second = results
    count = lax.axis_size("chan")
    second[0], _ = tie((second[0], first[0]))

    split = lambda back: back.reshape(count, -1, model)
    second_back = split(back_rows(*second[:4], weight))
    mixed, second_back = tie((mixed[0], second_back))
    near_mixed = over_z(mixed)
    peer_mixed = to_peer(mixed, (0, 1))
    first[0], second_back, near_out = tie((first[0], second_back, near_out))
    sent, kept = weight_grads(scalar(core), normed, flat_cot, first + second + [mixed])
    second_parts = to_all(second_back)
    first[0], sent, second_parts, far_out = tie((first[0], sent, second_parts, far_out))
    first_back = split(back_rows(*first[:4], weight))
    first_back, peer_mixed = tie((first_back, peer_mixed))
    far_mixed = over_z(peer_mixed)
    first_parts = to_all(first_back)

    ending = lambda rec, *refs: finish(
        scalar(rec * count + me), flat_tokens, flat_cot, norm_gain, *refs
    )
    second_parts, first_back = tie((second_parts, first_back))
    piece = ending(1, second_parts)
    sums = frame_sums(kept.astype(F32) + core_swap(sent).astype(F32))
    sums, first_parts = tie((sums, first_parts))
    piece = ending(0, first_parts, piece)
    pieces = [to_peer(piece, shift) for shift in SHIFTS]
    output = output_rows(flat_tokens, near_mixed, far_mixed, near_out, far_out)
    pieces[0], output = tie((pieces[0], output))
    places = jnp.stack([me] + [peer_index(me, shift, -1) for shift in SHIFTS]).astype(jnp.int32)
    grad_tokens = assemble(places, [piece] + pieces)
    sums, output = tie((sums, output))
    own_sums, got_sums = row_sums(sums)
    grad_proj = (own_sums + got_sums.astype(F32)).reshape(-1, 4, width)
    shape = (recs, frames, model)
    return (output.reshape(shape), grad_tokens.reshape(shape), grad_proj)


def solution(mesh):
    return jax.shard_map(
        shards,
        mesh=mesh,
        in_specs=(
            P("batch", "frames", None),
            P("batch", "frames", None),
            P(),
            P(),
            P(None, None, "chan"),
            P("chan", None),
            P("batch"),
            P("batch", None),
        ),
        out_specs=(
            P("batch", "frames", None),
            P("batch", "frames", None),
            P(("batch", "frames"), None, "chan"),
        ),
        check_vma=False,
    )
```

```python
import jax
import jax.numpy as jnp
from jax import lax
from jax.experimental import pallas as pl
from jax.experimental.pallas import tpu as pltpu
from jax.sharding import PartitionSpec as P

HEAD = 64
CTX = 256
EPS = 1e-05
NEG = -1e30

SHIFTS = ((2, 1), (2, 0), (3, 1), (1, 1), (0, 1), (3, 0), (1, 0))

F32 = jnp.float32
BF16 = jnp.bfloat16


def params(mebibytes=60):
    return pltpu.CompilerParams(vmem_limit_bytes=mebibytes * 1024 * 1024)


def dot_nn(a, b):
    return lax.dot_general(a, b, (((1,), (0,)), ((), ())), preferred_element_type=F32)


def dot_nt(a, b):
    return lax.dot_general(a, b, (((1,), (1,)), ((), ())), preferred_element_type=F32)


def dot_tn(a, b):
    return lax.dot_general(a, b, (((0,), (0,)), ((), ())), preferred_element_type=F32)


def norm_stats(tokens):
    values = tokens.astype(F32)
    centered = values - jnp.mean(values, axis=-1, keepdims=True)
    inverse = lax.rsqrt(jnp.mean(centered * centered, axis=-1, keepdims=True) + EPS)
    return centered * inverse, inverse


def project_body(
    lengths, tok, cot, gain, bias, weight, out_w, normed, q, kv, g, kv_first, kv_last, live
):
    width = q.shape[0]
    scaled, _ = norm_stats(tok[...])
    rows = (scaled * gain[...][None, :] + bias[...][None, :]).astype(BF16)
    normed[...] = rows
    qkv = dot_nt(weight[...], rows).astype(BF16)
    q[...] = qkv[:width]
    kv[...] = qkv[width:]
    kv_first[...] = qkv[width:, :CTX]
    kv_last[...] = qkv[width:, CTX:]
    rec, frames = pl.program_id(0), tok.shape[0]
    start = lax.axis_index("frames") * frames
    position = start + lax.broadcasted_iota(jnp.int32, (1, frames), 1)
    alive = jnp.where(position < lengths[rec], 1.0, 0.0)
    live[...] = alive
    g[...] = (dot_nt(out_w[...], cot[...]) * alive).astype(BF16)


def project(lengths, tokens, cotangent, gain, bias, weight, out_w):
    rows, model = tokens.shape
    width = out_w.shape[0]
    full = lambda shape: pl.BlockSpec(shape, lambda i: (0,) * len(shape))
    frames = 2 * CTX
    by_row = pl.BlockSpec((frames, model), lambda i: (i, 0))
    by_col = lambda n: pl.BlockSpec((n, frames), lambda i: (0, i))
    by_half = pl.BlockSpec((2 * width, CTX), lambda i: (0, i))
    return pl.pallas_call(
        project_body,
        grid=(rows // frames,),
        in_specs=[
            pl.BlockSpec(memory_space=pltpu.SMEM),
            by_row,
            by_row,
            full((model,)),
            full((model,)),
            full((3 * width, model)),
            full((width, model)),
        ],
        out_specs=[
            by_row,
            by_col(width),
            by_col(2 * width),
            by_col(width),
            by_half,
            by_half,
            by_col(1),
        ],
        out_shape=[
            jax.ShapeDtypeStruct((rows, model), BF16),
            jax.ShapeDtypeStruct((width, rows), BF16),
            jax.ShapeDtypeStruct((2 * width, rows), BF16),
            jax.ShapeDtypeStruct((width, rows), BF16),
            jax.ShapeDtypeStruct((2 * width, rows // 2), BF16),
            jax.ShapeDtypeStruct((2 * width, rows // 2), BF16),
            jax.ShapeDtypeStruct((1, rows), F32),
        ],
        compiler_params=params(),
        cost_estimate=pl.CostEstimate(flops=2400000000, bytes_accessed=15000000, transcendentals=0),
        name="project",
    )(lengths, tokens, cotangent, gain, bias, weight, out_w)


def attention_body(q, kv, before, after, g, seg_keys, seg_rows, live, *refs):
    mixed, dq, dkv, dbefore, dafter, acc, mask = refs[-7:]
    if len(refs) > 7:
        mixed[:, q.shape[1] :] = refs[0][...]
    width = q.shape[0]
    span = 3 * CTX
    kv_all = jnp.concatenate([before[...], kv[...], after[...]], axis=1)
    q_small = q[...] * jnp.asarray(HEAD**-0.5, BF16)
    grads = g[...]
    acc[...] = jnp.zeros_like(acc)
    seg_column = jnp.broadcast_to(seg_keys[0], (128, acc.shape[1])).T[:, :1]
    for tile in range(2):
        cols = slice(tile * CTX, (tile + 1) * CTX)
        keys = slice(tile * CTX, tile * CTX + span)
        away = (
            lax.broadcasted_iota(jnp.int32, (span, CTX), 0)
            - CTX
            - lax.broadcasted_iota(jnp.int32, (span, CTX), 1)
        )
        near = jnp.abs(away) <= CTX
        stretch = jnp.abs(seg_column[keys, :] - seg_rows[0, :, cols]) <= 1.0
        visible = (near & stretch) | (away == 0)
        mask[...] = jnp.where(visible, 0.0, NEG)
        for head in range(width // HEAD):
            d = slice(head * HEAD, (head + 1) * HEAD)
            dv = slice(width + head * HEAD, width + (head + 1) * HEAD)
            k_t, v_t = kv_all[d, keys], kv_all[dv, keys]
            q_t, g_t = q_small[d, cols], grads[d, cols]
            scores = dot_tn(k_t, q_t) + mask[...]
            weights = jnp.exp(scores - jnp.max(scores, axis=0, keepdims=True))
            weights = weights * (1.0 / jnp.sum(weights, axis=0, keepdims=True))
            rounded = weights.astype(BF16)
            out = dot_nn(v_t, rounded)
            mixed[d, cols] = (out * live[:, cols]).astype(BF16)
            grad_w = dot_tn(v_t, g_t)
            total = jnp.sum(out * g_t.astype(F32), axis=0, keepdims=True)
            grad_s = (weights * (grad_w - total)).astype(BF16)
            dq[d, cols] = (dot_nn(k_t, grad_s) * (HEAD**-0.5)).astype(BF16)
            acc[d, keys] += dot_nt(q_t, grad_s)
            acc[dv, keys] += dot_nt(g_t, rounded)
    frames = q.shape[1]
    dkv[...] = acc[:, CTX : CTX + frames]
    dbefore[...] = acc[:, :CTX].astype(BF16)
    dafter[...] = acc[:, CTX + frames :].astype(BF16)


def attention(rec, q, kv, before, after, g, seg_keys, seg_rows, live, *later):
    width, rows = q.shape
    recs, _, span = seg_keys.shape
    frames = rows // recs
    by_rec = lambda n, m: pl.BlockSpec((n, m), lambda i: (0, rec))
    whole = lambda n, m: pl.BlockSpec((n, m), lambda i: (0, 0))
    return pl.pallas_call(
        attention_body,
        grid=(1,),
        in_specs=[
            by_rec(width, frames),
            by_rec(2 * width, frames),
            by_rec(2 * width, CTX),
            by_rec(2 * width, CTX),
            by_rec(width, frames),
            pl.BlockSpec((1, 1, span), lambda i: (rec, 0, 0)),
            pl.BlockSpec((1, 1, frames), lambda i: (rec, 0, 0)),
            by_rec(1, frames),
        ]
        + [whole(width, frames)] * len(later),
        out_specs=[
            whole(width, frames * (1 + len(later))),
            whole(width, frames),
            whole(2 * width, frames),
            whole(2 * width, CTX),
            whole(2 * width, CTX),
        ],
        out_shape=[
            jax.ShapeDtypeStruct((width, frames * (1 + len(later))), BF16),
            jax.ShapeDtypeStruct((width, frames), BF16),
            jax.ShapeDtypeStruct((2 * width, frames), F32),
            jax.ShapeDtypeStruct((2 * width, CTX), BF16),
            jax.ShapeDtypeStruct((2 * width, CTX), BF16),
        ],
        scratch_shapes=[pltpu.VMEM((2 * width, span), F32), pltpu.VMEM((3 * CTX, CTX), F32)],
        compiler_params=params(),
        cost_estimate=pl.CostEstimate(flops=1000, bytes_accessed=1000, transcendentals=0),
        name="attention",
    )(q, kv, before, after, g, seg_keys, seg_rows, live, *later)


def kv_grads(own, left, right):
    beside = jnp.concatenate([left[...], right[...]], axis=1).astype(F32)
    return (own[...] + beside).astype(BF16)


def back_body(dq, own, left, right, weight, out, flipped):
    width = dq.shape[0]

    @pl.when(pl.program_id(0) == 0)
    def _():
        flipped[:, :width] = dq[...].T
        flipped[:, width:] = kv_grads(own, left, right).T

    out[...] = dot_nn(flipped[...], weight[...]).astype(BF16)


def back_rows(dq, own, left, right, weight):
    width, rows = dq.shape
    model = weight.shape[1]
    tile = 512
    full = lambda n, m: pl.BlockSpec((n, m), lambda i: (0, 0))
    by_col = lambda n: pl.BlockSpec((n, tile), lambda i: (0, i))
    return pl.pallas_call(
        back_body,
        grid=(model // tile,),
        in_specs=[
            full(width, rows),
            full(2 * width, rows),
            full(2 * width, rows // 2),
            full(2 * width, rows // 2),
            by_col(3 * width),
        ],
        out_specs=by_col(rows),
        out_shape=jax.ShapeDtypeStruct((rows, model), BF16),
        scratch_shapes=[pltpu.VMEM((rows, 3 * width), BF16)],
        compiler_params=params(),
        cost_estimate=pl.CostEstimate(flops=900000000, bytes_accessed=4000000, transcendentals=0),
        name="back",
    )(dq, own, left, right, weight)


def weight_grads_body(core, normed, cot, *rest):
    pieces, (sent, kept, grads, mixed) = rest[:-4], rest[-4:]
    width, frames = pieces[0].shape
    del core

    @pl.when(pl.program_id(0) == 0)
    def _():
        for rec in range(2):
            dq, own, left, right = pieces[4 * rec : 4 * rec + 4]
            rows = slice(rec * frames, (rec + 1) * frames)
            stacked = jnp.concatenate([dq[...], kv_grads(own, left, right)], axis=0)
            grads[rows, :] = stacked.T
            mixed[rows, :] = pieces[-1][:, rows].T

    sums = [dot_nn(normed[...].T, grads[...]), dot_nn(cot[...].T, mixed[...])]

    def write(target):
        for part, offset in zip(sums, (0, 3 * width)):
            shape = (target.shape[0], target.shape[2], part.shape[1])
            cols = slice(offset, offset + part.shape[1])
            target[:, 0, :, cols] = part.reshape(shape).astype(target.dtype)

    @pl.when(pl.program_id(0) < 2)
    def _():
        write(sent)

    @pl.when(pl.program_id(0) >= 2)
    def _():
        write(kept)


def weight_grads(core, normed, cotangent, pieces):
    rows, model = normed.shape
    width = pieces[0].shape[0]
    block = model // 4

    def by_step(i, c):
        return (0, (i % 2) * 2 + jnp.where(i < 2, 1 - c[0], c[0]))

    part = (4, 1, block // 4, 4 * width)
    return pl.pallas_call(
        weight_grads_body,
        grid_spec=pltpu.PrefetchScalarGridSpec(
            num_scalar_prefetch=1,
            grid=(4,),
            in_specs=[pl.BlockSpec((rows, block), by_step)] * 2
            + [pl.BlockSpec(piece.shape, lambda i, c: (0, 0)) for piece in pieces],
            out_specs=[
                pl.BlockSpec(part, lambda i, c: (0, jnp.minimum(i, 1), 0, 0)),
                pl.BlockSpec(part, lambda i, c: (0, jnp.maximum(i, 2) - 2, 0, 0)),
            ],
            scratch_shapes=[
                pltpu.VMEM((rows, 3 * width), BF16),
                pltpu.VMEM((rows, width), BF16),
            ],
        ),
        out_shape=[
            jax.ShapeDtypeStruct((4, 2, block // 4, 4 * width), BF16),
            jax.ShapeDtypeStruct((4, 2, block // 4, 4 * width), BF16),
        ],
        compiler_params=params(),
        cost_estimate=pl.CostEstimate(flops=10000000000, bytes_accessed=12000000, transcendentals=0),
        name="weight_grads",
    )(core, normed, cotangent, *pieces)


def output_body(tok, near, far, near_weight, far_weight, out):
    total = dot_nn(near[...].T, near_weight[...]) + dot_nn(far[...].T, far_weight[...])
    out[...] = (tok[...].astype(F32) + total).astype(BF16)


def output_rows(tokens, near, far, near_weight, far_weight):
    rows, model = tokens.shape
    depth = near.shape[0]
    block = 2 * CTX
    by_row = pl.BlockSpec((block, model), lambda i: (i, 0))
    by_col = pl.BlockSpec((depth, block), lambda i: (0, i))
    full = pl.BlockSpec((depth, model), lambda i: (0, 0))
    return pl.pallas_call(
        output_body,
        grid=(rows // block,),
        in_specs=[by_row, by_col, by_col, full, full],
        out_specs=by_row,
        out_shape=jax.ShapeDtypeStruct((rows, model), BF16),
        compiler_params=params(),
        cost_estimate=pl.CostEstimate(
            flops=10000000000, bytes_accessed=12000000, transcendentals=0
        ),
        name="output",
    )(tokens, near, far, near_weight, far_weight)


def finish_body(place, gain, tok, cot, parts, *refs):
    out = refs[-1]
    chunk = tok.shape[0]
    back = jnp.sum(parts[...].astype(F32), axis=0)
    scaled, inverse = norm_stats(tok[...])
    weighted = back * gain[...][None, :]
    first = jnp.mean(weighted, axis=-1, keepdims=True)
    second = jnp.mean(weighted * scaled, axis=-1, keepdims=True)
    grad = inverse * (weighted - first - scaled * second) + cot[...].astype(F32)
    out[:chunk, :] = grad.astype(BF16)
    if len(refs) > 1:
        out[chunk:, :] = refs[0][...]


def finish(place, tokens, cotangent, gain, parts, *later):
    count, chunk, model = parts.shape
    here = pl.BlockSpec((chunk, model), lambda i, p: (p[0], 0))
    whole = lambda n: pl.BlockSpec((n, model), lambda i, p: (0, 0))
    rows = chunk * (1 + len(later))
    return pl.pallas_call(
        finish_body,
        grid_spec=pltpu.PrefetchScalarGridSpec(
            num_scalar_prefetch=1,
            grid=(1,),
            in_specs=[
                pl.BlockSpec((model,), lambda i, p: (0,)),
                here,
                here,
                pl.BlockSpec((count, chunk, model), lambda i, p: (0, 0, 0)),
            ]
            + [whole(chunk)] * len(later),
            out_specs=whole(rows),
        ),
        out_shape=jax.ShapeDtypeStruct((rows, model), BF16),
        compiler_params=params(),
        cost_estimate=pl.CostEstimate(flops=10000000, bytes_accessed=3000000, transcendentals=0),
        name="finish",
    )(place, gain, tokens, cotangent, parts, *later)


def assemble_body(places, *refs):
    pieces, out = refs[:-1], refs[-1]
    chunk = pieces[0].shape[0] // 2
    half = out.shape[0] // 2
    for index, piece in enumerate(pieces):
        for rec in range(2):
            place = pl.multiple_of(rec * half + places[index] * chunk, chunk)
            out[pl.ds(place, chunk), :] = piece[rec * chunk : (rec + 1) * chunk, :]


def assemble(places, pieces):
    chunk, model = pieces[0].shape
    count = len(pieces)
    tile = 512
    by_col = lambda n: pl.BlockSpec((n, tile), lambda i: (0, i))
    return pl.pallas_call(
        assemble_body,
        grid=(model // tile,),
        in_specs=[pl.BlockSpec(memory_space=pltpu.SMEM)] + [by_col(chunk)] * count,
        out_specs=by_col(count * chunk),
        out_shape=jax.ShapeDtypeStruct((count * chunk, model), BF16),
        compiler_params=params(16),
        cost_estimate=pl.CostEstimate(flops=0, bytes_accessed=6000000, transcendentals=0),
        name="assemble",
    )(places, *pieces)


def to_peer(array, shift):
    dz, dy = shift
    pairs = [
        (z * 2 + y, ((z + dz) % 4) * 2 + (y + dy) % 2) for z in range(4) for y in range(2)
    ]
    return lax.ppermute(array, "chan", pairs)


def peer_index(me, shift, sign):
    dz, dy = shift
    return (((me >> 1) + sign * dz) & 3) * 2 + ((me & 1) ^ dy)


def to_all(array):
    return lax.all_to_all(array, "chan", 0, 0, tiled=True)


def pick(array, index, axis):
    return lax.dynamic_index_in_dim(array, index, axis, keepdims=False)


def core_swap(array):
    return lax.ppermute(array, "batch", [(0, 1), (1, 0), (2, 3), (3, 2)])


def frame_sums(pair):
    frame = lax.axis_index("frames")
    sums = pick(pair, frame, 0)
    for shift in (1, 3, 2):
        sent = pick(pair, (frame + shift) & 3, 0).astype(BF16)
        got = lax.ppermute(sent, "frames", [(i, (i + shift) % 4) for i in range(4)])
        sums = sums + got.astype(F32)
    return sums


def row_sums(sums):
    row = lax.axis_index("batch") >> 1
    sent = pick(sums, 1 - row, 0).astype(BF16)
    got = lax.ppermute(sent, "batch", [(0, 2), (1, 3), (2, 0), (3, 1)])
    return pick(sums, row, 0), got


def over_z(array):
    groups = [[0, 2, 4, 6], [1, 3, 5, 7]]
    return lax.all_gather(array, "chan", axis_index_groups=groups, tiled=True)


def shards(tokens, cotangent, norm_gain, norm_bias, qkv_weight, out_weight, lengths, segments):
    recs, frames, model = tokens.shape
    rows = recs * frames
    width = out_weight.shape[0]
    me = lax.axis_index("chan")
    start = lax.axis_index("frames") * frames
    scalar = lambda value: value.reshape(1).astype(jnp.int32)

    weight = qkv_weight.transpose(1, 2, 0).reshape(3 * width, model)
    tie = lax.optimization_barrier
    core = lax.axis_index("batch") & 1
    near_out = over_z(out_weight)

    flat_tokens = tokens.reshape(rows, model)
    flat_cot = cotangent.reshape(rows, model)
    reach = start - CTX + jnp.arange(frames + 2 * CTX, dtype=jnp.int32)
    padded = jnp.pad(segments, ((0, 0), (CTX, CTX)), constant_values=-10)
    seg_keys = lax.dynamic_slice_in_dim(padded, start, frames + 2 * CTX, 1)
    seg_keys = jnp.where(reach[None, :] < lengths[:, None], seg_keys, -10)
    seg_keys = seg_keys.astype(F32)[:, None, :]
    seg_rows = lax.dynamic_slice_in_dim(segments, start, frames, 1).astype(F32)[:, None, :]

    normed, q, kv, g, kv_first, kv_last, live = project(
        lengths, flat_tokens, flat_cot, norm_gain, norm_bias, weight, out_weight
    )
    size = lax.axis_size("frames")
    up = [(i, i + 1) for i in range(size - 1)]
    down = [(i + 1, i) for i in range(size - 1)]
    before = lax.ppermute(kv_last, "frames", up)
    after = lax.ppermute(kv_first, "frames", down)
    late_out, _ = tie((out_weight, kv_first))
    peer_out = to_peer(late_out, (0, 1))
    before, after, peer_out = tie((before, after, peer_out))
    far_out = over_z(peer_out)

    results, mixed = [None] * recs, []
    for rec in reversed(range(recs)):
        out, dq, dkv, dbefore, dafter = attention(
            rec, q, kv, before, after, g, seg_keys, seg_rows, live, *mixed
        )
        right = lax.ppermute(dbefore, "frames", down)
        left = lax.ppermute(dafter, "frames", up)
        mixed = [out]
        results[rec] = [dq, dkv, left, right]

    first, second = results
    count = lax.axis_size("chan")
    second[0], _ = tie((second[0], first[0]))

    split = lambda back: back.reshape(count, -1, model)
    second_back = split(back_rows(*second[:4], weight))
    mixed, second_back = tie((mixed[0], second_back))
    near_mixed = over_z(mixed)
    peer_mixed = to_peer(mixed, (0, 1))
    first[0], second_back, near_out = tie((first[0], second_back, near_out))
    sent, kept = weight_grads(scalar(core), normed, flat_cot, first + second + [mixed])
    second_parts = to_all(second_back)
    first[0], sent, second_parts, far_out = tie((first[0], sent, second_parts, far_out))
    first_back = split(back_rows(*first[:4], weight))
    first_back, peer_mixed = tie((first_back, peer_mixed))
    far_mixed = over_z(peer_mixed)
    first_parts = to_all(first_back)

    ending = lambda rec, *refs: finish(
        scalar(rec * count + me), flat_tokens, flat_cot, norm_gain, *refs
    )
    second_parts, first_back = tie((second_parts, first_back))
    piece = ending(1, second_parts)
    sums = frame_sums(kept.astype(F32) + core_swap(sent).astype(F32))
    sums, first_parts = tie((sums, first_parts))
    piece = ending(0, first_parts, piece)
    pieces = [to_peer(piece, shift) for shift in SHIFTS]
    output = output_rows(flat_tokens, near_mixed, far_mixed, near_out, far_out)
    pieces[0], output = tie((pieces[0], output))
    places = jnp.stack([me] + [peer_index(me, shift, -1) for shift in SHIFTS]).astype(jnp.int32)
    grad_tokens = assemble(places, [piece] + pieces)
    sums, output = tie((sums, output))
    own_sums, got_sums = row_sums(sums)
    grad_proj = (own_sums + got_sums.astype(F32)).reshape(-1, 4, width)
    shape = (recs, frames, model)
    return (output.reshape(shape), grad_tokens.reshape(shape), grad_proj)


def solution(mesh):
    return jax.shard_map(
        shards,
        mesh=mesh,
        in_specs=(
            P("batch", "frames", None),
            P("batch", "frames", None),
            P(),
            P(),
            P(None, None, "chan"),
            P("chan", None),
            P("batch"),
            P("batch", None),
        ),
        out_specs=(
            P("batch", "frames", None),
            P("batch", "frames", None),
            P(("batch", "frames"), None, "chan"),
        ),
        check_vma=False,
    )
```

```python
import jax
import jax.numpy as jnp
from jax import lax
from jax.experimental import pallas as pl
from jax.experimental.pallas import tpu as pltpu
from jax.sharding import PartitionSpec as P

HEAD = 64
CTX = 256
EPS = 1e-05
NEG = -1e30

SHIFTS = ((2, 1), (2, 0), (3, 1), (1, 1), (0, 1), (3, 0), (1, 0))

F32 = jnp.float32
BF16 = jnp.bfloat16


def params(mebibytes=60):
    return pltpu.CompilerParams(vmem_limit_bytes=mebibytes * 1024 * 1024)


def dot_nn(a, b):
    return lax.dot_general(a, b, (((1,), (0,)), ((), ())), preferred_element_type=F32)


def dot_nt(a, b):
    return lax.dot_general(a, b, (((1,), (1,)), ((), ())), preferred_element_type=F32)


def dot_tn(a, b):
    return lax.dot_general(a, b, (((0,), (0,)), ((), ())), preferred_element_type=F32)


def norm_stats(tokens):
    values = tokens.astype(F32)
    centered = values - jnp.mean(values, axis=-1, keepdims=True)
    inverse = lax.rsqrt(jnp.mean(centered * centered, axis=-1, keepdims=True) + EPS)
    return centered * inverse, inverse


def project_body(
    lengths, tok, cot, gain, bias, weight, out_w, normed, q, kv, g, kv_first, kv_last, live
):
    width = q.shape[0]
    scaled, _ = norm_stats(tok[...])
    rows = (scaled * gain[...][None, :] + bias[...][None, :]).astype(BF16)
    normed[...] = rows
    qkv = dot_nt(weight[...], rows).astype(BF16)
    q[...] = qkv[:width]
    kv[...] = qkv[width:]
    kv_first[...] = qkv[width:, :CTX]
    kv_last[...] = qkv[width:, CTX:]
    rec, frames = pl.program_id(0), tok.shape[0]
    start = lax.axis_index("frames") * frames
    position = start + lax.broadcasted_iota(jnp.int32, (1, frames), 1)
    alive = jnp.where(position < lengths[rec], 1.0, 0.0)
    live[...] = alive
    g[...] = (dot_nt(out_w[...], cot[...]) * alive).astype(BF16)


def project(lengths, tokens, cotangent, gain, bias, weight, out_w):
    rows, model = tokens.shape
    width = out_w.shape[0]
    full = lambda shape: pl.BlockSpec(shape, lambda i: (0,) * len(shape))
    frames = 2 * CTX
    by_row = pl.BlockSpec((frames, model), lambda i: (i, 0))
    by_col = lambda n: pl.BlockSpec((n, frames), lambda i: (0, i))
    by_half = pl.BlockSpec((2 * width, CTX), lambda i: (0, i))
    return pl.pallas_call(
        project_body,
        grid=(rows // frames,),
        in_specs=[
            pl.BlockSpec(memory_space=pltpu.SMEM),
            by_row,
            by_row,
            full((model,)),
            full((model,)),
            full((3 * width, model)),
            full((width, model)),
        ],
        out_specs=[
            by_row,
            by_col(width),
            by_col(2 * width),
            by_col(width),
            by_half,
            by_half,
            by_col(1),
        ],
        out_shape=[
            jax.ShapeDtypeStruct((rows, model), BF16),
            jax.ShapeDtypeStruct((width, rows), BF16),
            jax.ShapeDtypeStruct((2 * width, rows), BF16),
            jax.ShapeDtypeStruct((width, rows), BF16),
            jax.ShapeDtypeStruct((2 * width, rows // 2), BF16),
            jax.ShapeDtypeStruct((2 * width, rows // 2), BF16),
            jax.ShapeDtypeStruct((1, rows), F32),
        ],
        compiler_params=params(),
        cost_estimate=pl.CostEstimate(flops=2400000000, bytes_accessed=15000000, transcendentals=0),
        name="project",
    )(lengths, tokens, cotangent, gain, bias, weight, out_w)


def attention_body(q, kv, before, after, g, seg_keys, seg_rows, live, *refs):
    mixed, dq, dkv, dbefore, dafter, acc, mask = refs[-7:]
    if len(refs) > 7:
        mixed[:, q.shape[1] :] = refs[0][...]
    width = q.shape[0]
    span = 3 * CTX
    kv_all = jnp.concatenate([before[...], kv[...], after[...]], axis=1)
    q_small = q[...] * jnp.asarray(HEAD**-0.5, BF16)
    grads = g[...]
    acc[...] = jnp.zeros_like(acc)
    seg_column = jnp.broadcast_to(seg_keys[0], (128, acc.shape[1])).T[:, :1]
    for tile in range(2):
        cols = slice(tile * CTX, (tile + 1) * CTX)
        keys = slice(tile * CTX, tile * CTX + span)
        away = (
            lax.broadcasted_iota(jnp.int32, (span, CTX), 0)
            - CTX
            - lax.broadcasted_iota(jnp.int32, (span, CTX), 1)
        )
        near = jnp.abs(away) <= CTX
        stretch = jnp.abs(seg_column[keys, :] - seg_rows[0, :, cols]) <= 1.0
        visible = (near & stretch) | (away == 0)
        mask[...] = jnp.where(visible, 0.0, NEG)
        for head in range(width // HEAD):
            d = slice(head * HEAD, (head + 1) * HEAD)
            dv = slice(width + head * HEAD, width + (head + 1) * HEAD)
            k_t, v_t = kv_all[d, keys], kv_all[dv, keys]
            q_t, g_t = q_small[d, cols], grads[d, cols]
            scores = dot_tn(k_t, q_t) + mask[...]
            weights = jnp.exp(scores - jnp.max(scores, axis=0, keepdims=True))
            weights = weights * (1.0 / jnp.sum(weights, axis=0, keepdims=True))
            rounded = weights.astype(BF16)
            out = dot_nn(v_t, rounded)
            mixed[d, cols] = (out * live[:, cols]).astype(BF16)
            grad_w = dot_tn(v_t, g_t)
            total = jnp.sum(out * g_t.astype(F32), axis=0, keepdims=True)
            grad_s = (weights * (grad_w - total)).astype(BF16)
            dq[d, cols] = (dot_nn(k_t, grad_s) * (HEAD**-0.5)).astype(BF16)
            acc[d, keys] += dot_nt(q_t, grad_s)
            acc[dv, keys] += dot_nt(g_t, rounded)
    frames = q.shape[1]
    dkv[...] = acc[:, CTX : CTX + frames]
    dbefore[...] = acc[:, :CTX].astype(BF16)
    dafter[...] = acc[:, CTX + frames :].astype(BF16)


def attention(rec, q, kv, before, after, g, seg_keys, seg_rows, live, *later):
    width, rows = q.shape
    recs, _, span = seg_keys.shape
    frames = rows // recs
    by_rec = lambda n, m: pl.BlockSpec((n, m), lambda i: (0, rec))
    whole = lambda n, m: pl.BlockSpec((n, m), lambda i: (0, 0))
    return pl.pallas_call(
        attention_body,
        grid=(1,),
        in_specs=[
            by_rec(width, frames),
            by_rec(2 * width, frames),
            by_rec(2 * width, CTX),
            by_rec(2 * width, CTX),
            by_rec(width, frames),
            pl.BlockSpec((1, 1, span), lambda i: (rec, 0, 0)),
            pl.BlockSpec((1, 1, frames), lambda i: (rec, 0, 0)),
            by_rec(1, frames),
        ]
        + [whole(width, frames)] * len(later),
        out_specs=[
            whole(width, frames * (1 + len(later))),
            whole(width, frames),
            whole(2 * width, frames),
            whole(2 * width, CTX),
            whole(2 * width, CTX),
        ],
        out_shape=[
            jax.ShapeDtypeStruct((width, frames * (1 + len(later))), BF16),
            jax.ShapeDtypeStruct((width, frames), BF16),
            jax.ShapeDtypeStruct((2 * width, frames), F32),
            jax.ShapeDtypeStruct((2 * width, CTX), BF16),
            jax.ShapeDtypeStruct((2 * width, CTX), BF16),
        ],
        scratch_shapes=[pltpu.VMEM((2 * width, span), F32), pltpu.VMEM((3 * CTX, CTX), F32)],
        compiler_params=params(),
        cost_estimate=pl.CostEstimate(flops=1000, bytes_accessed=1000, transcendentals=0),
        name="attention",
    )(q, kv, before, after, g, seg_keys, seg_rows, live, *later)


def kv_grads(own, left, right):
    beside = jnp.concatenate([left[...], right[...]], axis=1).astype(F32)
    return (own[...] + beside).astype(BF16)


def back_body(dq, own, left, right, weight, out, flipped):
    width = dq.shape[0]

    @pl.when(pl.program_id(0) == 0)
    def _():
        flipped[:, :width] = dq[...].T
        flipped[:, width:] = kv_grads(own, left, right).T

    out[...] = dot_nn(flipped[...], weight[...]).astype(BF16)


def back_rows(dq, own, left, right, weight):
    width, rows = dq.shape
    model = weight.shape[1]
    tile = 512
    full = lambda n, m: pl.BlockSpec((n, m), lambda i: (0, 0))
    by_col = lambda n: pl.BlockSpec((n, tile), lambda i: (0, i))
    return pl.pallas_call(
        back_body,
        grid=(model // tile,),
        in_specs=[
            full(width, rows),
            full(2 * width, rows),
            full(2 * width, rows // 2),
            full(2 * width, rows // 2),
            by_col(3 * width),
        ],
        out_specs=by_col(rows),
        out_shape=jax.ShapeDtypeStruct((rows, model), BF16),
        scratch_shapes=[pltpu.VMEM((rows, 3 * width), BF16)],
        compiler_params=params(),
        cost_estimate=pl.CostEstimate(flops=900000000, bytes_accessed=4000000, transcendentals=0),
        name="back",
    )(dq, own, left, right, weight)


def weight_grads_body(core, normed, cot, *rest):
    pieces, (sent, kept, grads, mixed) = rest[:-4], rest[-4:]
    width, frames = pieces[0].shape
    del core

    @pl.when(pl.program_id(0) == 0)
    def _():
        for rec in range(2):
            dq, own, left, right = pieces[4 * rec : 4 * rec + 4]
            rows = slice(rec * frames, (rec + 1) * frames)
            stacked = jnp.concatenate([dq[...], kv_grads(own, left, right)], axis=0)
            grads[rows, :] = stacked.T
            mixed[rows, :] = pieces[-1][:, rows].T

    sums = [dot_nn(normed[...].T, grads[...]), dot_nn(cot[...].T, mixed[...])]

    def write(target):
        for part, offset in zip(sums, (0, 3 * width)):
            shape = (target.shape[0], target.shape[2], part.shape[1])
            cols = slice(offset, offset + part.shape[1])
            target[:, 0, :, cols] = part.reshape(shape).astype(target.dtype)

    @pl.when(pl.program_id(0) < 2)
    def _():
        write(sent)

    @pl.when(pl.program_id(0) >= 2)
    def _():
        write(kept)


def weight_grads(core, normed, cotangent, pieces):
    rows, model = normed.shape
    width = pieces[0].shape[0]
    block = model // 4

    def by_step(i, c):
        return (0, (i % 2) * 2 + jnp.where(i < 2, 1 - c[0], c[0]))

    part = (4, 1, block // 4, 4 * width)
    return pl.pallas_call(
        weight_grads_body,
        grid_spec=pltpu.PrefetchScalarGridSpec(
            num_scalar_prefetch=1,
            grid=(4,),
            in_specs=[pl.BlockSpec((rows, block), by_step)] * 2
            + [pl.BlockSpec(piece.shape, lambda i, c: (0, 0)) for piece in pieces],
            out_specs=[
                pl.BlockSpec(part, lambda i, c: (0, jnp.minimum(i, 1), 0, 0)),
                pl.BlockSpec(part, lambda i, c: (0, jnp.maximum(i, 2) - 2, 0, 0)),
            ],
            scratch_shapes=[
                pltpu.VMEM((rows, 3 * width), BF16),
                pltpu.VMEM((rows, width), BF16),
            ],
        ),
        out_shape=[
            jax.ShapeDtypeStruct((4, 2, block // 4, 4 * width), BF16),
            jax.ShapeDtypeStruct((4, 2, block // 4, 4 * width), BF16),
        ],
        compiler_params=params(),
        cost_estimate=pl.CostEstimate(flops=10000000000, bytes_accessed=12000000, transcendentals=0),
        name="weight_grads",
    )(core, normed, cotangent, *pieces)


def output_body(tok, near, far, *refs):
    weights, (out, stacks) = refs[:4], refs[4:]
    core = lax.axis_index("batch") & 1
    half = weights[0].shape[0] // 4
    total = tok[...].astype(F32)
    for index, weight in enumerate(weights):
        offset = core if index < 2 else 1 - core
        source = (near, far)[index % 2]
        for z in range(4):
            place = pl.multiple_of((2 * z + offset) * half, half)
            stacks[index, z * half : (z + 1) * half, :] = source[pl.ds(place, half), :]
        total = total + dot_nn(stacks[index].T, weight[...])
    out[...] = total.astype(BF16)


def output_rows(tokens, near, far, weights):
    rows, model = tokens.shape
    depth = weights[0].shape[0]
    block = 2 * CTX
    by_row = pl.BlockSpec((block, model), lambda i: (i, 0))
    by_col = pl.BlockSpec((2 * depth, block), lambda i: (0, i))
    full = pl.BlockSpec((depth, model), lambda i: (0, 0))
    return pl.pallas_call(
        output_body,
        grid=(rows // block,),
        in_specs=[by_row, by_col, by_col] + [full] * 4,
        out_specs=by_row,
        out_shape=jax.ShapeDtypeStruct((rows, model), BF16),
        scratch_shapes=[pltpu.VMEM((4, depth, block), BF16)],
        compiler_params=params(),
        cost_estimate=pl.CostEstimate(
            flops=10000000000, bytes_accessed=12000000, transcendentals=0
        ),
        name="output",
    )(tokens, near, far, *weights)


def finish_body(place, gain, tok, cot, parts, *refs):
    out = refs[-1]
    chunk = tok.shape[0]
    back = jnp.sum(parts[...].astype(F32), axis=0)
    scaled, inverse = norm_stats(tok[...])
    weighted = back * gain[...][None, :]
    first = jnp.mean(weighted, axis=-1, keepdims=True)
    second = jnp.mean(weighted * scaled, axis=-1, keepdims=True)
    grad = inverse * (weighted - first - scaled * second) + cot[...].astype(F32)
    out[:chunk, :] = grad.astype(BF16)
    if len(refs) > 1:
        out[chunk:, :] = refs[0][...]


def finish(place, tokens, cotangent, gain, parts, *later):
    count, chunk, model = parts.shape
    here = pl.BlockSpec((chunk, model), lambda i, p: (p[0], 0))
    whole = lambda n: pl.BlockSpec((n, model), lambda i, p: (0, 0))
    rows = chunk * (1 + len(later))
    return pl.pallas_call(
        finish_body,
        grid_spec=pltpu.PrefetchScalarGridSpec(
            num_scalar_prefetch=1,
            grid=(1,),
            in_specs=[
                pl.BlockSpec((model,), lambda i, p: (0,)),
                here,
                here,
                pl.BlockSpec((count, chunk, model), lambda i, p: (0, 0, 0)),
            ]
            + [whole(chunk)] * len(later),
            out_specs=whole(rows),
        ),
        out_shape=jax.ShapeDtypeStruct((rows, model), BF16),
        compiler_params=params(),
        cost_estimate=pl.CostEstimate(flops=10000000, bytes_accessed=3000000, transcendentals=0),
        name="finish",
    )(place, gain, tokens, cotangent, parts, *later)


def assemble_body(places, *refs):
    pieces, out = refs[:-1], refs[-1]
    chunk = pieces[0].shape[0] // 2
    half = out.shape[0] // 2
    for index, piece in enumerate(pieces):
        for rec in range(2):
            place = pl.multiple_of(rec * half + places[index] * chunk, chunk)
            out[pl.ds(place, chunk), :] = piece[rec * chunk : (rec + 1) * chunk, :]


def assemble(places, pieces):
    chunk, model = pieces[0].shape
    count = len(pieces)
    tile = 512
    by_col = lambda n: pl.BlockSpec((n, tile), lambda i: (0, i))
    return pl.pallas_call(
        assemble_body,
        grid=(model // tile,),
        in_specs=[pl.BlockSpec(memory_space=pltpu.SMEM)] + [by_col(chunk)] * count,
        out_specs=by_col(count * chunk),
        out_shape=jax.ShapeDtypeStruct((count * chunk, model), BF16),
        compiler_params=params(16),
        cost_estimate=pl.CostEstimate(flops=0, bytes_accessed=6000000, transcendentals=0),
        name="assemble",
    )(places, *pieces)


def to_peer(array, shift):
    dz, dy = shift
    pairs = [
        (z * 2 + y, ((z + dz) % 4) * 2 + (y + dy) % 2) for z in range(4) for y in range(2)
    ]
    return lax.ppermute(array, "chan", pairs)


def peer_index(me, shift, sign):
    dz, dy = shift
    return (((me >> 1) + sign * dz) & 3) * 2 + ((me & 1) ^ dy)


def to_all(array):
    return lax.all_to_all(array, "chan", 0, 0, tiled=True)


def pick(array, index, axis):
    return lax.dynamic_index_in_dim(array, index, axis, keepdims=False)


def core_swap(array):
    return lax.ppermute(array, "batch", [(0, 1), (1, 0), (2, 3), (3, 2)])


def frame_sums(pair):
    frame = lax.axis_index("frames")
    sums = pick(pair, frame, 0)
    for shift in (1, 3, 2):
        sent = pick(pair, (frame + shift) & 3, 0).astype(BF16)
        got = lax.ppermute(sent, "frames", [(i, (i + shift) % 4) for i in range(4)])
        sums = sums + got.astype(F32)
    return sums


def row_sums(sums):
    row = lax.axis_index("batch") >> 1
    sent = pick(sums, 1 - row, 0).astype(BF16)
    got = lax.ppermute(sent, "batch", [(0, 2), (1, 3), (2, 0), (3, 1)])
    return pick(sums, row, 0), got


def over_z(array):
    groups = [[0, 2, 4, 6], [1, 3, 5, 7]]
    return lax.all_gather(array, "chan", axis_index_groups=groups, tiled=True)


def shards(tokens, cotangent, norm_gain, norm_bias, qkv_weight, out_weight, lengths, segments):
    recs, frames, model = tokens.shape
    rows = recs * frames
    width = out_weight.shape[0]
    me = lax.axis_index("chan")
    start = lax.axis_index("frames") * frames
    scalar = lambda value: value.reshape(1).astype(jnp.int32)

    weight = qkv_weight.transpose(1, 2, 0).reshape(3 * width, model)
    tie = lax.optimization_barrier
    core = lax.axis_index("batch") & 1
    half_out = lax.dynamic_slice_in_dim(out_weight, core * (width // 2), width // 2, 0)
    near_out = over_z(half_out)

    flat_tokens = tokens.reshape(rows, model)
    flat_cot = cotangent.reshape(rows, model)
    reach = start - CTX + jnp.arange(frames + 2 * CTX, dtype=jnp.int32)
    padded = jnp.pad(segments, ((0, 0), (CTX, CTX)), constant_values=-10)
    seg_keys = lax.dynamic_slice_in_dim(padded, start, frames + 2 * CTX, 1)
    seg_keys = jnp.where(reach[None, :] < lengths[:, None], seg_keys, -10)
    seg_keys = seg_keys.astype(F32)[:, None, :]
    seg_rows = lax.dynamic_slice_in_dim(segments, start, frames, 1).astype(F32)[:, None, :]

    normed, q, kv, g, kv_first, kv_last, live = project(
        lengths, flat_tokens, flat_cot, norm_gain, norm_bias, weight, out_weight
    )
    size = lax.axis_size("frames")
    up = [(i, i + 1) for i in range(size - 1)]
    down = [(i + 1, i) for i in range(size - 1)]
    late_out, kv_first = tie((half_out, kv_first))
    peer_out = to_peer(late_out, (0, 1))
    before = lax.ppermute(kv_last, "frames", up)
    after = lax.ppermute(kv_first, "frames", down)
    before, after, peer_out = tie((before, after, peer_out))
    far_out = over_z(peer_out)

    results, mixed = [None] * recs, []
    for rec in reversed(range(recs)):
        out, dq, dkv, dbefore, dafter = attention(
            rec, q, kv, before, after, g, seg_keys, seg_rows, live, *mixed
        )
        right = lax.ppermute(dbefore, "frames", down)
        left = lax.ppermute(dafter, "frames", up)
        mixed = [out]
        results[rec] = [dq, dkv, left, right]

    first, second = results
    count = lax.axis_size("chan")
    second[0], _ = tie((second[0], first[0]))

    split = lambda back: back.reshape(count, -1, model)
    second_back = split(back_rows(*second[:4], weight))
    mixed, second_back = tie((mixed[0], second_back))
    near_mixed = over_z(mixed)
    peer_mixed = to_peer(mixed, (0, 1))
    first[0], second_back, far_out, near_out = tie((first[0], second_back, far_out, near_out))
    sent, kept = weight_grads(scalar(core), normed, flat_cot, first + second + [mixed])
    second_parts = to_all(second_back)
    first[0], sent, second_parts = tie((first[0], sent, second_parts))
    first_back = split(back_rows(*first[:4], weight))
    first_back, peer_mixed = tie((first_back, peer_mixed))
    far_mixed = over_z(peer_mixed)
    first_parts = to_all(first_back)

    ending = lambda rec, *refs: finish(
        scalar(rec * count + me), flat_tokens, flat_cot, norm_gain, *refs
    )
    second_parts, first_back = tie((second_parts, first_back))
    piece = ending(1, second_parts)
    sums = frame_sums(kept.astype(F32) + core_swap(sent).astype(F32))
    sums, first_parts = tie((sums, first_parts))
    piece = ending(0, first_parts, piece)
    pieces = [to_peer(piece, shift) for shift in SHIFTS]
    own = [near_out, far_out]
    output = output_rows(
        flat_tokens, near_mixed, far_mixed, own + [core_swap(array) for array in own]
    )
    pieces[0], output = tie((pieces[0], output))
    places = jnp.stack([me] + [peer_index(me, shift, -1) for shift in SHIFTS]).astype(jnp.int32)
    grad_tokens = assemble(places, [piece] + pieces)
    sums, output = tie((sums, output))
    own_sums, got_sums = row_sums(sums)
    grad_proj = (own_sums + got_sums.astype(F32)).reshape(-1, 4, width)
    shape = (recs, frames, model)
    return (output.reshape(shape), grad_tokens.reshape(shape), grad_proj)


def solution(mesh):
    return jax.shard_map(
        shards,
        mesh=mesh,
        in_specs=(
            P("batch", "frames", None),
            P("batch", "frames", None),
            P(),
            P(),
            P(None, None, "chan"),
            P("chan", None),
            P("batch"),
            P("batch", None),
        ),
        out_specs=(
            P("batch", "frames", None),
            P("batch", "frames", None),
            P(("batch", "frames"), None, "chan"),
        ),
        check_vma=False,
    )
```

```python
import jax
import jax.numpy as jnp
from jax import lax
from jax.experimental import pallas as pl
from jax.experimental.pallas import tpu as pltpu
from jax.sharding import PartitionSpec as P

HEAD = 64
CTX = 256
EPS = 1e-05
NEG = -1e30

SHIFTS = ((2, 1), (3, 1), (1, 1), (0, 1))

F32 = jnp.float32
BF16 = jnp.bfloat16


def params(mebibytes=60):
    return pltpu.CompilerParams(vmem_limit_bytes=mebibytes * 1024 * 1024)


def dot_nn(a, b):
    return lax.dot_general(a, b, (((1,), (0,)), ((), ())), preferred_element_type=F32)


def dot_nt(a, b):
    return lax.dot_general(a, b, (((1,), (1,)), ((), ())), preferred_element_type=F32)


def dot_tn(a, b):
    return lax.dot_general(a, b, (((0,), (0,)), ((), ())), preferred_element_type=F32)


def norm_stats(tokens):
    values = tokens.astype(F32)
    centered = values - jnp.mean(values, axis=-1, keepdims=True)
    inverse = lax.rsqrt(jnp.mean(centered * centered, axis=-1, keepdims=True) + EPS)
    return centered * inverse, inverse


def project_body(
    lengths, tok, cot, gain, bias, weight, out_w, normed, q, kv, g, kv_first, kv_last, live
):
    width = q.shape[0]
    scaled, _ = norm_stats(tok[...])
    rows = (scaled * gain[...][None, :] + bias[...][None, :]).astype(BF16)
    normed[...] = rows
    qkv = dot_nt(weight[...], rows).astype(BF16)
    q[...] = qkv[:width]
    kv[...] = qkv[width:]
    kv_first[...] = qkv[width:, :CTX]
    kv_last[...] = qkv[width:, CTX:]
    rec, frames = pl.program_id(0), tok.shape[0]
    start = lax.axis_index("frames") * frames
    position = start + lax.broadcasted_iota(jnp.int32, (1, frames), 1)
    alive = jnp.where(position < lengths[rec], 1.0, 0.0)
    live[...] = alive
    g[...] = (dot_nt(out_w[...], cot[...]) * alive).astype(BF16)


def project(lengths, tokens, cotangent, gain, bias, weight, out_w):
    rows, model = tokens.shape
    width = out_w.shape[0]
    full = lambda shape: pl.BlockSpec(shape, lambda i: (0,) * len(shape))
    frames = 2 * CTX
    by_row = pl.BlockSpec((frames, model), lambda i: (i, 0))
    by_col = lambda n: pl.BlockSpec((n, frames), lambda i: (0, i))
    by_half = pl.BlockSpec((2 * width, CTX), lambda i: (0, i))
    return pl.pallas_call(
        project_body,
        grid=(rows // frames,),
        in_specs=[
            pl.BlockSpec(memory_space=pltpu.SMEM),
            by_row,
            by_row,
            full((model,)),
            full((model,)),
            full((3 * width, model)),
            full((width, model)),
        ],
        out_specs=[
            by_row,
            by_col(width),
            by_col(2 * width),
            by_col(width),
            by_half,
            by_half,
            by_col(1),
        ],
        out_shape=[
            jax.ShapeDtypeStruct((rows, model), BF16),
            jax.ShapeDtypeStruct((width, rows), BF16),
            jax.ShapeDtypeStruct((2 * width, rows), BF16),
            jax.ShapeDtypeStruct((width, rows), BF16),
            jax.ShapeDtypeStruct((2 * width, rows // 2), BF16),
            jax.ShapeDtypeStruct((2 * width, rows // 2), BF16),
            jax.ShapeDtypeStruct((1, rows), F32),
        ],
        compiler_params=params(),
        cost_estimate=pl.CostEstimate(flops=2400000000, bytes_accessed=15000000, transcendentals=0),
        name="project",
    )(lengths, tokens, cotangent, gain, bias, weight, out_w)


def attention_body(q, kv, before, after, g, seg_keys, seg_rows, live, *refs):
    mixed, dq, dkv, dbefore, dafter, acc, mask = refs[-7:]
    if len(refs) > 7:
        mixed[:, q.shape[1] :] = refs[0][...]
    width = q.shape[0]
    span = 3 * CTX
    kv_all = jnp.concatenate([before[...], kv[...], after[...]], axis=1)
    q_small = q[...] * jnp.asarray(HEAD**-0.5, BF16)
    grads = g[...]
    acc[...] = jnp.zeros_like(acc)
    seg_column = jnp.broadcast_to(seg_keys[0], (128, acc.shape[1])).T[:, :1]
    for tile in range(2):
        cols = slice(tile * CTX, (tile + 1) * CTX)
        keys = slice(tile * CTX, tile * CTX + span)
        away = (
            lax.broadcasted_iota(jnp.int32, (span, CTX), 0)
            - CTX
            - lax.broadcasted_iota(jnp.int32, (span, CTX), 1)
        )
        near = jnp.abs(away) <= CTX
        stretch = jnp.abs(seg_column[keys, :] - seg_rows[0, :, cols]) <= 1.0
        visible = (near & stretch) | (away == 0)
        mask[...] = jnp.where(visible, 0.0, NEG)
        for head in range(width // HEAD):
            d = slice(head * HEAD, (head + 1) * HEAD)
            dv = slice(width + head * HEAD, width + (head + 1) * HEAD)
            k_t, v_t = kv_all[d, keys], kv_all[dv, keys]
            q_t, g_t = q_small[d, cols], grads[d, cols]
            scores = dot_tn(k_t, q_t) + mask[...]
            weights = jnp.exp(scores - jnp.max(scores, axis=0, keepdims=True))
            weights = weights * (1.0 / jnp.sum(weights, axis=0, keepdims=True))
            rounded = weights.astype(BF16)
            out = dot_nn(v_t, rounded)
            mixed[d, cols] = (out * live[:, cols]).astype(BF16)
            grad_w = dot_tn(v_t, g_t)
            total = jnp.sum(out * g_t.astype(F32), axis=0, keepdims=True)
            grad_s = (weights * (grad_w - total)).astype(BF16)
            dq[d, cols] = (dot_nn(k_t, grad_s) * (HEAD**-0.5)).astype(BF16)
            acc[d, keys] += dot_nt(q_t, grad_s)
            acc[dv, keys] += dot_nt(g_t, rounded)
    frames = q.shape[1]
    dkv[...] = acc[:, CTX : CTX + frames]
    dbefore[...] = acc[:, :CTX].astype(BF16)
    dafter[...] = acc[:, CTX + frames :].astype(BF16)


def attention(rec, q, kv, before, after, g, seg_keys, seg_rows, live, *later):
    width, rows = q.shape
    recs, _, span = seg_keys.shape
    frames = rows // recs
    by_rec = lambda n, m: pl.BlockSpec((n, m), lambda i: (0, rec))
    whole = lambda n, m: pl.BlockSpec((n, m), lambda i: (0, 0))
    return pl.pallas_call(
        attention_body,
        grid=(1,),
        in_specs=[
            by_rec(width, frames),
            by_rec(2 * width, frames),
            by_rec(2 * width, CTX),
            by_rec(2 * width, CTX),
            by_rec(width, frames),
            pl.BlockSpec((1, 1, span), lambda i: (rec, 0, 0)),
            pl.BlockSpec((1, 1, frames), lambda i: (rec, 0, 0)),
            by_rec(1, frames),
        ]
        + [whole(width, frames)] * len(later),
        out_specs=[
            whole(width, frames * (1 + len(later))),
            whole(width, frames),
            whole(2 * width, frames),
            whole(2 * width, CTX),
            whole(2 * width, CTX),
        ],
        out_shape=[
            jax.ShapeDtypeStruct((width, frames * (1 + len(later))), BF16),
            jax.ShapeDtypeStruct((width, frames), BF16),
            jax.ShapeDtypeStruct((2 * width, frames), F32),
            jax.ShapeDtypeStruct((2 * width, CTX), BF16),
            jax.ShapeDtypeStruct((2 * width, CTX), BF16),
        ],
        scratch_shapes=[pltpu.VMEM((2 * width, span), F32), pltpu.VMEM((3 * CTX, CTX), F32)],
        compiler_params=params(),
        cost_estimate=pl.CostEstimate(flops=1000, bytes_accessed=1000, transcendentals=0),
        name="attention",
    )(q, kv, before, after, g, seg_keys, seg_rows, live, *later)


def kv_grads(own, left, right):
    beside = jnp.concatenate([left[...], right[...]], axis=1).astype(F32)
    return (own[...] + beside).astype(BF16)


def back_body(dq, own, left, right, weight, out, flipped):
    width = dq.shape[0]

    @pl.when(pl.program_id(0) == 0)
    def _():
        flipped[:, :width] = dq[...].T
        flipped[:, width:] = kv_grads(own, left, right).T

    out[...] = dot_nn(flipped[...], weight[...]).astype(BF16)


def back_rows(dq, own, left, right, weight):
    width, rows = dq.shape
    model = weight.shape[1]
    tile = 512
    full = lambda n, m: pl.BlockSpec((n, m), lambda i: (0, 0))
    by_col = lambda n: pl.BlockSpec((n, tile), lambda i: (0, i))
    return pl.pallas_call(
        back_body,
        grid=(model // tile,),
        in_specs=[
            full(width, rows),
            full(2 * width, rows),
            full(2 * width, rows // 2),
            full(2 * width, rows // 2),
            by_col(3 * width),
        ],
        out_specs=by_col(rows),
        out_shape=jax.ShapeDtypeStruct((rows, model), BF16),
        scratch_shapes=[pltpu.VMEM((rows, 3 * width), BF16)],
        compiler_params=params(),
        cost_estimate=pl.CostEstimate(flops=900000000, bytes_accessed=4000000, transcendentals=0),
        name="back",
    )(dq, own, left, right, weight)


def weight_grads_body(core, normed, cot, *rest):
    pieces, (sent, kept, grads, mixed) = rest[:-4], rest[-4:]
    width, frames = pieces[0].shape
    del core

    @pl.when(pl.program_id(0) == 0)
    def _():
        for rec in range(2):
            dq, own, left, right = pieces[4 * rec : 4 * rec + 4]
            rows = slice(rec * frames, (rec + 1) * frames)
            stacked = jnp.concatenate([dq[...], kv_grads(own, left, right)], axis=0)
            grads[rows, :] = stacked.T
            mixed[rows, :] = pieces[-1][:, rows].T

    sums = [dot_nn(normed[...].T, grads[...]), dot_nn(cot[...].T, mixed[...])]

    def write(target):
        for part, offset in zip(sums, (0, 3 * width)):
            shape = (target.shape[0], target.shape[2], part.shape[1])
            cols = slice(offset, offset + part.shape[1])
            target[:, 0, :, cols] = part.reshape(shape).astype(target.dtype)

    @pl.when(pl.program_id(0) < 2)
    def _():
        write(sent)

    @pl.when(pl.program_id(0) >= 2)
    def _():
        write(kept)


def weight_grads(core, normed, cotangent, pieces):
    rows, model = normed.shape
    width = pieces[0].shape[0]
    block = model // 4

    def by_step(i, c):
        return (0, (i % 2) * 2 + jnp.where(i < 2, 1 - c[0], c[0]))

    part = (4, 1, block // 4, 4 * width)
    return pl.pallas_call(
        weight_grads_body,
        grid_spec=pltpu.PrefetchScalarGridSpec(
            num_scalar_prefetch=1,
            grid=(4,),
            in_specs=[pl.BlockSpec((rows, block), by_step)] * 2
            + [pl.BlockSpec(piece.shape, lambda i, c: (0, 0)) for piece in pieces],
            out_specs=[
                pl.BlockSpec(part, lambda i, c: (0, jnp.minimum(i, 1), 0, 0)),
                pl.BlockSpec(part, lambda i, c: (0, jnp.maximum(i, 2) - 2, 0, 0)),
            ],
            scratch_shapes=[
                pltpu.VMEM((rows, 3 * width), BF16),
                pltpu.VMEM((rows, width), BF16),
            ],
        ),
        out_shape=[
            jax.ShapeDtypeStruct((4, 2, block // 4, 4 * width), BF16),
            jax.ShapeDtypeStruct((4, 2, block // 4, 4 * width), BF16),
        ],
        compiler_params=params(),
        cost_estimate=pl.CostEstimate(flops=10000000000, bytes_accessed=12000000, transcendentals=0),
        name="weight_grads",
    )(core, normed, cotangent, *pieces)


def output_body(tok, near, far, *refs):
    weights, (out, stacks) = refs[:4], refs[4:]
    core = lax.axis_index("batch") & 1
    half = weights[0].shape[0] // 4
    total = tok[...].astype(F32)
    for index, weight in enumerate(weights):
        offset = core if index < 2 else 1 - core
        source = (near, far)[index % 2]
        for z in range(4):
            place = pl.multiple_of((2 * z + offset) * half, half)
            stacks[index, z * half : (z + 1) * half, :] = source[pl.ds(place, half), :]
        total = total + dot_nn(stacks[index].T, weight[...])
    out[...] = total.astype(BF16)


def output_rows(tokens, near, far, weights):
    rows, model = tokens.shape
    depth = weights[0].shape[0]
    block = 2 * CTX
    by_row = pl.BlockSpec((block, model), lambda i: (i, 0))
    by_col = pl.BlockSpec((2 * depth, block), lambda i: (0, i))
    full = pl.BlockSpec((depth, model), lambda i: (0, 0))
    return pl.pallas_call(
        output_body,
        grid=(rows // block,),
        in_specs=[by_row, by_col, by_col] + [full] * 4,
        out_specs=by_row,
        out_shape=jax.ShapeDtypeStruct((rows, model), BF16),
        scratch_shapes=[pltpu.VMEM((4, depth, block), BF16)],
        compiler_params=params(),
        cost_estimate=pl.CostEstimate(
            flops=10000000000, bytes_accessed=12000000, transcendentals=0
        ),
        name="output",
    )(tokens, near, far, *weights)


def finish_body(place, gain, tok, cot, parts, *refs):
    out = refs[-1]
    chunk = tok.shape[0]
    back = jnp.sum(parts[...].astype(F32), axis=0)
    scaled, inverse = norm_stats(tok[...])
    weighted = back * gain[...][None, :]
    first = jnp.mean(weighted, axis=-1, keepdims=True)
    second = jnp.mean(weighted * scaled, axis=-1, keepdims=True)
    grad = inverse * (weighted - first - scaled * second) + cot[...].astype(F32)
    out[:chunk, :] = grad.astype(BF16)
    if len(refs) > 1:
        out[chunk:, :] = refs[0][...]
        copies = refs[1]
        copies[...] = jnp.broadcast_to(out[...][None], copies.shape)


def finish(place, tokens, cotangent, gain, parts, *later):
    count, chunk, model = parts.shape
    here = pl.BlockSpec((chunk, model), lambda i, p: (p[0], 0))
    whole = lambda n: pl.BlockSpec((n, model), lambda i, p: (0, 0))
    rows = chunk * (1 + len(later))
    return pl.pallas_call(
        finish_body,
        grid_spec=pltpu.PrefetchScalarGridSpec(
            num_scalar_prefetch=1,
            grid=(1,),
            in_specs=[
                pl.BlockSpec((model,), lambda i, p: (0,)),
                here,
                here,
                pl.BlockSpec((count, chunk, model), lambda i, p: (0, 0, 0)),
            ]
            + [whole(chunk)] * len(later),
            out_specs=[pl.BlockSpec((4, rows, model), lambda i, p: (0, 0, 0))] * len(later)
            + [whole(rows)],
        ),
        out_shape=[jax.ShapeDtypeStruct((4, rows, model), BF16)] * len(later)
        + [jax.ShapeDtypeStruct((rows, model), BF16)],
        compiler_params=params(),
        cost_estimate=pl.CostEstimate(flops=10000000, bytes_accessed=3000000, transcendentals=0),
        name="finish",
    )(place, gain, tokens, cotangent, parts, *later)


def assemble_body(places, near, *refs):
    pieces, out = refs[:-1], refs[-1]
    chunk = near.shape[1] // 2
    half = out.shape[0] // 2
    blocks = [near.at[z] for z in range(near.shape[0])] + list(pieces)
    for index, block in enumerate(blocks):
        for rec in range(2):
            place = pl.multiple_of(rec * half + places[index] * chunk, chunk)
            out[pl.ds(place, chunk), :] = block[rec * chunk : (rec + 1) * chunk, :]


def assemble(places, near, pieces):
    depth, chunk, model = near.shape
    rows = 2 * depth * chunk
    tile = 512
    by_col = lambda n: pl.BlockSpec((n, tile), lambda i: (0, i))
    return pl.pallas_call(
        assemble_body,
        grid=(model // tile,),
        in_specs=[
            pl.BlockSpec(memory_space=pltpu.SMEM),
            pl.BlockSpec((depth, chunk, tile), lambda i: (0, 0, i)),
        ]
        + [by_col(chunk)] * len(pieces),
        out_specs=by_col(rows),
        out_shape=jax.ShapeDtypeStruct((rows, model), BF16),
        compiler_params=params(16),
        cost_estimate=pl.CostEstimate(flops=0, bytes_accessed=6000000, transcendentals=0),
        name="assemble",
    )(places, near, *pieces)


def to_peer(array, shift):
    dz, dy = shift
    pairs = [
        (z * 2 + y, ((z + dz) % 4) * 2 + (y + dy) % 2) for z in range(4) for y in range(2)
    ]
    return lax.ppermute(array, "chan", pairs)


def peer_index(me, shift, sign):
    dz, dy = shift
    return (((me >> 1) + sign * dz) & 3) * 2 + ((me & 1) ^ dy)


def to_all(array):
    return lax.all_to_all(array, "chan", 0, 0, tiled=True)


def pick(array, index, axis):
    return lax.dynamic_index_in_dim(array, index, axis, keepdims=False)


def core_swap(array):
    return lax.ppermute(array, "batch", [(0, 1), (1, 0), (2, 3), (3, 2)])


def frame_sums(pair):
    frame = lax.axis_index("frames")
    sums = pick(pair, frame, 0)
    for shift in (1, 3, 2):
        sent = pick(pair, (frame + shift) & 3, 0).astype(BF16)
        got = lax.ppermute(sent, "frames", [(i, (i + shift) % 4) for i in range(4)])
        sums = sums + got.astype(F32)
    return sums


def row_sums(sums):
    row = lax.axis_index("batch") >> 1
    sent = pick(sums, 1 - row, 0).astype(BF16)
    got = lax.ppermute(sent, "batch", [(0, 2), (1, 3), (2, 0), (3, 1)])
    return pick(sums, row, 0), got


def over_z(array):
    groups = [[0, 2, 4, 6], [1, 3, 5, 7]]
    return lax.all_gather(array, "chan", axis_index_groups=groups, tiled=True)


def shards(tokens, cotangent, norm_gain, norm_bias, qkv_weight, out_weight, lengths, segments):
    recs, frames, model = tokens.shape
    rows = recs * frames
    width = out_weight.shape[0]
    me = lax.axis_index("chan")
    start = lax.axis_index("frames") * frames
    scalar = lambda value: value.reshape(1).astype(jnp.int32)

    weight = qkv_weight.transpose(1, 2, 0).reshape(3 * width, model)
    tie = lax.optimization_barrier
    core = lax.axis_index("batch") & 1
    half_out = lax.dynamic_slice_in_dim(out_weight, core * (width // 2), width // 2, 0)
    near_out = over_z(half_out)

    flat_tokens = tokens.reshape(rows, model)
    flat_cot = cotangent.reshape(rows, model)
    reach = start - CTX + jnp.arange(frames + 2 * CTX, dtype=jnp.int32)
    padded = jnp.pad(segments, ((0, 0), (CTX, CTX)), constant_values=-10)
    seg_keys = lax.dynamic_slice_in_dim(padded, start, frames + 2 * CTX, 1)
    seg_keys = jnp.where(reach[None, :] < lengths[:, None], seg_keys, -10)
    seg_keys = seg_keys.astype(F32)[:, None, :]
    seg_rows = lax.dynamic_slice_in_dim(segments, start, frames, 1).astype(F32)[:, None, :]

    normed, q, kv, g, kv_first, kv_last, live = project(
        lengths, flat_tokens, flat_cot, norm_gain, norm_bias, weight, out_weight
    )
    size = lax.axis_size("frames")
    up = [(i, i + 1) for i in range(size - 1)]
    down = [(i + 1, i) for i in range(size - 1)]
    late_out, kv_first = tie((half_out, kv_first))
    peer_out = to_peer(late_out, (0, 1))
    before = lax.ppermute(kv_last, "frames", up)
    after = lax.ppermute(kv_first, "frames", down)
    before, after, peer_out = tie((before, after, peer_out))
    far_out = over_z(peer_out)

    results, mixed = [None] * recs, []
    for rec in reversed(range(recs)):
        out, dq, dkv, dbefore, dafter = attention(
            rec, q, kv, before, after, g, seg_keys, seg_rows, live, *mixed
        )
        right = lax.ppermute(dbefore, "frames", down)
        left = lax.ppermute(dafter, "frames", up)
        mixed = [out]
        results[rec] = [dq, dkv, left, right]

    first, second = results
    count = lax.axis_size("chan")
    second[0], _ = tie((second[0], first[0]))

    split = lambda back: back.reshape(count, -1, model)
    second_back = split(back_rows(*second[:4], weight))
    mixed, second_back = tie((mixed[0], second_back))
    near_mixed = over_z(mixed)
    peer_mixed = to_peer(mixed, (0, 1))
    first[0], second_back, far_out, near_out = tie((first[0], second_back, far_out, near_out))
    sent, kept = weight_grads(scalar(core), normed, flat_cot, first + second + [mixed])
    second_parts = to_all(second_back)
    first[0], sent, second_parts = tie((first[0], sent, second_parts))
    first_back = split(back_rows(*first[:4], weight))
    first_back, peer_mixed = tie((first_back, peer_mixed))
    far_mixed = over_z(peer_mixed)
    first_parts = to_all(first_back)

    ending = lambda rec, *refs: finish(
        scalar(rec * count + me), flat_tokens, flat_cot, norm_gain, *refs
    )
    second_parts, first_back = tie((second_parts, first_back))
    (piece,) = ending(1, second_parts)
    sums = frame_sums(kept.astype(F32) + core_swap(sent).astype(F32))
    sums, first_parts = tie((sums, first_parts))
    copies, piece = ending(0, first_parts, piece)
    rings = [[0, 2, 4, 6], [1, 3, 5, 7]]
    near = lax.all_to_all(copies, "chan", 0, 0, axis_index_groups=rings, tiled=True)
    pieces = [to_peer(piece, shift) for shift in SHIFTS]
    own = [near_out, far_out]
    output = output_rows(
        flat_tokens, near_mixed, far_mixed, own + [core_swap(array) for array in own]
    )
    pieces[0], output = tie((pieces[0], output))
    places = [2 * z + (me & 1) for z in range(4)]
    places = jnp.stack(places + [peer_index(me, shift, -1) for shift in SHIFTS])
    grad_tokens = assemble(places.astype(jnp.int32), near, pieces)
    sums, output = tie((sums, output))
    own_sums, got_sums = row_sums(sums)
    grad_proj = (own_sums + got_sums.astype(F32)).reshape(-1, 4, width)
    shape = (recs, frames, model)
    return (output.reshape(shape), grad_tokens.reshape(shape), grad_proj)


def solution(mesh):
    return jax.shard_map(
        shards,
        mesh=mesh,
        in_specs=(
            P("batch", "frames", None),
            P("batch", "frames", None),
            P(),
            P(),
            P(None, None, "chan"),
            P("chan", None),
            P("batch"),
            P("batch", None),
        ),
        out_specs=(
            P("batch", "frames", None),
            P("batch", "frames", None),
            P(("batch", "frames"), None, "chan"),
        ),
        check_vma=False,
    )
```

```python
import jax
import jax.numpy as jnp
from jax import lax
from jax.experimental import pallas as pl
from jax.experimental.pallas import tpu as pltpu
from jax.sharding import PartitionSpec as P

HEAD = 64
CTX = 256
EPS = 1e-05
NEG = -1e30

SHIFTS = ((2, 1), (3, 1), (1, 1), (0, 1))

F32 = jnp.float32
BF16 = jnp.bfloat16


def params(mebibytes=60):
    return pltpu.CompilerParams(vmem_limit_bytes=mebibytes * 1024 * 1024)


def dot_nn(a, b):
    return lax.dot_general(a, b, (((1,), (0,)), ((), ())), preferred_element_type=F32)


def dot_nt(a, b):
    return lax.dot_general(a, b, (((1,), (1,)), ((), ())), preferred_element_type=F32)


def dot_tn(a, b):
    return lax.dot_general(a, b, (((0,), (0,)), ((), ())), preferred_element_type=F32)


def norm_stats(tokens):
    values = tokens.astype(F32)
    centered = values - jnp.mean(values, axis=-1, keepdims=True)
    inverse = lax.rsqrt(jnp.mean(centered * centered, axis=-1, keepdims=True) + EPS)
    return centered * inverse, inverse


def project_body(
    lengths, tok, cot, gain, bias, weight, out_w, normed, q, kv, g, kv_first, kv_last, live
):
    width = q.shape[0]
    scaled, _ = norm_stats(tok[...])
    rows = (scaled * gain[...][None, :] + bias[...][None, :]).astype(BF16)
    normed[...] = rows
    qkv = dot_nt(weight[...], rows).astype(BF16)
    q[...] = qkv[:width]
    kv[...] = qkv[width:]
    kv_first[...] = qkv[width:, :CTX]
    kv_last[...] = qkv[width:, CTX:]
    rec, frames = pl.program_id(0), tok.shape[0]
    start = lax.axis_index("frames") * frames
    position = start + lax.broadcasted_iota(jnp.int32, (1, frames), 1)
    alive = jnp.where(position < lengths[rec], 1.0, 0.0)
    live[...] = alive
    g[...] = (dot_nt(out_w[...], cot[...]) * alive).astype(BF16)


def project(lengths, tokens, cotangent, gain, bias, weight, out_w):
    rows, model = tokens.shape
    width = out_w.shape[0]
    full = lambda shape: pl.BlockSpec(shape, lambda i: (0,) * len(shape))
    frames = 2 * CTX
    by_row = pl.BlockSpec((frames, model), lambda i: (i, 0))
    by_col = lambda n: pl.BlockSpec((n, frames), lambda i: (0, i))
    by_half = pl.BlockSpec((2 * width, CTX), lambda i: (0, i))
    return pl.pallas_call(
        project_body,
        grid=(rows // frames,),
        in_specs=[
            pl.BlockSpec(memory_space=pltpu.SMEM),
            by_row,
            by_row,
            full((model,)),
            full((model,)),
            full((3 * width, model)),
            full((width, model)),
        ],
        out_specs=[
            by_row,
            by_col(width),
            by_col(2 * width),
            by_col(width),
            by_half,
            by_half,
            by_col(1),
        ],
        out_shape=[
            jax.ShapeDtypeStruct((rows, model), BF16),
            jax.ShapeDtypeStruct((width, rows), BF16),
            jax.ShapeDtypeStruct((2 * width, rows), BF16),
            jax.ShapeDtypeStruct((width, rows), BF16),
            jax.ShapeDtypeStruct((2 * width, rows // 2), BF16),
            jax.ShapeDtypeStruct((2 * width, rows // 2), BF16),
            jax.ShapeDtypeStruct((1, rows), F32),
        ],
        compiler_params=params(),
        cost_estimate=pl.CostEstimate(flops=2400000000, bytes_accessed=15000000, transcendentals=0),
        name="project",
    )(lengths, tokens, cotangent, gain, bias, weight, out_w)


def attention_body(q, kv, before, after, g, seg_keys, seg_rows, live, *refs):
    mixed, dq, dkv, dbefore, dafter, acc, mask = refs[-7:]
    if len(refs) > 7:
        mixed[:, q.shape[1] :] = refs[0][...]
    width = q.shape[0]
    span = 3 * CTX
    kv_all = jnp.concatenate([before[...], kv[...], after[...]], axis=1)
    q_small = q[...] * jnp.asarray(HEAD**-0.5, BF16)
    grads = g[...]
    acc[...] = jnp.zeros_like(acc)
    seg_column = jnp.broadcast_to(seg_keys[0], (128, acc.shape[1])).T[:, :1]
    for tile in range(2):
        cols = slice(tile * CTX, (tile + 1) * CTX)
        keys = slice(tile * CTX, tile * CTX + span)
        away = (
            lax.broadcasted_iota(jnp.int32, (span, CTX), 0)
            - CTX
            - lax.broadcasted_iota(jnp.int32, (span, CTX), 1)
        )
        near = jnp.abs(away) <= CTX
        stretch = jnp.abs(seg_column[keys, :] - seg_rows[0, :, cols]) <= 1.0
        visible = (near & stretch) | (away == 0)
        mask[...] = jnp.where(visible, 0.0, NEG)
        for head in range(width // HEAD):
            d = slice(head * HEAD, (head + 1) * HEAD)
            dv = slice(width + head * HEAD, width + (head + 1) * HEAD)
            k_t, v_t = kv_all[d, keys], kv_all[dv, keys]
            q_t, g_t = q_small[d, cols], grads[d, cols]
            scores = dot_tn(k_t, q_t) + mask[...]
            weights = jnp.exp(scores - jnp.max(scores, axis=0, keepdims=True))
            weights = weights * (1.0 / jnp.sum(weights, axis=0, keepdims=True))
            rounded = weights.astype(BF16)
            out = dot_nn(v_t, rounded)
            mixed[d, cols] = (out * live[:, cols]).astype(BF16)
            grad_w = dot_tn(v_t, g_t)
            total = jnp.sum(out * g_t.astype(F32), axis=0, keepdims=True)
            grad_s = (weights * (grad_w - total)).astype(BF16)
            dq[d, cols] = (dot_nn(k_t, grad_s) * (HEAD**-0.5)).astype(BF16)
            acc[d, keys] += dot_nt(q_t, grad_s)
            acc[dv, keys] += dot_nt(g_t, rounded)
    frames = q.shape[1]
    dkv[...] = acc[:, CTX : CTX + frames]
    dbefore[...] = acc[:, :CTX].astype(BF16)
    dafter[...] = acc[:, CTX + frames :].astype(BF16)


def attention(rec, q, kv, before, after, g, seg_keys, seg_rows, live, *later):
    width, rows = q.shape
    recs, _, span = seg_keys.shape
    frames = rows // recs
    by_rec = lambda n, m: pl.BlockSpec((n, m), lambda i: (0, rec))
    whole = lambda n, m: pl.BlockSpec((n, m), lambda i: (0, 0))
    return pl.pallas_call(
        attention_body,
        grid=(1,),
        in_specs=[
            by_rec(width, frames),
            by_rec(2 * width, frames),
            by_rec(2 * width, CTX),
            by_rec(2 * width, CTX),
            by_rec(width, frames),
            pl.BlockSpec((1, 1, span), lambda i: (rec, 0, 0)),
            pl.BlockSpec((1, 1, frames), lambda i: (rec, 0, 0)),
            by_rec(1, frames),
        ]
        + [whole(width, frames)] * len(later),
        out_specs=[
            whole(width, frames * (1 + len(later))),
            whole(width, frames),
            whole(2 * width, frames),
            whole(2 * width, CTX),
            whole(2 * width, CTX),
        ],
        out_shape=[
            jax.ShapeDtypeStruct((width, frames * (1 + len(later))), BF16),
            jax.ShapeDtypeStruct((width, frames), BF16),
            jax.ShapeDtypeStruct((2 * width, frames), F32),
            jax.ShapeDtypeStruct((2 * width, CTX), BF16),
            jax.ShapeDtypeStruct((2 * width, CTX), BF16),
        ],
        scratch_shapes=[pltpu.VMEM((2 * width, span), F32), pltpu.VMEM((3 * CTX, CTX), F32)],
        compiler_params=params(),
        cost_estimate=pl.CostEstimate(flops=1000, bytes_accessed=1000, transcendentals=0),
        name="attention",
    )(q, kv, before, after, g, seg_keys, seg_rows, live, *later)


def kv_grads(own, left, right):
    beside = jnp.concatenate([left[...], right[...]], axis=1).astype(F32)
    return (own[...] + beside).astype(BF16)


def back_body(dq, own, left, right, weight, out, flipped):
    width = dq.shape[0]

    @pl.when(pl.program_id(0) == 0)
    def _():
        flipped[:, :width] = dq[...].T
        flipped[:, width:] = kv_grads(own, left, right).T

    out[...] = dot_nn(flipped[...], weight[...]).astype(BF16)


def back_rows(dq, own, left, right, weight):
    width, rows = dq.shape
    model = weight.shape[1]
    tile = 512
    full = lambda n, m: pl.BlockSpec((n, m), lambda i: (0, 0))
    by_col = lambda n: pl.BlockSpec((n, tile), lambda i: (0, i))
    return pl.pallas_call(
        back_body,
        grid=(model // tile,),
        in_specs=[
            full(width, rows),
            full(2 * width, rows),
            full(2 * width, rows // 2),
            full(2 * width, rows // 2),
            by_col(3 * width),
        ],
        out_specs=by_col(rows),
        out_shape=jax.ShapeDtypeStruct((rows, model), BF16),
        scratch_shapes=[pltpu.VMEM((rows, 3 * width), BF16)],
        compiler_params=params(),
        cost_estimate=pl.CostEstimate(flops=900000000, bytes_accessed=4000000, transcendentals=0),
        name="back",
    )(dq, own, left, right, weight)


def weight_grads_body(core, normed, cot, *rest):
    pieces, (sent, kept, grads, mixed) = rest[:-4], rest[-4:]
    width, frames = pieces[0].shape
    del core

    @pl.when(pl.program_id(0) == 0)
    def _():
        for rec in range(2):
            dq, own, left, right = pieces[4 * rec : 4 * rec + 4]
            rows = slice(rec * frames, (rec + 1) * frames)
            stacked = jnp.concatenate([dq[...], kv_grads(own, left, right)], axis=0)
            grads[rows, :] = stacked.T
            mixed[rows, :] = pieces[-1][:, rows].T

    sums = [dot_nn(normed[...].T, grads[...]), dot_nn(cot[...].T, mixed[...])]

    def write(target):
        for part, offset in zip(sums, (0, 3 * width)):
            shape = (target.shape[0], target.shape[2], part.shape[1])
            cols = slice(offset, offset + part.shape[1])
            target[:, 0, :, cols] = part.reshape(shape).astype(target.dtype)

    @pl.when(pl.program_id(0) < 2)
    def _():
        write(sent)

    @pl.when(pl.program_id(0) >= 2)
    def _():
        write(kept)


def weight_grads(core, normed, cotangent, pieces):
    rows, model = normed.shape
    width = pieces[0].shape[0]
    block = model // 4

    def by_step(i, c):
        return (0, (i % 2) * 2 + jnp.where(i < 2, 1 - c[0], c[0]))

    part = (4, 1, block // 4, 4 * width)
    return pl.pallas_call(
        weight_grads_body,
        grid_spec=pltpu.PrefetchScalarGridSpec(
            num_scalar_prefetch=1,
            grid=(4,),
            in_specs=[pl.BlockSpec((rows, block), by_step)] * 2
            + [pl.BlockSpec(piece.shape, lambda i, c: (0, 0)) for piece in pieces],
            out_specs=[
                pl.BlockSpec(part, lambda i, c: (0, jnp.minimum(i, 1), 0, 0)),
                pl.BlockSpec(part, lambda i, c: (0, jnp.maximum(i, 2) - 2, 0, 0)),
            ],
            scratch_shapes=[
                pltpu.VMEM((rows, 3 * width), BF16),
                pltpu.VMEM((rows, width), BF16),
            ],
        ),
        out_shape=[
            jax.ShapeDtypeStruct((4, 2, block // 4, 4 * width), BF16),
            jax.ShapeDtypeStruct((4, 2, block // 4, 4 * width), BF16),
        ],
        compiler_params=params(),
        cost_estimate=pl.CostEstimate(flops=10000000000, bytes_accessed=12000000, transcendentals=0),
        name="weight_grads",
    )(core, normed, cotangent, *pieces)


def output_body(tok, near, far, *refs):
    weights, (out, stacks) = refs[:4], refs[4:]
    core = lax.axis_index("batch") & 1
    half = weights[0].shape[0] // 4
    total = tok[...].astype(F32)
    for index, weight in enumerate(weights):
        offset = core if index < 2 else 1 - core
        source = (near, far)[index % 2]
        for z in range(4):
            place = pl.multiple_of((2 * z + offset) * half, half)
            stacks[index, z * half : (z + 1) * half, :] = source[pl.ds(place, half), :]
        total = total + dot_nn(stacks[index].T, weight[...])
    out[...] = total.astype(BF16)


def output_rows(tokens, near, far, weights):
    rows, model = tokens.shape
    depth = weights[0].shape[0]
    block = 2 * CTX
    by_row = pl.BlockSpec((block, model), lambda i: (i, 0))
    by_col = pl.BlockSpec((2 * depth, block), lambda i: (0, i))
    full = pl.BlockSpec((depth, model), lambda i: (0, 0))
    return pl.pallas_call(
        output_body,
        grid=(rows // block,),
        in_specs=[by_row, by_col, by_col] + [full] * 4,
        out_specs=by_row,
        out_shape=jax.ShapeDtypeStruct((rows, model), BF16),
        scratch_shapes=[pltpu.VMEM((4, depth, block), BF16)],
        compiler_params=params(),
        cost_estimate=pl.CostEstimate(
            flops=10000000000, bytes_accessed=12000000, transcendentals=0
        ),
        name="output",
    )(tokens, near, far, *weights)


def finish_body(place, gain, tok, cot, parts, *refs):
    out = refs[-1]
    chunk = tok.shape[0]
    back = jnp.sum(parts[...].astype(F32), axis=0)
    scaled, inverse = norm_stats(tok[...])
    weighted = back * gain[...][None, :]
    first = jnp.mean(weighted, axis=-1, keepdims=True)
    second = jnp.mean(weighted * scaled, axis=-1, keepdims=True)
    grad = inverse * (weighted - first - scaled * second) + cot[...].astype(F32)
    out[:chunk, :] = grad.astype(BF16)
    if len(refs) > 1:
        out[chunk:, :] = refs[0][...]
        copies = refs[1]
        copies[...] = jnp.broadcast_to(out[...][None], copies.shape)


def finish(place, tokens, cotangent, gain, parts, *later):
    count, chunk, model = parts.shape
    here = pl.BlockSpec((chunk, model), lambda i, p: (p[0], 0))
    whole = lambda n: pl.BlockSpec((n, model), lambda i, p: (0, 0))
    rows = chunk * (1 + len(later))
    return pl.pallas_call(
        finish_body,
        grid_spec=pltpu.PrefetchScalarGridSpec(
            num_scalar_prefetch=1,
            grid=(1,),
            in_specs=[
                pl.BlockSpec((model,), lambda i, p: (0,)),
                here,
                here,
                pl.BlockSpec((count, chunk, model), lambda i, p: (0, 0, 0)),
            ]
            + [whole(chunk)] * len(later),
            out_specs=[pl.BlockSpec((4, rows, model), lambda i, p: (0, 0, 0))] * len(later)
            + [whole(rows)],
        ),
        out_shape=[jax.ShapeDtypeStruct((4, rows, model), BF16)] * len(later)
        + [jax.ShapeDtypeStruct((rows, model), BF16)],
        compiler_params=params(),
        cost_estimate=pl.CostEstimate(flops=10000000, bytes_accessed=3000000, transcendentals=0),
        name="finish",
    )(place, gain, tokens, cotangent, parts, *later)


def assemble_body(places, near, *refs):
    pieces, out = refs[:-1], refs[-1]
    chunk = near.shape[1] // 2
    half = out.shape[0] // 2
    blocks = [near.at[z] for z in range(near.shape[0])] + list(pieces)
    for index, block in enumerate(blocks):
        for rec in range(2):
            place = pl.multiple_of(rec * half + places[index] * chunk, chunk)
            out[pl.ds(place, chunk), :] = block[rec * chunk : (rec + 1) * chunk, :]


def assemble(places, near, pieces):
    depth, chunk, model = near.shape
    rows = 2 * depth * chunk
    tile = 512
    by_col = lambda n: pl.BlockSpec((n, tile), lambda i: (0, i))
    return pl.pallas_call(
        assemble_body,
        grid=(model // tile,),
        in_specs=[
            pl.BlockSpec(memory_space=pltpu.SMEM),
            pl.BlockSpec((depth, chunk, tile), lambda i: (0, 0, i)),
        ]
        + [by_col(chunk)] * len(pieces),
        out_specs=by_col(rows),
        out_shape=jax.ShapeDtypeStruct((rows, model), BF16),
        compiler_params=params(16),
        cost_estimate=pl.CostEstimate(flops=0, bytes_accessed=6000000, transcendentals=0),
        name="assemble",
    )(places, near, *pieces)


def to_peer(array, shift):
    dz, dy = shift
    pairs = [
        (z * 2 + y, ((z + dz) % 4) * 2 + (y + dy) % 2) for z in range(4) for y in range(2)
    ]
    return lax.ppermute(array, "chan", pairs)


def peer_index(me, shift, sign):
    dz, dy = shift
    return (((me >> 1) + sign * dz) & 3) * 2 + ((me & 1) ^ dy)


def to_all(array):
    return lax.all_to_all(array, "chan", 0, 0, tiled=True)


def pick(array, index, axis):
    return lax.dynamic_index_in_dim(array, index, axis, keepdims=False)


def core_swap(array):
    return lax.ppermute(array, "batch", [(0, 1), (1, 0), (2, 3), (3, 2)])


def frame_sums(pair):
    frame = lax.axis_index("frames")
    sums = pick(pair, frame, 0)
    for shift in (1, 3, 2):
        sent = pick(pair, (frame + shift) & 3, 0).astype(BF16)
        got = lax.ppermute(sent, "frames", [(i, (i + shift) % 4) for i in range(4)])
        sums = sums + got.astype(F32)
    return sums


def row_sums(sums):
    row = lax.axis_index("batch") >> 1
    sent = pick(sums, 1 - row, 0).astype(BF16)
    got = lax.ppermute(sent, "batch", [(0, 2), (1, 3), (2, 0), (3, 1)])
    return pick(sums, row, 0), got


def over_z(array):
    groups = [[0, 2, 4, 6], [1, 3, 5, 7]]
    return lax.all_gather(array, "chan", axis_index_groups=groups, tiled=True)


def shards(tokens, cotangent, norm_gain, norm_bias, qkv_weight, out_weight, lengths, segments):
    recs, frames, model = tokens.shape
    rows = recs * frames
    width = out_weight.shape[0]
    me = lax.axis_index("chan")
    start = lax.axis_index("frames") * frames
    scalar = lambda value: value.reshape(1).astype(jnp.int32)

    weight = qkv_weight.transpose(1, 2, 0).reshape(3 * width, model)
    tie = lax.optimization_barrier
    core = lax.axis_index("batch") & 1
    half_out = lax.dynamic_slice_in_dim(out_weight, core * (width // 2), width // 2, 0)
    near_out = over_z(half_out)

    flat_tokens = tokens.reshape(rows, model)
    flat_cot = cotangent.reshape(rows, model)
    reach = start - CTX + jnp.arange(frames + 2 * CTX, dtype=jnp.int32)
    padded = jnp.pad(segments, ((0, 0), (CTX, CTX)), constant_values=-10)
    seg_keys = lax.dynamic_slice_in_dim(padded, start, frames + 2 * CTX, 1)
    seg_keys = jnp.where(reach[None, :] < lengths[:, None], seg_keys, -10)
    seg_keys = seg_keys.astype(F32)[:, None, :]
    seg_rows = lax.dynamic_slice_in_dim(segments, start, frames, 1).astype(F32)[:, None, :]

    normed, q, kv, g, kv_first, kv_last, live = project(
        lengths, flat_tokens, flat_cot, norm_gain, norm_bias, weight, out_weight
    )
    size = lax.axis_size("frames")
    up = [(i, i + 1) for i in range(size - 1)]
    down = [(i + 1, i) for i in range(size - 1)]
    late_out, kv_first = tie((half_out, kv_first))
    peer_out = to_peer(late_out, (0, 1))
    before = lax.ppermute(kv_last, "frames", up)
    after = lax.ppermute(kv_first, "frames", down)
    before, after, peer_out = tie((before, after, peer_out))
    far_out = over_z(peer_out)

    results, mixed = [None] * recs, []
    for rec in reversed(range(recs)):
        out, dq, dkv, dbefore, dafter = attention(
            rec, q, kv, before, after, g, seg_keys, seg_rows, live, *mixed
        )
        right = lax.ppermute(dbefore, "frames", down)
        left = lax.ppermute(dafter, "frames", up)
        mixed = [out]
        results[rec] = [dq, dkv, left, right]

    first, second = results
    count = lax.axis_size("chan")
    second[0], _ = tie((second[0], first[0]))

    split = lambda back: back.reshape(count, -1, model)
    second_back = split(back_rows(*second[:4], weight))
    mixed, second_back = tie((mixed[0], second_back))
    near_mixed = over_z(mixed)
    peer_mixed = to_peer(mixed, (0, 1))
    first[0], second_back, far_out, near_out = tie((first[0], second_back, far_out, near_out))
    sent, kept = weight_grads(scalar(core), normed, flat_cot, first + second + [mixed])
    second_parts = to_all(second_back)
    first[0], sent, second_parts = tie((first[0], sent, second_parts))
    first_back = split(back_rows(*first[:4], weight))
    first_back, peer_mixed = tie((first_back, peer_mixed))
    far_mixed = over_z(peer_mixed)
    first_parts = to_all(first_back)

    ending = lambda rec, *refs: finish(
        scalar(rec * count + me), flat_tokens, flat_cot, norm_gain, *refs
    )
    second_parts, first_back = tie((second_parts, first_back))
    (piece,) = ending(1, second_parts)
    sums = frame_sums(kept.astype(F32) + core_swap(sent).astype(F32))
    sums, first_parts = tie((sums, first_parts))
    copies, piece = ending(0, first_parts, piece)
    rings = [[0, 2, 4, 6], [1, 3, 5, 7]]
    near = lax.all_to_all(copies, "chan", 0, 0, axis_index_groups=rings, tiled=True)
    pieces = [to_peer(piece, shift) for shift in SHIFTS]
    own = [near_out, far_out]
    output = output_rows(
        flat_tokens, near_mixed, far_mixed, own + [core_swap(array) for array in own]
    )
    pieces[0], output = tie((pieces[0], output))
    places = [2 * z + (me & 1) for z in range(4)]
    places = jnp.stack(places + [peer_index(me, shift, -1) for shift in SHIFTS])
    grad_tokens = assemble(places.astype(jnp.int32), near, pieces)
    own_sums, got_sums = row_sums(sums)
    got_sums, output = tie((got_sums, output))
    grad_proj = (own_sums + got_sums.astype(F32)).reshape(-1, 4, width)
    shape = (recs, frames, model)
    return (output.reshape(shape), grad_tokens.reshape(shape), grad_proj)


def solution(mesh):
    return jax.shard_map(
        shards,
        mesh=mesh,
        in_specs=(
            P("batch", "frames", None),
            P("batch", "frames", None),
            P(),
            P(),
            P(None, None, "chan"),
            P("chan", None),
            P("batch"),
            P("batch", None),
        ),
        out_specs=(
            P("batch", "frames", None),
            P("batch", "frames", None),
            P(("batch", "frames"), None, "chan"),
        ),
        check_vma=False,
    )
```
